32 devices in a mesh: rep: 16 (over z, x, core), shard: 2 (over y).
Axes of the slice: x: 2, y: 2, z: 4, core: 2. Of those that a mesh axis runs over, the one named last changes fastest.
Arguments:
- hidden_in: bfloat16 [16384, 1536], P(('rep', 'shard')), may hold values from -6 to 6
- segment_ids: int32 [32, 512], P(('rep', 'shard')), may hold values from 0 to 7, never falling along the last dimension, each value on 1 to 256 neighbouring positions
- routes: int32 [16384, 4], P(('rep', 'shard')), may hold values from 0 to 7, all different within a row; in each aligned block of 512 rows (0 to 511, 512 to 1023, ...) at most 384 rows name the same one
- out_grad: bfloat16 [16384, 1536], P(('rep', 'shard')), may hold values from -6 to 6
- norm1_gain: bfloat16 [1536], P('shard'), may hold values from 0.25 to 1.75
- w_query: bfloat16 [1536, 1536], P('shard'), may hold values from -0.15625 to 0.15625
- key_weight: bfloat16 [1536, 256], P('shard'), may hold values from -0.15625 to 0.15625
- value_weight: bfloat16 [1536, 256], P('shard'), may hold values from -0.15625 to 0.15625
- w_out: bfloat16 [1536, 1536], P('shard'), may hold values from -0.625 to 0.625
- norm2_gain: bfloat16 [1536], P('shard'), may hold values from 0.25 to 1.75
- w_router: bfloat16 [1536, 8], P('shard'), may hold values from -0.078125 to 0.078125
- w_gate: bfloat16 [8, 1536, 768], P(None, 'shard'), may hold values from -0.15625 to 0.15625
- w_up: bfloat16 [8, 1536, 768], P(None, 'shard'), may hold values from -0.15625 to 0.15625
- w_down: bfloat16 [8, 1536, 768], P(None, 'shard'), may hold values from -0.625 to 0.625
Outputs:
- hidden_out: bfloat16 [16384, 1536], P(('rep', 'shard'))
- hidden_grad: bfloat16 [16384, 1536], P(('rep', 'shard'))
- norm1_gain_grad: float32 [1536], P('shard')
- query_grad: float32 [1536, 1536], P('shard')
- key_grad: float32 [1536, 256], P('shard')
- value_grad: float32 [1536, 256], P('shard')
- out_proj_grad: float32 [1536, 1536], P('shard')
- norm2_gain_grad: float32 [1536], P('shard')
- router_grad: float32 [1536, 8], P('shard')
- gate_grad: float32 [8, 1536, 768], P(None, 'shard')
- up_grad: float32 [8, 1536, 768], P(None, 'shard')
- down_grad: float32 [8, 1536, 768], P(None, 'shard')
The draws below stay inside these ranges and needn't reach their ends.
Inputs may be any that keep to these rules, and one draw needn't show every extreme that they name: `routes`: each row names 4 different experts; in the rows of one device no expert is named more than 384 times, and some expert reaches that count. `segment_ids`: along each sequence the ids never fall, every id appears, each document has 1 to 256 tokens and some document has exactly 256.
All inputs are finite; a program needn't handle non-finite values.
Results may differ from the reference program's by a relative error of at most 0.022.
Values may be sent and summed in bfloat16 or wider, within the bound.
A program may use at most 320 MiB of HBM per device.

```python
import math
import jax
import jax.numpy as jnp
import numpy as np
from jax import lax

MODEL_WIDTH = 1536
QUERY_HEADS = 12
KEY_VALUE_HEADS = 2
HEAD_SIZE = 128
FF = 768
TOPK = 4
EXPERTS = 8
SEGMENTS = 8
TOK_DEV = 512
CAP = 384
SEG_MOST = 256
SEQS = 32
TOKENS = 16384


def shard_levels(key, shape, pieces, least, high):
    factor_of, own = 1.0, jax.random.fold_in(key, 6)
    for dim, shards_of in pieces:
        steps = jnp.exp(jax.random.uniform(jax.random.fold_in(own, dim), (shards_of,), jnp.float32, least / len(pieces), high / len(pieces)))
        factor_of = factor_of * jnp.repeat(steps, shape[dim] // shards_of).reshape([-1 if axis == dim else 1 for axis in range(len(shape))])
    return factor_of


def profile(number_of, total, most, slope):
    portions = [(1 << 20) // math.isqrt(grade ** slope) + 1 for grade in range(2, number_of + 1)]
    surplus, holding = total - most - (number_of - 1), [1] * (number_of - 1)
    while surplus > 0:
        candidates = [i for i in range(number_of - 1) if holding[i] < most]
        whole, budget = sum([portions[i] for i in candidates]), surplus
        for i in candidates:
            more = min(most - holding[i], max(1, budget * portions[i] // whole), surplus)
            holding[i] = holding[i] + more
            surplus = surplus - more
    return np.array([most] + holding)


def uneven(key, amount, total, most, lean):
    if amount == 2:
        one = jax.random.randint(key, (), max(1, total - most), min(most, total - 1) + 1)
        return jnp.stack([one, total - one])
    sizes = jnp.asarray(profile(amount, total, most, lean), jnp.int32)
    couples = (amount - 1) // 2
    source_of, receiver = sizes[1:1 + 2 * couples:2], sizes[2:2 + 2 * couples:2]
    room = jnp.minimum(source_of - 1, most - receiver)
    moved = jax.random.randint(jax.random.fold_in(key, 1), (couples,), 0, 1 << 20) % (room + 1)
    sizes = sizes.at[1:1 + 2 * couples:2].set(source_of - moved).at[2:2 + 2 * couples:2].set(receiver + moved)
    return sizes[jax.random.permutation(jax.random.fold_in(key, 2), amount)]


def shared_out(stream_key, own, number, rows, number_of, top, most, skew):
    ranking = jax.random.permutation(stream_key, number_of)
    crowded, ordinary = load_shares(number_of, rows * top, most, skew, True), load_shares(number_of, rows * top, most, skew, False)
    places = jnp.arange(number_of)

    def named(lengths, rotation):
        used = int((lengths > 0).sum())
        fixed = max(1, used // 4)
        passed = fixed + (places - fixed + rotation * (used - fixed)) % max(1, number_of - fixed)
        return jnp.zeros((number_of,), jnp.int32).at[ranking[jnp.where(places < fixed, places, passed)]].set(jnp.asarray(lengths, jnp.int32))

    lengths = jnp.where(number % 4 == 0, named(crowded, number // 4), named(ordinary, number - number // 4 - 1))
    mixed = jax.random.permutation(jax.random.fold_in(own, 3), number_of)
    source_of, sink = mixed[0:number_of // 2 * 2:2], mixed[1:number_of // 2 * 2:2]
    margin = jnp.minimum(lengths[source_of] - 1, most - lengths[sink]) // 2
    margin = jnp.where((source_of == ranking[0]) | (sink == ranking[0]) | (lengths[sink] == 0), 0, jnp.maximum(margin, 0))
    passed = jax.random.randint(jax.random.fold_in(own, 4), (number_of // 2,), 0, 1 << 20) % (margin + 1)
    lengths = lengths.at[source_of].add(-passed).at[sink].add(passed)
    items = jnp.searchsorted(jnp.cumsum(lengths), jnp.arange(rows * top), side="right").astype(jnp.int32)
    table = items.reshape(top, rows).T
    table = table[jax.random.permutation(jax.random.fold_in(own, 1), rows)]
    rotation = jax.random.randint(jax.random.fold_in(own, 2), (rows, 1), 0, top)
    return jnp.take_along_axis(table, (jnp.arange(top)[None, :] + rotation) % top, axis=1)


def load_shares(count, total, limit, skew, full):
    loads = [(1 << 20) // math.isqrt(rank ** skew) + 1 for rank in range(1, count + 1)]
    largest = limit if full else min(limit, max(-(-total // count), total * loads[0] // sum(loads)))
    least = 1 if total - largest >= count - 1 else 0
    holding, rest = [largest] + [least] * (count - 1), total - largest - least * (count - 1)
    while rest > 0:
        free = [i for i in range(1, count) if holding[i] < largest] or [i for i in range(1, count) if holding[i] < limit]
        pool, remaining = sum([loads[i] for i in free]), rest
        for i in free:
            extra = min(limit - holding[i], max(1, remaining * loads[i] // pool), rest)
            holding[i] = holding[i] + extra
            rest = rest - extra
    return np.array(holding)


def normal_values(own_key, extent, spread, bound, pieces=(), kind=jnp.bfloat16):
    drawn = spread * jax.random.normal(own_key, extent, jnp.float32)
    if pieces:
        drawn = drawn * shard_levels(own_key, extent, pieces, -0.22, 0.18)
    return jnp.clip(drawn, -bound, bound).astype(kind)


def setup_inputs(seed: int = 0) -> dict:
    arg_keys = jax.random.split(jax.random.key(seed), 15)
    hidden_in = normal_values(arg_keys[0], (TOKENS, MODEL_WIDTH), 1.0, 6.0, ((0, 32),))
    segment_ids = jax.vmap(lambda own: jnp.searchsorted(jnp.cumsum(uneven(own, SEGMENTS, TOK_DEV, SEG_MOST, 2)), jnp.arange(TOK_DEV), side="right"))(jax.random.split(arg_keys[1], SEQS)).reshape((SEQS, TOK_DEV)).astype(jnp.int32)
    routes_keys = jax.random.split(jax.random.fold_in(arg_keys[2], 1), TOKENS // TOK_DEV)
    routes_turns = jax.random.permutation(jax.random.fold_in(arg_keys[2], 3), TOKENS // TOK_DEV)
    routes = jax.vmap(lambda own, number: shared_out(jax.random.fold_in(arg_keys[2], 2), own, number, TOK_DEV, EXPERTS, TOPK, CAP, 2))(routes_keys, routes_turns).reshape((TOKENS, TOPK))
    out_grad = normal_values(arg_keys[3], (TOKENS, MODEL_WIDTH), 1.0, 6.0, ((0, 32),))
    norm1_gain = jnp.clip(1.0 + 0.15 * jax.random.normal(arg_keys[4], (MODEL_WIDTH,), jnp.float32), 0.25, 1.75).astype(jnp.bfloat16)
    w_query = normal_values(arg_keys[5], (MODEL_WIDTH, QUERY_HEADS * HEAD_SIZE), MODEL_WIDTH ** -0.5, 0.15625, ((0, 2),))
    key_weight = normal_values(arg_keys[6], (MODEL_WIDTH, KEY_VALUE_HEADS * HEAD_SIZE), MODEL_WIDTH ** -0.5, 0.15625, ((0, 2),))
    value_weight = normal_values(arg_keys[7], (MODEL_WIDTH, KEY_VALUE_HEADS * HEAD_SIZE), MODEL_WIDTH ** -0.5, 0.15625, ((0, 2),))
    w_out = normal_values(arg_keys[8], (QUERY_HEADS * HEAD_SIZE, MODEL_WIDTH), (QUERY_HEADS * HEAD_SIZE // 16) ** -0.5, 0.625, ((0, 2),))
    norm2_gain = jnp.clip(1.0 + 0.15 * jax.random.normal(arg_keys[9], (MODEL_WIDTH,), jnp.float32), 0.25, 1.75).astype(jnp.bfloat16)
    w_router = normal_values(arg_keys[10], (MODEL_WIDTH, EXPERTS), (4 * MODEL_WIDTH) ** -0.5, 0.078125, ((0, 2),))
    w_gate = normal_values(arg_keys[11], (EXPERTS, MODEL_WIDTH, FF), MODEL_WIDTH ** -0.5, 0.15625, ((1, 2),))
    w_up = normal_values(arg_keys[12], (EXPERTS, MODEL_WIDTH, FF), MODEL_WIDTH ** -0.5, 0.15625, ((1, 2),))
    w_down = normal_values(arg_keys[13], (EXPERTS, MODEL_WIDTH, FF), (FF // 8) ** -0.5, 0.625, ((1, 2),))
    return dict(hidden_in=hidden_in, segment_ids=segment_ids, routes=routes, out_grad=out_grad, norm1_gain=norm1_gain, w_query=w_query, key_weight=key_weight, value_weight=value_weight, w_out=w_out, norm2_gain=norm2_gain, w_router=w_router, w_gate=w_gate, w_up=w_up, w_down=w_down)


epsilon = 1e-06
rope_base = 1000000.0
highest = lax.Precision.HIGHEST

@jax.custom_vjp
def lowered_rows(v):
    return lax.optimization_barrier(v.astype(jnp.bfloat16)).astype(jnp.float32)

@jax.custom_vjp
def lowered_pullback(v):
    return v

def low_keep(v):
    return (lowered_rows(v), None)

def low_pass(kept, grad):
    return (grad,)

def back_keep(v):
    return (v, None)

def back_low(kept, grad):
    return (lowered_rows(grad),)
lowered_rows.defvjp(low_keep, low_pass)
lowered_pullback.defvjp(back_keep, back_low)

def tables(sequence_length, row_width):
    frequency = rope_base ** (-2.0 * jnp.arange(row_width // 2, dtype=jnp.float32) / row_width)
    angles = jnp.arange(sequence_length, dtype=jnp.float32)[:, None] * frequency[None, :]
    angles = jnp.concatenate([angles, angles], axis=-1)
    return (jnp.cos(angles)[:, None, :], jnp.sin(angles)[:, None, :])

def apply_rotary(values, rotary_cosine, rotary_sine):
    half_width = values.shape[-1] // 2
    turned = jnp.concatenate([-values[..., half_width:], values[..., :half_width]], axis=-1)
    return values * rotary_cosine + turned * rotary_sine

def matrix_product(left_side, right_side):
    return jnp.dot(left_side, right_side, precision=highest)

def normalize(values, gain_vector):
    scale_rows = lax.rsqrt(lax.optimization_barrier(jnp.mean(values * values, axis=-1, keepdims=True)) + epsilon)
    return values * scale_rows * gain_vector

def softmax_rows(values):
    top_value = lax.optimization_barrier(jnp.max(values, axis=-1, keepdims=True))
    exp_values = jnp.exp(values - top_value)
    return exp_values / lax.optimization_barrier(jnp.sum(exp_values, axis=-1, keepdims=True))

def layer_forward(params, hidden, segments, route_rows):
    norm1_gain, w_query, key_weight, value_weight, w_out, norm2_gain, w_router, w_gate, w_up, w_down = params
    sequence_length = hidden.shape[0]
    shard_group_width = QUERY_HEADS // KEY_VALUE_HEADS
    rotary_cosine, rotary_sine = tables(sequence_length, HEAD_SIZE)
    normalized_rows = lowered_rows(normalize(hidden, norm1_gain))
    unrotated_query = lowered_pullback(matrix_product(normalized_rows, w_query)).reshape(sequence_length, QUERY_HEADS, HEAD_SIZE)
    unrotated_key = lowered_pullback(matrix_product(normalized_rows, key_weight)).reshape(sequence_length, KEY_VALUE_HEADS, HEAD_SIZE)
    value_matrix = lowered_rows(lowered_pullback(matrix_product(normalized_rows, value_weight))).reshape(sequence_length, KEY_VALUE_HEADS, HEAD_SIZE)
    query_matrix = lowered_rows(apply_rotary(unrotated_query, rotary_cosine, rotary_sine)).reshape(sequence_length, KEY_VALUE_HEADS, shard_group_width, HEAD_SIZE)
    key_rows = lowered_rows(apply_rotary(unrotated_key, rotary_cosine, rotary_sine))
    scores = jnp.einsum('qkgd,skd->kgqs', query_matrix, key_rows, precision=highest) * HEAD_SIZE ** (-0.5)
    scores = lowered_pullback(scores)
    position = jnp.arange(sequence_length)
    allowed = (position[None, :] <= position[:, None]) & (segments[:, None] == segments[None, :])
    scores = jnp.where(allowed, scores, -1e+30)
    attn_probs = lowered_rows(softmax_rows(scores))
    mixed_heads = jnp.einsum('kgqs,skd->qkgd', attn_probs, value_matrix, precision=highest)
    mixed_heads = lowered_rows(lowered_pullback(mixed_heads.reshape(sequence_length, QUERY_HEADS * HEAD_SIZE)))
    branch = lowered_pullback(matrix_product(mixed_heads, w_out))
    middle = hidden + branch
    normed_two = lowered_rows(normalize(middle, norm2_gain))
    logits = lowered_pullback(matrix_product(normed_two, w_router))
    router = softmax_rows(logits)
    onehot = (route_rows[:, :, None] == jnp.arange(EXPERTS)[None, None, :]).astype(jnp.float32)
    chosen = lax.optimization_barrier(jnp.sum(onehot, axis=1))
    picked = router * chosen
    gate_weights = picked / lax.optimization_barrier(jnp.sum(picked, axis=-1, keepdims=True))
    combined = jnp.zeros_like(middle)
    for expert in range(EXPERTS):
        expert_rows = lowered_pullback(normed_two)
        gate_pre = lowered_pullback(matrix_product(expert_rows, w_gate[expert]))
        lift_pre = lowered_pullback(matrix_product(expert_rows, w_up[expert]))
        inner_act = lowered_rows(gate_pre * jax.nn.sigmoid(gate_pre) * lift_pre)
        output = lowered_rows(lowered_pullback(jnp.dot(inner_act, w_down[expert].T, precision=highest)))
        combined = combined + gate_weights[:, expert:expert + 1] * output
    return middle + combined

def reference(hidden_in, segment_ids, routes, out_grad, norm1_gain, w_query, key_weight, value_weight, w_out, norm2_gain, w_router, w_gate, w_up, w_down):
    params = tuple((weight.astype(jnp.float32) for weight in (norm1_gain, w_query, key_weight, value_weight, w_out, norm2_gain, w_router, w_gate, w_up, w_down)))
    hidden = hidden_in.astype(jnp.float32).reshape(SEQS, TOK_DEV, MODEL_WIDTH)
    cotangent = out_grad.astype(jnp.float32).reshape(SEQS, TOK_DEV, MODEL_WIDTH)
    route_blocks = routes.reshape(SEQS, TOK_DEV, TOPK)

    def seq_step(totals, inputs):
        seq_rows, segments, route_rows, upstream = inputs
        output, pullback = jax.vjp(lambda weights, values: layer_forward(weights, values, segments, route_rows), params, seq_rows)
        weight_grads, row_grad = pullback(upstream)
        totals = jax.tree.map(lambda first_sum, second_sum: first_sum + second_sum, totals, weight_grads)
        return (totals, (output, row_grad))
    zero_grads = tuple((jnp.zeros_like(weight) for weight in params))
    totals, (outputs, row_grads) = lax.scan(seq_step, zero_grads, (hidden, segment_ids, route_blocks, cotangent))
    return (outputs.reshape(TOKENS, MODEL_WIDTH).astype(jnp.bfloat16), row_grads.reshape(TOKENS, MODEL_WIDTH).astype(jnp.bfloat16), totals[0], totals[1], totals[2], totals[3], totals[4], totals[5], totals[6], totals[7], totals[8], totals[9])
```

```python
import functools

import jax
import jax.numpy as jnp
from jax import lax
from jax.experimental import pallas as pl
from jax.experimental.pallas import tpu as pltpu
from jax.sharding import PartitionSpec as P

MODEL_WIDTH = 1536
QUERY_HEADS = 12
KEY_VALUE_HEADS = 2
HEAD_SIZE = 128
TOPK = 4
FF = 768
HALF = 768
ROWS = 512
PAD = 128
WIDE = MODEL_WIDTH + PAD
CHUNK = 192
PER = HALF // CHUNK
CHUNKS = 6 * PER

epsilon = 1e-06
rope_base = 1000000.0
MESH = pl.DeviceIdType.MESH
bf16 = jnp.bfloat16
f32 = jnp.float32


def tables(sequence_length, row_width):
    frequency = rope_base ** (-2.0 * jnp.arange(row_width // 2, dtype=jnp.float32) / row_width)
    angles = jnp.arange(sequence_length, dtype=jnp.float32)[:, None] * frequency[None, :]
    angles = jnp.concatenate([angles, angles], axis=-1)
    return (jnp.cos(angles)[:, None, :], jnp.sin(angles)[:, None, :])


def apply_rotary(values, rotary_cosine, rotary_sine):
    half_width = values.shape[-1] // 2
    turned = jnp.concatenate([-values[..., half_width:], values[..., :half_width]], axis=-1)
    return values * rotary_cosine + turned * rotary_sine


def contract(left_side, right_side, left_dim, right_dim):
    return lax.dot_general(
        left_side,
        right_side,
        (((left_dim,), (right_dim,)), ((), ())),
        preferred_element_type=jnp.float32,
    )


def normalize(values, gain_vector):
    scale_rows = lax.rsqrt(jnp.mean(values * values, axis=-1, keepdims=True) + epsilon)
    return (values * scale_rows * gain_vector, scale_rows)


def norm_back(values, scale_rows, gain_vector, upstream):
    scaled = upstream * gain_vector
    gain_grad = jnp.sum(upstream * values * scale_rows, axis=0)
    inner_sum = jnp.sum(scaled * values, axis=-1, keepdims=True)
    return (scaled * scale_rows - values * scale_rows**3 * inner_sum / values.shape[-1], gain_grad)


def softmax_rows(values):
    top_value = jnp.max(values, axis=-1, keepdims=True)
    exp_values = jnp.exp(values - top_value)
    return exp_values / jnp.sum(exp_values, axis=-1, keepdims=True)


def place():
    rep = lax.axis_index("rep")
    y = lax.axis_index("shard")
    return rep // 4, (rep // 2) % 2, rep % 2, y


def at(z, x, c, y):
    return ((z * 2 + x) * 2 + c, y)


def remote(src, dst, send, recv, device):
    return pltpu.make_async_remote_copy(
        src_ref=src,
        dst_ref=dst,
        send_sem=send,
        recv_sem=recv,
        device_id=device,
        device_id_type=MESH,
    )


def greet(partners):
    barrier = pltpu.get_barrier_semaphore()
    for device in partners:
        pl.semaphore_signal(barrier, inc=1, device_id=device, device_id_type=MESH)
    pl.semaphore_wait(barrier, len(partners))


def gather_kernel(
    wq, wk, wv, wo, sm, g, wg, wu, wd,
    wqf, wkf, wvf, wof, smf, g4, w0,
    loc, y_s, y_r, x_s, x_r, c_s, c_r, d_s, d_r, z_s, z_r,
):
    z, x, c, y = place()
    ydev, xdev, cdev = at(z, x, c, 1 - y), at(z, 1 - x, c, y), at(z, x, 1 - c, y)
    zdev = at(z + 1 - 2 * (z % 2), x, c, y)
    greet((ydev, xdev, cdev, zdev))
    parts, fulls, experts = (wq, wk, wv, wo), (wqf, wkf, wvf, wof), (wg, wu, wd)
    piece = HALF // 4
    mine = pl.ds((2 * x + c) * piece, piece)
    theirs = pl.ds((2 * (1 - x) + c) * piece, piece)
    expert = 2 * (2 * x + c)
    h = z % 2
    ys, xs, cs, ds, zs = [], [], [], [], []
    for a in range(4):
        ys.append(remote(parts[a].at[mine], fulls[a].at[y, mine], y_s.at[a], y_r.at[a], ydev))
        ys[a].start()
    ys.append(remote(sm, smf.at[y], y_s.at[4], y_r.at[4], ydev))
    ys[4].start()
    xs_g = remote(g, g4.at[2], x_s.at[4], x_r.at[4], xdev)
    cs_g = remote(g, g4.at[1], c_s.at[4], c_r.at[4], cdev)
    cs_g.start()
    for m in range(3):
        ys.append(
            remote(
                experts[m].at[expert, pl.ds(h * 384, 384)],
                w0.at[m, pl.ds(y * HALF + h * 384, 384)],
                y_s.at[5 + m],
                y_r.at[5 + m],
                ydev,
            )
        )
        ys[5 + m].start()
    locs = [pltpu.make_async_copy(parts[a], fulls[a].at[y], loc.at[a]) for a in range(4)]
    locs.append(pltpu.make_async_copy(sm, smf.at[y], loc.at[4]))
    locs.append(pltpu.make_async_copy(g, g4.at[0], loc.at[5]))
    for m in range(3):
        locs.append(
            pltpu.make_async_copy(
                experts[m].at[expert], w0.at[m, pl.ds(y * HALF, HALF)], loc.at[6 + m]
            )
        )
    for copy in locs:
        copy.start()
    for a in range(4):
        ys[a].wait_recv()
        xs.append(
            remote(
                fulls[a].at[1 - y, mine], fulls[a].at[1 - y, mine], x_s.at[a], x_r.at[a], xdev
            )
        )
        cs.append(
            remote(
                fulls[a].at[1 - y, mine], fulls[a].at[1 - y, mine], c_s.at[a], c_r.at[a], cdev
            )
        )
        xs[a].start()
        cs[a].start()
    xs_g.start()
    for a in range(4):
        xs[a].wait_recv()
        ds.append(
            remote(
                fulls[a].at[1 - y, theirs], fulls[a].at[1 - y, theirs], d_s.at[a], d_r.at[a], cdev
            )
        )
        ds[a].start()
    for m in range(3):
        ys[5 + m].wait_recv()
        rows = pl.ds((1 - y) * HALF + h * 384, 384)
        zs.append(remote(w0.at[m, rows], w0.at[m, rows], z_s.at[m], z_r.at[m], zdev))
        zs[m].start()
    xs_g.wait_recv()
    ds_g = remote(g4.at[2], g4.at[3], d_s.at[4], d_r.at[4], cdev)
    ds_g.start()
    ys[4].wait_recv()
    for copy in ys:
        copy.wait_send()
    for copy in xs + [xs_g]:
        copy.wait_send()
    xs_g = None
    for copy in cs + [cs_g] + ds + [ds_g] + zs:
        copy.wait()
    for copy in locs:
        copy.wait()


def gather_call(wq, wk, wv, wo, sm, g, wg, wu, wd):
    anyspace = pl.BlockSpec(memory_space=pl.ANY)
    shapes = [
        (2, HALF, MODEL_WIDTH),
        (2, HALF, 256),
        (2, HALF, 256),
        (2, HALF, MODEL_WIDTH),
        (2, 16, HALF),
        (4, ROWS, MODEL_WIDTH),
        (3, MODEL_WIDTH, FF),
    ]
    dma = pltpu.SemaphoreType.DMA
    return pl.pallas_call(
        gather_kernel,
        out_shape=[jax.ShapeDtypeStruct(s, bf16) for s in shapes],
        in_specs=[anyspace] * 9,
        out_specs=[anyspace] * 7,
        scratch_shapes=[dma((9,)), dma((8,)), dma((8,))] + [dma((5,))] * 6 + [dma((3,))] * 2,
        compiler_params=pltpu.CompilerParams(collective_id=1, has_side_effects=True),
        name="gather_weights",
    )(wq, wk, wv, wo, sm, g, wg, wu, wd)


def expert_kernel(
    hg, g4, w0, wg, wu, wd,
    r_own, r_core, r_x, o_own, o_core, o_x, out, gr, ya, za, zb,
    H, G, W, ACT, DG, RS, OS, CR, CO, STG, VA, VB, VS, VZ, VT, VF, FN,
    loc, h_s, h_r, wy_s, wy_r, wz_s, wz_r, stg_sem, y_s, y_r, ld_a, ld_b,
    z1_s, z1_r, ld_z, z2_s, z2_r, ld_f, z3_s, z3_r, fo, x_s, x_r, c1_s, c1_r, c2_s, c2_r,
    rc_s, rc_r, rx_s, rx_r, rd_s, rd_r, ro,
):
    z, x, c, y = place()
    mid = (z == 1) | (z == 2)
    ydev, xdev, cdev = at(z, x, c, 1 - y), at(z, 1 - x, c, y), at(z, x, 1 - c, y)
    zdev = at(z + 1 - 2 * (z % 2), x, c, y)
    mdev = at(3 - z, x, c, y)
    greet((ydev, xdev, cdev, zdev, mdev))
    shards = (wg, wu, wd)
    e0 = 2 * (2 * x + c)
    h = z % 2

    hx = remote(hg, H.at[pl.ds(2 * ROWS, ROWS)], h_s.at[0], h_r.at[0], xdev)
    hc = remote(hg, H.at[pl.ds(ROWS, ROWS)], h_s.at[1], h_r.at[1], cdev)
    hx.start()
    hc.start()
    own = [
        pltpu.make_async_copy(hg, H.at[pl.ds(0, ROWS)], loc.at[0]),
        pltpu.make_async_copy(g4, G, loc.at[1]),
        pltpu.make_async_copy(w0, W.at[0], loc.at[2]),
    ]
    for m in range(3):
        own.append(
            pltpu.make_async_copy(
                shards[m].at[e0 + 1], W.at[1, m, pl.ds(y * HALF, HALF)], loc.at[3 + m]
            )
        )
    wys = []
    for m in range(3):
        wys.append(
            remote(
                shards[m].at[e0 + 1, pl.ds(h * 384, 384)],
                W.at[1, m, pl.ds(y * HALF + h * 384, 384)],
                wy_s.at[m],
                wy_r.at[m],
                ydev,
            )
        )
        wys[m].start()
    for copy in own:
        copy.start()

    def gate_of(j, rows):
        lane = lax.broadcasted_iota(jnp.int32, (2 * ROWS, PAD), 1)
        packed = H[rows, MODEL_WIDTH:].astype(f32)
        picked = (lane == e0 + j) | (lane == e0 + j + 8)
        return jnp.sum(jnp.where(picked, packed, 0.0), axis=1, keepdims=True), lane

    def forward(j, first):
        rows = pl.ds(first, 2 * ROWS)
        gate, lane = gate_of(j, rows)

        def step(t, total):
            columns = pl.ds(pl.multiple_of(t * 256, 256), 256)
            ug = jnp.dot(
                H[rows, :MODEL_WIDTH], W[j, 0, :, columns], preferred_element_type=f32
            )
            uu = jnp.dot(
                H[rows, :MODEL_WIDTH], W[j, 1, :, columns], preferred_element_type=f32
            )
            dh = jnp.dot(G[rows, :], W[j, 2, :, columns], preferred_element_type=f32)
            sigma = jax.nn.sigmoid(ug)
            silu = ug * sigma
            hid = silu * uu
            ACT[j, 0, rows, columns] = (hid * gate).astype(bf16)
            dhg = dh * gate
            ACT[j, 1, rows, columns] = (dhg * uu * sigma * (1.0 + ug * (1.0 - sigma))).astype(bf16)
            ACT[j, 2, rows, columns] = (dhg * silu).astype(bf16)
            return total + jnp.sum(hid * dh, axis=1, keepdims=True)

        total = lax.fori_loop(0, FF // 256, step, jnp.zeros((2 * ROWS, 1), f32))
        high = total.astype(bf16).astype(f32)
        low = total - high
        here = jnp.where(lane == e0 + j, high, jnp.where(lane == e0 + j + 8, low, 0.0))
        if j == 0:
            DG[rows, :] = here.astype(bf16)
        else:
            DG[rows, :] = (DG[rows, :].astype(f32) + here).astype(bf16)

    def nt(j, k, rows, m, ns):
        return lax.dot_general(
            ACT[j, k, rows, :],
            W[j, m, ns, :],
            (((1,), (1,)), ((), ())),
            preferred_element_type=f32,
        )

    def back_rows(rows, ns):
        o = nt(0, 0, rows, 2, ns) + nt(1, 0, rows, 2, ns)
        d = nt(0, 1, rows, 0, ns) + nt(0, 2, rows, 1, ns)
        d = d + nt(1, 1, rows, 0, ns) + nt(1, 2, rows, 1, ns)
        return o, d

    def weight_tile(j, m, left, half, i, slot):
        at_row = half * HALF + i * 384
        lhs = left[:, pl.ds(pl.multiple_of(at_row, 128), 384)]
        act = (m + 1) % 3
        rhs = ACT[j, act]
        tile = lax.dot_general(lhs, rhs, (((0,), (0,)), ((), ())), preferred_element_type=f32)
        STG[slot] = tile.astype(bf16)
        copy = pltpu.make_async_copy(
            STG.at[slot], gr.at[j, m, pl.ds(at_row, 384)], stg_sem.at[slot]
        )
        copy.start()
        return copy

    def y_copy(k):
        j, m, i = k // (3 * PER), (k // PER) % 3, k % PER
        return remote(
            gr.at[j, m, pl.ds((1 - y) * HALF + i * CHUNK, CHUNK)],
            ya.at[k],
            y_s.at[k],
            y_r.at[k],
            ydev,
        )

    def weight_pair(j, m, left, i):
        away = weight_tile(j, m, left, 1 - y, i, 0)
        here = weight_tile(j, m, left, y, i, 1)
        away.wait()
        first = (j * 3 + m) * PER + i * (384 // CHUNK)
        for n in range(384 // CHUNK):
            y_copy(first + n).start()
        here.wait()

    def weight_grads(j, slots):
        done = 0
        for left, m0, steps in ((H, 0, 4), (G, 2, 2)):

            def step(q, _, left=left, m0=m0):
                weight_pair(j, m0 + q // 2, left, q % 2)
                return 0

            lax.fori_loop(0, steps, step, 0)
        del done, slots

    def spot(k, expert):
        j, m, i = k // (3 * PER), (k // PER) % 3, k % PER
        return out.at[m, expert + j, pl.ds(i * CHUNK, CHUNK)]

    def load_a(k):
        j, m, i = k // (3 * PER), (k // PER) % 3, k % PER
        return pltpu.make_async_copy(
            gr.at[j, m, pl.ds(y * HALF + i * CHUNK, CHUNK)], VA.at[k % 2], ld_a.at[k % 2]
        )

    def load_b(k):
        return pltpu.make_async_copy(ya.at[k], VB.at[k % 2], ld_b.at[k % 2])

    def load_z(k):
        return pltpu.make_async_copy(za.at[k], VZ.at[k % 2], ld_z.at[k % 2])

    def load_f(k):
        return pltpu.make_async_copy(zb.at[k], VF.at[k % 2], ld_f.at[k % 2])

    def z1_copy(k):
        return remote(VS.at[k % 4], za.at[k], z1_s.at[k], z1_r.at[k], zdev)

    def z2_copy(k):
        return remote(VT.at[k % 4], zb.at[k], z2_s.at[k], z2_r.at[k], mdev)

    def z3_copy(k):
        return remote(FN.at[k % 4], spot(k, e0), z3_s.at[k], z3_r.at[k], zdev)

    def store_f(k):
        return pltpu.make_async_copy(FN.at[k % 4], spot(k, e0), fo.at[k % 4])

    def x_copy(k):
        return remote(spot(k, e0), spot(k, e0), x_s.at[k], x_r.at[k], xdev)

    def c1_copy(k):
        return remote(spot(k, e0), spot(k, e0), c1_s.at[k], c1_r.at[k], cdev)

    def c2_copy(k):
        other = 2 * (2 * (1 - x) + c)
        return remote(spot(k, other), spot(k, other), c2_s.at[k], c2_r.at[k], cdev)

    def when(k, cond=None):
        ok = (k >= 0) & (k < CHUNKS)
        return pl.when(ok if cond is None else ok & cond)

    def slot(s):
        k_cx = s - 11

        @when(k_cx)
        def _():
            x_copy(k_cx).wait_recv()
            c2_copy(k_cx).start()

        k_x = s - 9

        @when(k_x, mid)
        def _():
            store_f(k_x).wait()
            z3_copy(k_x).wait_send()

        @when(k_x, jnp.logical_not(mid))
        def _():
            z3_copy(k_x).wait_recv()

        @when(k_x)
        def _():
            x_copy(k_x).start()
            c1_copy(k_x).start()

        k_fa = s - 7

        @when(k_fa, mid)
        def _():
            load_f(k_fa).wait()
            z2_copy(k_fa).wait_send()
            FN[k_fa % 4] = (VT[k_fa % 4].astype(f32) + VF[k_fa % 2].astype(f32)).astype(bf16)
            z3_copy(k_fa).start()
            store_f(k_fa).start()

        k_fl = s - 6

        @when(k_fl, mid)
        def _():
            z2_copy(k_fl).wait_recv()
            load_f(k_fl).start()

        k_za = s - 4

        @when(k_za, mid)
        def _():
            load_z(k_za).wait()
            VT[k_za % 4] = (VS[k_za % 4].astype(f32) + VZ[k_za % 2].astype(f32)).astype(bf16)
            z2_copy(k_za).start()

        k_zl = s - 3

        @when(k_zl, mid)
        def _():
            z1_copy(k_zl).wait_recv()
            load_z(k_zl).start()

        @when(s - 5, jnp.logical_not(mid))
        def _():
            z1_copy(s - 5).wait_send()

        k_a = s - 1

        @when(k_a)
        def _():
            load_a(k_a).wait()
            load_b(k_a).wait()
            VS[k_a % 4] = (VA[k_a % 2].astype(f32) + VB[k_a % 2].astype(f32)).astype(bf16)

        @when(k_a, jnp.logical_not(mid))
        def _():
            z1_copy(k_a).start()

        @when(s)
        def _():
            y_copy(s).wait_recv()
            load_a(s).start()
            load_b(s).start()

    def slots(first, last):
        def step(s, _):
            slot(s)
            return 0

        lax.fori_loop(first, last, step, 0)

    own[1].wait()
    own[2].wait()
    own[0].wait()
    hc.wait_recv()
    forward(0, 0)
    hx.wait_recv()
    hd = remote(
        H.at[pl.ds(2 * ROWS, ROWS)], H.at[pl.ds(3 * ROWS, ROWS)], h_s.at[2], h_r.at[2], cdev
    )
    hd.start()
    wzs = []
    for m in range(3):
        wys[m].wait_recv()
        rows = pl.ds((1 - y) * HALF + h * 384, 384)
        wzs.append(remote(W.at[1, m, rows], W.at[1, m, rows], wz_s.at[m], wz_r.at[m], zdev))
        wzs[m].start()
    hd.wait_recv()
    forward(0, 2 * ROWS)
    weight_grads(0, 0)
    for m in range(3):
        wzs[m].wait_recv()
        own[3 + m].wait()
    forward(1, 0)
    slots(0, 2)
    forward(1, 2 * ROWS)
    slots(2, 4)

    def tail(buffer_r, rows):
        buffer_r[:, MODEL_WIDTH:] = DG[rows, :]

    third, second = pl.ds(3 * ROWS, ROWS), pl.ds(2 * ROWS, ROWS)

    def rc_copy(t, which):
        ns = pl.ds(pl.multiple_of(t * 512, 512), 512)
        src, dst = ((RS, CR), (OS, CO))[which]
        return remote(
            src.at[t % 2], dst.at[:, ns], rc_s.at[which, t], rc_r.at[which, t], cdev
        )

    for t in range(3):
        ns = pl.ds(t * 512, 512)
        if t == 2:
            rc_copy(0, 0).wait_send()
            rc_copy(0, 1).wait_send()
        o, d = back_rows(third, ns)
        RS[t % 2] = d.astype(bf16)
        OS[t % 2] = o.astype(bf16)
        rc_copy(t, 0).start()
        rc_copy(t, 1).start()
    dg_copy = remote(
        DG.at[third], CR.at[:, pl.ds(MODEL_WIDTH, PAD)], rd_s.at[0], rd_r.at[0], cdev
    )
    dg_copy.start()
    slots(4, 6)
    for t in range(3):
        ns = pl.ds(t * 512, 512)
        o, d = back_rows(second, ns)
        rc_copy(t, 0).wait_recv()
        rc_copy(t, 1).wait_recv()
        CR[:, ns] = (CR[:, ns].astype(f32) + d).astype(bf16)
        CO[:, ns] = (CO[:, ns].astype(f32) + o).astype(bf16)
    dg_copy.wait_recv()
    CR[:, MODEL_WIDTH:] = CR[:, MODEL_WIDTH:] + DG[second, :]
    rx = remote(CR, r_x, rx_s.at[0], rx_r.at[0], xdev)
    ox = remote(CO, o_x, rx_s.at[1], rx_r.at[1], xdev)
    rx.start()
    ox.start()
    slots(6, 8)
    weight_grads(1, 0)
    slots(8, 10)
    for which, (src, dst) in enumerate(((RS, CR), (OS, CO))):
        for t in (1, 2):
            rc_copy(t, which).wait_send()
    dg_copy.wait_send()

    def rb_copy(t, which):
        src, dst = ((RS, r_core), (OS, o_core))[which]
        return remote(
            src.at[t % 2],
            dst.at[:, pl.ds(t * 512, 512)],
            rd_s.at[1 + which * 3 + t],
            rd_r.at[1 + which * 3 + t],
            cdev,
        )

    def ro_copy(t, which):
        src, dst = ((RS, r_own), (OS, o_own))[which]
        return pltpu.make_async_copy(
            src.at[t % 2], dst.at[:, pl.ds(t * 512, 512)], ro.at[which, t]
        )

    first = pl.ds(ROWS, ROWS)
    tail_b = remote(
        DG.at[first], r_core.at[:, pl.ds(MODEL_WIDTH, PAD)], rd_s.at[7], rd_r.at[7], cdev
    )
    tail_b.start()
    tail_o = pltpu.make_async_copy(
        DG.at[pl.ds(0, ROWS)], r_own.at[:, pl.ds(MODEL_WIDTH, PAD)], ro.at[0, 3]
    )
    tail_o.start()
    for t in range(3):
        if t == 2:
            rb_copy(0, 0).wait_send()
            rb_copy(0, 1).wait_send()
        o, d = back_rows(first, pl.ds(t * 512, 512))
        RS[t % 2] = d.astype(bf16)
        OS[t % 2] = o.astype(bf16)
        rb_copy(t, 0).start()
        rb_copy(t, 1).start()
    slots(10, 12)
    for t in range(3):
        if t < 2:
            rb_copy(2 - t, 0).wait_send()
            rb_copy(2 - t, 1).wait_send()
        else:
            ro_copy(0, 0).wait()
            ro_copy(0, 1).wait()
        o, d = back_rows(pl.ds(0, ROWS), pl.ds(t * 512, 512))
        RS[t % 2] = d.astype(bf16)
        OS[t % 2] = o.astype(bf16)
        ro_copy(t, 0).start()
        ro_copy(t, 1).start()
    slots(12, CHUNKS + 11)
    for which in range(2):
        for t in (1, 2):
            ro_copy(t, which).wait()
        for t in range(3):
            rb_copy(t, which).wait_recv()
    tail_b.wait()
    tail_o.wait()
    rx.wait()
    ox.wait()

    def finish(k, _):
        x_copy(k).wait_send()
        c1_copy(k).wait()
        c2_copy(k).wait()
        y_copy(k).wait_send()
        return 0

    lax.fori_loop(0, CHUNKS, finish, 0)
    for m in range(3):
        wys[m].wait_send()
        wzs[m].wait_send()
    hx.wait_send()
    hc.wait_send()
    hd.wait_send()


def expert_call(hg, g4, w0, wg, wu, wd):
    anyspace = pl.BlockSpec(memory_space=pl.ANY)
    dma = pltpu.SemaphoreType.DMA
    vmem = lambda *s: pltpu.VMEM(s, bf16)
    shapes = [(ROWS, WIDE)] * 3 + [(ROWS, MODEL_WIDTH)] * 3
    shapes += [(3, 8, HALF, FF), (2, 3, MODEL_WIDTH, FF)] + [(CHUNKS, CHUNK, FF)] * 3
    scratch = [
        vmem(4 * ROWS, WIDE),
        vmem(4 * ROWS, MODEL_WIDTH),
        vmem(2, 3, MODEL_WIDTH, FF),
        vmem(2, 3, 4 * ROWS, FF),
        vmem(4 * ROWS, PAD),
        vmem(2, ROWS, 512),
        vmem(2, ROWS, 512),
        vmem(ROWS, WIDE),
        vmem(ROWS, MODEL_WIDTH),
        vmem(2, 384, FF),
        vmem(2, CHUNK, FF),
        vmem(2, CHUNK, FF),
        vmem(4, CHUNK, FF),
        vmem(2, CHUNK, FF),
        vmem(4, CHUNK, FF),
        vmem(2, CHUNK, FF),
        vmem(4, CHUNK, FF),
        dma((6,)), dma((3,)), dma((3,)), dma((3,)), dma((3,)), dma((3,)), dma((3,)),
        dma((2,)), dma((CHUNKS,)), dma((CHUNKS,)), dma((2,)), dma((2,)),
        dma((CHUNKS,)), dma((CHUNKS,)), dma((2,)), dma((CHUNKS,)), dma((CHUNKS,)), dma((2,)),
        dma((CHUNKS,)), dma((CHUNKS,)), dma((4,)), dma((CHUNKS,)), dma((CHUNKS,)),
        dma((CHUNKS,)), dma((CHUNKS,)), dma((CHUNKS,)), dma((CHUNKS,)),
        dma((2, 3)), dma((2, 3)), dma((2,)), dma((2,)), dma((8,)), dma((8,)), dma((2, 4)),
    ]
    return pl.pallas_call(
        expert_kernel,
        out_shape=[jax.ShapeDtypeStruct(s, bf16) for s in shapes],
        in_specs=[anyspace] * 6,
        out_specs=[anyspace] * len(shapes),
        scratch_shapes=scratch,
        compiler_params=pltpu.CompilerParams(
            collective_id=2, has_side_effects=True, vmem_limit_bytes=66 * 1000 * 1000
        ),
        name="experts",
    )(hg, g4, w0, wg, wu, wd)[:7]


def attention_forward(hidden, segments, gain_one, w_q, w_k, w_v, w_o, gain_two):
    sequence_length = hidden.shape[0]
    group = QUERY_HEADS // KEY_VALUE_HEADS
    head_scale = HEAD_SIZE ** (-0.5)
    cosine, sine = tables(sequence_length, HEAD_SIZE)
    normed_f, scale_one = normalize(hidden, gain_one)
    h1 = normed_f.astype(bf16)
    qr = jnp.dot(h1, w_q, preferred_element_type=f32)
    kr = jnp.dot(h1, w_k, preferred_element_type=f32)
    values = jnp.dot(h1, w_v, preferred_element_type=f32).astype(bf16)
    values = values.reshape(sequence_length, KEY_VALUE_HEADS, HEAD_SIZE)
    qr = qr.reshape(sequence_length, QUERY_HEADS, HEAD_SIZE)
    kr = kr.reshape(sequence_length, KEY_VALUE_HEADS, HEAD_SIZE)
    queries = apply_rotary(qr, cosine, sine).astype(bf16)
    queries = queries.reshape(sequence_length, KEY_VALUE_HEADS, group, HEAD_SIZE)
    keys = apply_rotary(kr, cosine, sine).astype(bf16)
    position = jnp.arange(sequence_length)
    allowed = (position[None, :] <= position[:, None]) & (segments[:, None] == segments[None, :])
    scores = jnp.einsum("qkgd,skd->kgqs", queries, keys, preferred_element_type=f32) * head_scale
    scores = jnp.where(allowed, scores, -1e30)
    top_score = jnp.max(scores, axis=-1, keepdims=True)
    exp_scores = jnp.exp(scores - top_score)
    sum_exp = jnp.sum(exp_scores, axis=-1, keepdims=True)
    log_total = top_score + jnp.log(sum_exp)
    probs = (exp_scores / sum_exp).astype(bf16)
    mixed = jnp.einsum("kgqs,skd->qkgd", probs, values, preferred_element_type=f32)
    mixed = mixed.reshape(sequence_length, QUERY_HEADS * HEAD_SIZE).astype(bf16)
    middle = hidden + jnp.dot(mixed, w_o, preferred_element_type=f32)
    normed_two_f, scale_two = normalize(middle, gain_two)
    h2 = normed_two_f.astype(bf16)
    kept = (scale_one, h1, queries, keys, values, allowed, log_total, mixed, middle, scale_two)
    return h2, kept


def router_forward(h2, w_router, routes):
    logits = jnp.dot(h2, w_router, preferred_element_type=f32)
    probs = softmax_rows(logits)
    experts = w_router.shape[1]
    chosen = jnp.any(
        routes[:, :, None] == jnp.arange(experts, dtype=jnp.int32)[None, None, :], axis=1
    )
    picked = jnp.where(chosen, probs, 0.0)
    total = jnp.sum(picked, axis=-1, keepdims=True)
    return probs, chosen, total, picked / total


def router_backward(h2, w_router, probs, chosen, total, gates, gate_grads):
    gate_grads = jnp.where(chosen, gate_grads, 0.0)
    weighted = jnp.sum(gate_grads * gates, axis=-1, keepdims=True)
    prob_grad = jnp.where(chosen, (gate_grads - weighted) / total, 0.0)
    logit_grad = probs * (prob_grad - jnp.sum(prob_grad * probs, axis=-1, keepdims=True))
    logit_grad = logit_grad.astype(bf16)
    return contract(h2, logit_grad, 0, 0), contract(logit_grad, w_router, 1, 1)


def attention_backward(hidden, kept, gain_one, w_q, w_k, w_v, w_o, gain_two, upstream, dh2):
    scale_one, h1, queries, keys, values, allowed, log_total, mixed, middle, scale_two = kept
    sequence_length = hidden.shape[0]
    group = QUERY_HEADS // KEY_VALUE_HEADS
    head_scale = HEAD_SIZE ** (-0.5)
    cosine, sine = tables(sequence_length, HEAD_SIZE)
    middle_norm_grad, gain_two_grad = norm_back(middle, scale_two, gain_two, dh2)
    middle_grad = upstream + middle_norm_grad
    branch_grad = middle_grad.astype(bf16)
    out_proj_sum = contract(mixed, branch_grad, 0, 0)
    mixed_grad = contract(branch_grad, w_o, 1, 1).astype(bf16)
    mixed_grad = mixed_grad.reshape(sequence_length, KEY_VALUE_HEADS, group, HEAD_SIZE)
    probs = jnp.exp(
        jnp.einsum("qkgd,skd->kgqs", queries, keys, preferred_element_type=f32) * head_scale
        - log_total
    )
    probs = jnp.where(allowed, probs, 0.0)
    prob_back = jnp.einsum("qkgd,skd->kgqs", mixed_grad, values, preferred_element_type=f32)
    score_grad = probs * (prob_back - jnp.sum(prob_back * probs, axis=-1, keepdims=True))
    score_grad = score_grad.astype(bf16)
    dq = jnp.einsum("kgqs,skd->qkgd", score_grad, keys, preferred_element_type=f32) * head_scale
    dq = dq.reshape(sequence_length, QUERY_HEADS, HEAD_SIZE)
    dq = apply_rotary(dq, cosine, -sine).astype(bf16)
    dq = dq.reshape(sequence_length, QUERY_HEADS * HEAD_SIZE)
    dk = jnp.einsum("kgqs,qkgd->skd", score_grad, queries, preferred_element_type=f32) * head_scale
    dk = apply_rotary(dk, cosine, -sine).astype(bf16)
    dk = dk.reshape(sequence_length, KEY_VALUE_HEADS * HEAD_SIZE)
    dv = jnp.einsum("kgqs,qkgd->skd", probs.astype(bf16), mixed_grad, preferred_element_type=f32)
    dv = dv.astype(bf16).reshape(sequence_length, KEY_VALUE_HEADS * HEAD_SIZE)
    query_sum = contract(h1, dq, 0, 0)
    key_sum = contract(h1, dk, 0, 0)
    value_sum = contract(h1, dv, 0, 0)
    dh1 = contract(dq, w_q, 1, 1) + contract(dk, w_k, 1, 1) + contract(dv, w_v, 1, 1)
    hidden_norm_grad, gain_one_grad = norm_back(hidden, scale_one, gain_one, dh1)
    hidden_grad = (middle_grad + hidden_norm_grad).astype(bf16)
    return hidden_grad, (
        gain_one_grad,
        query_sum,
        key_sum,
        value_sum,
        out_proj_sum,
        gain_two_grad,
    )


def reduce_over_all(value, dimension):
    value = lax.psum_scatter(
        value.astype(bf16), "shard", scatter_dimension=dimension, tiled=True
    ).astype(f32)
    return lax.psum(value.astype(bf16), "rep").astype(f32)


def local(
    hidden_in,
    segment_ids,
    routes,
    out_grad,
    norm1_gain,
    w_query,
    key_weight,
    value_weight,
    w_out,
    norm2_gain,
    w_router,
    w_gate,
    w_up,
    w_down,
):
    small = jnp.concatenate(
        [norm1_gain[None], norm2_gain[None], w_router.T, jnp.zeros((6, HALF), bf16)], axis=0
    )
    w_q, w_k, w_v, w_o, small, g4, w0 = gather_call(
        w_query, key_weight, value_weight, w_out, small, out_grad, w_gate, w_up, w_down
    )
    whole = lambda w: w.reshape(MODEL_WIDTH, w.shape[-1])
    w_q, w_k, w_v, w_o = whole(w_q), whole(w_k), whole(w_v), whole(w_o)
    small = small.transpose(1, 0, 2).reshape(16, MODEL_WIDTH)
    gain_one, gain_two = small[0].astype(f32), small[1].astype(f32)
    router = small[2:10].T
    hidden = hidden_in.astype(f32)
    h2, kept = attention_forward(
        hidden, segment_ids[0], gain_one, w_q, w_k, w_v, w_o, gain_two
    )
    probs, chosen, total, gates = router_forward(h2, router, routes)
    high = gates.astype(bf16)
    low = (gates - high.astype(f32)).astype(bf16)
    hg = jnp.concatenate([h2, high, low, jnp.zeros((ROWS, PAD - 16), bf16)], axis=1)
    r_own, r_core, r_x, o_own, o_core, o_x, grads = expert_call(
        hg, g4.reshape(4 * ROWS, MODEL_WIDTH), w0, w_gate, w_up, w_down
    )
    add = lambda a, b, c: a.astype(f32) + b.astype(f32) + c.astype(f32)
    middle = kept[8]
    hidden_out = (middle + add(o_own, o_core, o_x)).astype(bf16)
    returned = add(r_own, r_core, r_x)
    gate_grads = returned[:, 1536:1544] + returned[:, 1544:1552]
    router_sum, routed = router_backward(h2, router, probs, chosen, total, gates, gate_grads)
    dh2 = routed + returned[:, :MODEL_WIDTH]
    hidden_grad, sums = attention_backward(
        hidden, kept, gain_one, w_q, w_k, w_v, w_o, gain_two, out_grad.astype(f32), dh2
    )
    attn = [reduce_over_all(value, 0) for value in sums + (router_sum,)]
    grads = [grads[m].astype(f32) for m in range(3)]
    return (hidden_out, hidden_grad, *attn, *grads)


def local_any(
    hidden_in,
    segment_ids,
    routes,
    out_grad,
    norm1_gain,
    w_query,
    key_weight,
    value_weight,
    w_out,
    norm2_gain,
    w_router,
    w_gate,
    w_up,
    w_down,
):
    wide = lambda w, axis: lax.all_gather(w, "shard", axis=axis, tiled=True)
    gain_one, gain_two = wide(norm1_gain, 0).astype(f32), wide(norm2_gain, 0).astype(f32)
    w_q, w_k, w_v, w_o = (wide(w, 0) for w in (w_query, key_weight, value_weight, w_out))
    router = wide(w_router, 0)
    hidden = hidden_in.astype(f32)
    h2, kept = attention_forward(
        hidden, segment_ids[0], gain_one, w_q, w_k, w_v, w_o, gain_two
    )
    probs, chosen, total, gates = router_forward(h2, router, routes)
    full = [wide(w, 1) for w in (w_gate, w_up, w_down)]

    def expert(carry, inputs):
        mixed, dh2 = carry
        gate_weight, up_weight, down_weight, gate = inputs
        gate = gate[:, None]
        ug = jnp.dot(h2, gate_weight, preferred_element_type=f32)
        uu = jnp.dot(h2, up_weight, preferred_element_type=f32)
        dh = jnp.dot(out_grad, down_weight, preferred_element_type=f32)
        sigma = jax.nn.sigmoid(ug)
        silu = ug * sigma
        hid = silu * uu
        gate_grad = jnp.sum(hid * dh, axis=1)
        hidden_rows = (hid * gate).astype(bf16)
        dug = (dh * gate * uu * sigma * (1.0 + ug * (1.0 - sigma))).astype(bf16)
        duu = (dh * gate * silu).astype(bf16)
        mixed = mixed + contract(hidden_rows, down_weight, 1, 1)
        dh2 = dh2 + contract(dug, gate_weight, 1, 1) + contract(duu, up_weight, 1, 1)
        sums = (contract(h2, dug, 0, 0), contract(h2, duu, 0, 0))
        sums = sums + (contract(out_grad, hidden_rows, 0, 0),)
        return (mixed, dh2), (gate_grad, *(s.astype(bf16) for s in sums))

    zeros = jnp.zeros(hidden.shape, f32)
    (mixed, dh2), (gate_grads, *sums) = lax.scan(expert, (zeros, zeros), (*full, gates.T))
    hidden_out = (kept[8] + mixed).astype(bf16)
    router_sum, routed = router_backward(h2, router, probs, chosen, total, gates, gate_grads.T)
    hidden_grad, attn = attention_backward(
        hidden, kept, gain_one, w_q, w_k, w_v, w_o, gain_two, out_grad.astype(f32), routed + dh2
    )
    attn = [reduce_over_all(value, 0) for value in attn + (router_sum,)]
    grads = [reduce_over_all(value, 1) for value in sums]
    return (hidden_out, hidden_grad, *attn, *grads)


def solution(mesh):
    rows, vector, matrix = P(("rep", "shard"), None), P("shard"), P("shard", None)
    stack = P(None, "shard", None)
    in_specs = (
        rows, rows, rows, rows, vector, matrix, matrix, matrix, matrix, vector, matrix,
        stack, stack, stack,
    )
    out_specs = (
        rows, rows, vector, matrix, matrix, matrix, matrix, vector, matrix, stack, stack, stack,
    )
    fits = dict(mesh.shape) == {"rep": 16, "shard": 2}
    body = local if fits else local_any
    return jax.shard_map(body, mesh=mesh, in_specs=in_specs, out_specs=out_specs, check_vma=False)
```

```python
import functools

import jax
import jax.numpy as jnp
from jax import lax
from jax.experimental import pallas as pl
from jax.experimental.pallas import tpu as pltpu
from jax.sharding import PartitionSpec as P

MODEL_WIDTH = 1536
QUERY_HEADS = 12
KEY_VALUE_HEADS = 2
HEAD_SIZE = 128
TOPK = 4
FF = 768
HALF = 768
ROWS = 512
PAD = 128
WIDE = MODEL_WIDTH + PAD
CHUNK = 192
PER = HALF // CHUNK
CHUNKS = 6 * PER

epsilon = 1e-06
rope_base = 1000000.0
MESH = pl.DeviceIdType.MESH
bf16 = jnp.bfloat16
f32 = jnp.float32


def tables(sequence_length, row_width):
    frequency = rope_base ** (-2.0 * jnp.arange(row_width // 2, dtype=jnp.float32) / row_width)
    angles = jnp.arange(sequence_length, dtype=jnp.float32)[:, None] * frequency[None, :]
    angles = jnp.concatenate([angles, angles], axis=-1)
    return (jnp.cos(angles)[:, None, :], jnp.sin(angles)[:, None, :])


def apply_rotary(values, rotary_cosine, rotary_sine):
    half_width = values.shape[-1] // 2
    turned = jnp.concatenate([-values[..., half_width:], values[..., :half_width]], axis=-1)
    return values * rotary_cosine + turned * rotary_sine


def contract(left_side, right_side, left_dim, right_dim):
    return lax.dot_general(
        left_side,
        right_side,
        (((left_dim,), (right_dim,)), ((), ())),
        preferred_element_type=jnp.float32,
    )


def normalize(values, gain_vector):
    scale_rows = lax.rsqrt(jnp.mean(values * values, axis=-1, keepdims=True) + epsilon)
    return (values * scale_rows * gain_vector, scale_rows)


def norm_back(values, scale_rows, gain_vector, upstream):
    scaled = upstream * gain_vector
    gain_grad = jnp.sum(upstream * values * scale_rows, axis=0)
    inner_sum = jnp.sum(scaled * values, axis=-1, keepdims=True)
    return (scaled * scale_rows - values * scale_rows**3 * inner_sum / values.shape[-1], gain_grad)


def softmax_rows(values):
    top_value = jnp.max(values, axis=-1, keepdims=True)
    exp_values = jnp.exp(values - top_value)
    return exp_values / jnp.sum(exp_values, axis=-1, keepdims=True)


def place():
    rep = lax.axis_index("rep")
    y = lax.axis_index("shard")
    return rep // 4, (rep // 2) % 2, rep % 2, y


def at(z, x, c, y):
    return ((z * 2 + x) * 2 + c, y)


def remote(src, dst, send, recv, device):
    return pltpu.make_async_remote_copy(
        src_ref=src,
        dst_ref=dst,
        send_sem=send,
        recv_sem=recv,
        device_id=device,
        device_id_type=MESH,
    )


def greet(partners):
    barrier = pltpu.get_barrier_semaphore()
    for device in partners:
        pl.semaphore_signal(barrier, inc=1, device_id=device, device_id_type=MESH)
    pl.semaphore_wait(barrier, len(partners))


def gather_kernel(
    wq, wk, wv, wo, sm, g, wg, wu, wd,
    wqf, wkf, wvf, wof, smf, g4, w0,
    bq, bk, bv, bo, bs, bg, loc, y_s, y_r, x_s, x_r, c_s, c_r, d_s, d_r, z_s, z_r,
):
    z, x, c, y = place()
    ydev, xdev, cdev = at(z, x, c, 1 - y), at(z, 1 - x, c, y), at(z, x, 1 - c, y)
    zdev = at(z + 1 - 2 * (z % 2), x, c, y)
    greet((ydev, xdev, cdev, zdev))
    parts, fulls, experts = (wq, wk, wv, wo), (wqf, wkf, wvf, wof), (wg, wu, wd)
    piece = HALF // 4
    mine = pl.ds((2 * x + c) * piece, piece)
    theirs = pl.ds((2 * (1 - x) + c) * piece, piece)
    expert = 2 * (2 * x + c)
    h = z % 2
    ys, xs, cs, ds, zs = [], [], [], [], []
    for a in range(4):
        ys.append(remote(parts[a].at[mine], fulls[a].at[y, mine], y_s.at[a], y_r.at[a], ydev))
        ys[a].start()
    ys.append(remote(sm, smf.at[y], y_s.at[4], y_r.at[4], ydev))
    ys[4].start()
    xs_g = remote(g, g4.at[2], x_s.at[4], x_r.at[4], xdev)
    cs_g = remote(g, g4.at[1], c_s.at[4], c_r.at[4], cdev)
    cs_g.start()
    for m in range(3):
        ys.append(
            remote(
                experts[m].at[expert, pl.ds(h * 384, 384)],
                w0.at[m, pl.ds(h * 384, 384)],
                y_s.at[5 + m],
                y_r.at[5 + m],
                ydev,
            )
        )
        ys[5 + m].start()
    pairs = [(parts[a], (bq, bk, bv, bo)[a], fulls[a].at[y]) for a in range(4)]
    pairs += [(sm, bs, smf.at[y]), (g, bg, g4.at[0])]
    loads = [pltpu.make_async_copy(p[0], p[1], loc.at[i]) for i, p in enumerate(pairs)]
    locs = [pltpu.make_async_copy(p[1], p[2], loc.at[6 + i]) for i, p in enumerate(pairs)]
    for copy in loads:
        copy.start()
    for i in range(6):
        loads[i].wait()
        locs[i].start()
    for a in range(4):
        ys[a].wait_recv()
        xs.append(
            remote(
                fulls[a].at[1 - y, mine], fulls[a].at[1 - y, mine], x_s.at[a], x_r.at[a], xdev
            )
        )
        cs.append(
            remote(
                fulls[a].at[1 - y, mine], fulls[a].at[1 - y, mine], c_s.at[a], c_r.at[a], cdev
            )
        )
        xs[a].start()
        cs[a].start()
    xs_g.start()
    for a in range(4):
        xs[a].wait_recv()
        ds.append(
            remote(
                fulls[a].at[1 - y, theirs], fulls[a].at[1 - y, theirs], d_s.at[a], d_r.at[a], cdev
            )
        )
        ds[a].start()
    for m in range(3):
        ys[5 + m].wait_recv()
        rows = pl.ds(h * 384, 384)
        zs.append(remote(w0.at[m, rows], w0.at[m, rows], z_s.at[m], z_r.at[m], zdev))
        zs[m].start()
    xs_g.wait_recv()
    ds_g = remote(g4.at[2], g4.at[3], d_s.at[4], d_r.at[4], cdev)
    ds_g.start()
    ys[4].wait_recv()
    for copy in ys:
        copy.wait_send()
    for copy in xs + [xs_g]:
        copy.wait_send()
    xs_g = None
    for copy in cs + [cs_g] + ds + [ds_g] + zs:
        copy.wait()
    for copy in locs:
        copy.wait()


def gather_call(wq, wk, wv, wo, sm, g, wg, wu, wd):
    anyspace = pl.BlockSpec(memory_space=pl.ANY)
    shapes = [
        (2, HALF, MODEL_WIDTH),
        (2, HALF, 256),
        (2, HALF, 256),
        (2, HALF, MODEL_WIDTH),
        (2, 16, HALF),
        (4, ROWS, MODEL_WIDTH),
        (3, HALF, FF),
    ]
    dma = pltpu.SemaphoreType.DMA
    return pl.pallas_call(
        gather_kernel,
        out_shape=[jax.ShapeDtypeStruct(s, bf16) for s in shapes],
        in_specs=[anyspace] * 9,
        out_specs=[anyspace] * 7,
        scratch_shapes=[
            pltpu.VMEM(s, bf16)
            for s in (
                (HALF, MODEL_WIDTH), (HALF, 256), (HALF, 256), (HALF, MODEL_WIDTH), (16, HALF),
                (ROWS, MODEL_WIDTH),
            )
        ]
        + [dma((12,)), dma((8,)), dma((8,))] + [dma((5,))] * 6 + [dma((3,))] * 2,
        compiler_params=pltpu.CompilerParams(collective_id=1, has_side_effects=True),
        name="gather_weights",
    )(wq, wk, wv, wo, sm, g, wg, wu, wd)


def expert_kernel(
    hg, g4, w0, wg, wu, wd,
    r_own, r_core, r_x, o_own, o_core, o_x, out, gr, ya, za, zb,
    H, G, W, ACT, DG, RS, OS, CR, CO, STG, VA, VB, VS, VZ, VT, VF, FN,
    loc, h_s, h_r, wy_s, wy_r, wz_s, wz_r, stg_sem, y_s, y_r, ld_a, ld_b,
    z1_s, z1_r, ld_z, z2_s, z2_r, ld_f, z3_s, z3_r, fo, x_s, x_r, c1_s, c1_r, c2_s, c2_r,
    rc_s, rc_r, rx_s, rx_r, rd_s, rd_r, ro,
):
    z, x, c, y = place()
    mid = (z == 1) | (z == 2)
    ydev, xdev, cdev = at(z, x, c, 1 - y), at(z, 1 - x, c, y), at(z, x, 1 - c, y)
    zdev = at(z + 1 - 2 * (z % 2), x, c, y)
    mdev = at(3 - z, x, c, y)
    greet((ydev, xdev, cdev, zdev, mdev))
    shards = (wg, wu, wd)
    e0 = 2 * (2 * x + c)
    h = z % 2

    hx = remote(hg, H.at[pl.ds(2 * ROWS, ROWS)], h_s.at[0], h_r.at[0], xdev)
    hc = remote(hg, H.at[pl.ds(ROWS, ROWS)], h_s.at[1], h_r.at[1], cdev)
    hx.start()
    hc.start()
    own = [
        pltpu.make_async_copy(hg, H.at[pl.ds(0, ROWS)], loc.at[0]),
        pltpu.make_async_copy(g4, G, loc.at[1]),
        pltpu.make_async_copy(w0, W.at[0, :, pl.ds((1 - y) * HALF, HALF)], loc.at[2]),
    ]
    for m in range(3):
        own.append(
            pltpu.make_async_copy(
                shards[m].at[e0 + 1], W.at[1, m, pl.ds(y * HALF, HALF)], loc.at[3 + m]
            )
        )
    for m in range(3):
        own.append(
            pltpu.make_async_copy(
                shards[m].at[e0], W.at[0, m, pl.ds(y * HALF, HALF)], loc.at[6 + m]
            )
        )
    wys = []
    for m in range(3):
        wys.append(
            remote(
                shards[m].at[e0 + 1, pl.ds(h * 384, 384)],
                W.at[1, m, pl.ds(y * HALF + h * 384, 384)],
                wy_s.at[m],
                wy_r.at[m],
                ydev,
            )
        )
        wys[m].start()
    for copy in own:
        copy.start()

    def gate_of(j, rows):
        lane = lax.broadcasted_iota(jnp.int32, (2 * ROWS, PAD), 1)
        packed = H[rows, MODEL_WIDTH:].astype(f32)
        picked = (lane == e0 + j) | (lane == e0 + j + 8)
        return jnp.sum(jnp.where(picked, packed, 0.0), axis=1, keepdims=True), lane

    def forward(j, first):
        rows = pl.ds(first, 2 * ROWS)
        gate, lane = gate_of(j, rows)

        def step(t, total):
            columns = pl.ds(pl.multiple_of(t * 256, 256), 256)
            ug = jnp.dot(
                H[rows, :MODEL_WIDTH], W[j, 0, :, columns], preferred_element_type=f32
            )
            uu = jnp.dot(
                H[rows, :MODEL_WIDTH], W[j, 1, :, columns], preferred_element_type=f32
            )
            dh = jnp.dot(G[rows, :], W[j, 2, :, columns], preferred_element_type=f32)
            sigma = jax.nn.sigmoid(ug)
            silu = ug * sigma
            hid = silu * uu
            ACT[j, 0, rows, columns] = (hid * gate).astype(bf16)
            dhg = dh * gate
            ACT[j, 1, rows, columns] = (dhg * uu * sigma * (1.0 + ug * (1.0 - sigma))).astype(bf16)
            ACT[j, 2, rows, columns] = (dhg * silu).astype(bf16)
            return total + jnp.sum(hid * dh, axis=1, keepdims=True)

        total = lax.fori_loop(0, FF // 256, step, jnp.zeros((2 * ROWS, 1), f32))
        high = total.astype(bf16).astype(f32)
        low = total - high
        here = jnp.where(lane == e0 + j, high, jnp.where(lane == e0 + j + 8, low, 0.0))
        if j == 0:
            DG[rows, :] = here.astype(bf16)
        else:
            DG[rows, :] = (DG[rows, :].astype(f32) + here).astype(bf16)

    def nt(j, k, rows, m, ns):
        return lax.dot_general(
            ACT[j, k, rows, :],
            W[j, m, ns, :],
            (((1,), (1,)), ((), ())),
            preferred_element_type=f32,
        )

    def back_rows(rows, ns):
        o = nt(0, 0, rows, 2, ns) + nt(1, 0, rows, 2, ns)
        d = nt(0, 1, rows, 0, ns) + nt(0, 2, rows, 1, ns)
        d = d + nt(1, 1, rows, 0, ns) + nt(1, 2, rows, 1, ns)
        return o, d

    def weight_tile(j, m, left, half, i, slot):
        at_row = half * HALF + i * 384
        lhs = left[:, pl.ds(pl.multiple_of(at_row, 128), 384)]
        act = (m + 1) % 3
        rhs = ACT[j, act]
        tile = lax.dot_general(lhs, rhs, (((0,), (0,)), ((), ())), preferred_element_type=f32)
        STG[slot] = tile.astype(bf16)
        copy = pltpu.make_async_copy(
            STG.at[slot], gr.at[j, m, pl.ds(at_row, 384)], stg_sem.at[slot]
        )
        copy.start()
        return copy

    def y_copy(k):
        j, m, i = k // (3 * PER), (k // PER) % 3, k % PER
        return remote(
            gr.at[j, m, pl.ds((1 - y) * HALF + i * CHUNK, CHUNK)],
            ya.at[k],
            y_s.at[k],
            y_r.at[k],
            ydev,
        )

    def weight_pair(j, m, left, i):
        away = weight_tile(j, m, left, 1 - y, i, 0)
        here = weight_tile(j, m, left, y, i, 1)
        away.wait()
        first = (j * 3 + m) * PER + i * (384 // CHUNK)
        for n in range(384 // CHUNK):
            y_copy(first + n).start()
        here.wait()

    def weight_grads(j, slots):
        done = 0
        for left, m0, steps in ((H, 0, 4), (G, 2, 2)):

            def step(q, _, left=left, m0=m0):
                weight_pair(j, m0 + q // 2, left, q % 2)
                return 0

            lax.fori_loop(0, steps, step, 0)
        del done, slots

    def spot(k, expert):
        j, m, i = k // (3 * PER), (k // PER) % 3, k % PER
        return out.at[m, expert + j, pl.ds(i * CHUNK, CHUNK)]

    def load_a(k):
        j, m, i = k // (3 * PER), (k // PER) % 3, k % PER
        return pltpu.make_async_copy(
            gr.at[j, m, pl.ds(y * HALF + i * CHUNK, CHUNK)], VA.at[k % 2], ld_a.at[k % 2]
        )

    def load_b(k):
        return pltpu.make_async_copy(ya.at[k], VB.at[k % 2], ld_b.at[k % 2])

    def load_z(k):
        return pltpu.make_async_copy(za.at[k], VZ.at[k % 2], ld_z.at[k % 2])

    def load_f(k):
        return pltpu.make_async_copy(zb.at[k], VF.at[k % 2], ld_f.at[k % 2])

    def z1_copy(k):
        return remote(VS.at[k % 4], za.at[k], z1_s.at[k], z1_r.at[k], zdev)

    def z2_copy(k):
        return remote(VT.at[k % 4], zb.at[k], z2_s.at[k], z2_r.at[k], mdev)

    def z3_copy(k):
        return remote(FN.at[k % 4], spot(k, e0), z3_s.at[k], z3_r.at[k], zdev)

    def store_f(k):
        return pltpu.make_async_copy(FN.at[k % 4], spot(k, e0), fo.at[k % 4])

    def x_copy(k):
        return remote(spot(k, e0), spot(k, e0), x_s.at[k], x_r.at[k], xdev)

    def c1_copy(k):
        return remote(spot(k, e0), spot(k, e0), c1_s.at[k], c1_r.at[k], cdev)

    def c2_copy(k):
        other = 2 * (2 * (1 - x) + c)
        return remote(spot(k, other), spot(k, other), c2_s.at[k], c2_r.at[k], cdev)

    def when(k, cond=None):
        ok = (k >= 0) & (k < CHUNKS)
        return pl.when(ok if cond is None else ok & cond)

    def slot(s):
        k_cx = s - 11

        @when(k_cx)
        def _():
            x_copy(k_cx).wait_recv()
            c2_copy(k_cx).start()

        k_x = s - 9

        @when(k_x, mid)
        def _():
            store_f(k_x).wait()
            z3_copy(k_x).wait_send()

        @when(k_x, jnp.logical_not(mid))
        def _():
            z3_copy(k_x).wait_recv()

        @when(k_x)
        def _():
            x_copy(k_x).start()
            c1_copy(k_x).start()

        k_fa = s - 7

        @when(k_fa, mid)
        def _():
            load_f(k_fa).wait()
            z2_copy(k_fa).wait_send()
            FN[k_fa % 4] = (VT[k_fa % 4].astype(f32) + VF[k_fa % 2].astype(f32)).astype(bf16)
            z3_copy(k_fa).start()
            store_f(k_fa).start()

        k_fl = s - 6

        @when(k_fl, mid)
        def _():
            z2_copy(k_fl).wait_recv()
            load_f(k_fl).start()

        k_za = s - 4

        @when(k_za, mid)
        def _():
            load_z(k_za).wait()
            VT[k_za % 4] = (VS[k_za % 4].astype(f32) + VZ[k_za % 2].astype(f32)).astype(bf16)
            z2_copy(k_za).start()

        k_zl = s - 3

        @when(k_zl, mid)
        def _():
            z1_copy(k_zl).wait_recv()
            load_z(k_zl).start()

        @when(s - 5, jnp.logical_not(mid))
        def _():
            z1_copy(s - 5).wait_send()

        k_a = s - 1

        @when(k_a)
        def _():
            load_a(k_a).wait()
            load_b(k_a).wait()
            VS[k_a % 4] = (VA[k_a % 2].astype(f32) + VB[k_a % 2].astype(f32)).astype(bf16)

        @when(k_a, jnp.logical_not(mid))
        def _():
            z1_copy(k_a).start()

        @when(s)
        def _():
            y_copy(s).wait_recv()
            load_a(s).start()
            load_b(s).start()

    def slots(first, last):
        def step(s, _):
            slot(s)
            return 0

        lax.fori_loop(first, last, step, 0)

    own[1].wait()
    own[2].wait()
    own[0].wait()
    for m in range(3):
        own[6 + m].wait()
    hc.wait_recv()
    forward(0, 0)
    hx.wait_recv()
    hd = remote(
        H.at[pl.ds(2 * ROWS, ROWS)], H.at[pl.ds(3 * ROWS, ROWS)], h_s.at[2], h_r.at[2], cdev
    )
    hd.start()
    wzs = []
    for m in range(3):
        wys[m].wait_recv()
        rows = pl.ds((1 - y) * HALF + h * 384, 384)
        wzs.append(remote(W.at[1, m, rows], W.at[1, m, rows], wz_s.at[m], wz_r.at[m], zdev))
        wzs[m].start()
    hd.wait_recv()
    forward(0, 2 * ROWS)
    weight_grads(0, 0)
    for m in range(3):
        wzs[m].wait_recv()
        own[3 + m].wait()
    forward(1, 0)
    slots(0, 2)
    forward(1, 2 * ROWS)
    slots(2, 4)

    def tail(buffer_r, rows):
        buffer_r[:, MODEL_WIDTH:] = DG[rows, :]

    third, second = pl.ds(3 * ROWS, ROWS), pl.ds(2 * ROWS, ROWS)

    def rc_copy(t, which):
        ns = pl.ds(pl.multiple_of(t * 512, 512), 512)
        src, dst = ((RS, CR), (OS, CO))[which]
        return remote(
            src.at[t % 2], dst.at[:, ns], rc_s.at[which, t], rc_r.at[which, t], cdev
        )

    for t in range(3):
        ns = pl.ds(t * 512, 512)
        if t == 2:
            rc_copy(0, 0).wait_send()
            rc_copy(0, 1).wait_send()
        o, d = back_rows(third, ns)
        RS[t % 2] = d.astype(bf16)
        OS[t % 2] = o.astype(bf16)
        rc_copy(t, 0).start()
        rc_copy(t, 1).start()
    dg_copy = remote(
        DG.at[third], CR.at[:, pl.ds(MODEL_WIDTH, PAD)], rd_s.at[0], rd_r.at[0], cdev
    )
    dg_copy.start()
    slots(4, 6)
    for t in range(3):
        ns = pl.ds(t * 512, 512)
        o, d = back_rows(second, ns)
        rc_copy(t, 0).wait_recv()
        rc_copy(t, 1).wait_recv()
        CR[:, ns] = (CR[:, ns].astype(f32) + d).astype(bf16)
        CO[:, ns] = (CO[:, ns].astype(f32) + o).astype(bf16)
    dg_copy.wait_recv()
    CR[:, MODEL_WIDTH:] = CR[:, MODEL_WIDTH:] + DG[second, :]
    rx = remote(CR, r_x, rx_s.at[0], rx_r.at[0], xdev)
    ox = remote(CO, o_x, rx_s.at[1], rx_r.at[1], xdev)
    rx.start()
    ox.start()
    slots(6, 8)
    weight_grads(1, 0)
    slots(8, 10)
    for which, (src, dst) in enumerate(((RS, CR), (OS, CO))):
        for t in (1, 2):
            rc_copy(t, which).wait_send()
    dg_copy.wait_send()

    def rb_copy(t, which):
        src, dst = ((RS, r_core), (OS, o_core))[which]
        return remote(
            src.at[t % 2],
            dst.at[:, pl.ds(t * 512, 512)],
            rd_s.at[1 + which * 3 + t],
            rd_r.at[1 + which * 3 + t],
            cdev,
        )

    def ro_copy(t, which):
        src, dst = ((RS, r_own), (OS, o_own))[which]
        return pltpu.make_async_copy(
            src.at[t % 2], dst.at[:, pl.ds(t * 512, 512)], ro.at[which, t]
        )

    first = pl.ds(ROWS, ROWS)
    tail_b = remote(
        DG.at[first], r_core.at[:, pl.ds(MODEL_WIDTH, PAD)], rd_s.at[7], rd_r.at[7], cdev
    )
    tail_b.start()
    tail_o = pltpu.make_async_copy(
        DG.at[pl.ds(0, ROWS)], r_own.at[:, pl.ds(MODEL_WIDTH, PAD)], ro.at[0, 3]
    )
    tail_o.start()
    for t in range(3):
        if t == 2:
            rb_copy(0, 0).wait_send()
            rb_copy(0, 1).wait_send()
        o, d = back_rows(first, pl.ds(t * 512, 512))
        RS[t % 2] = d.astype(bf16)
        OS[t % 2] = o.astype(bf16)
        rb_copy(t, 0).start()
        rb_copy(t, 1).start()
    slots(10, 12)
    for t in range(3):
        if t < 2:
            rb_copy(2 - t, 0).wait_send()
            rb_copy(2 - t, 1).wait_send()
        else:
            ro_copy(0, 0).wait()
            ro_copy(0, 1).wait()
        o, d = back_rows(pl.ds(0, ROWS), pl.ds(t * 512, 512))
        RS[t % 2] = d.astype(bf16)
        OS[t % 2] = o.astype(bf16)
        ro_copy(t, 0).start()
        ro_copy(t, 1).start()
    slots(12, CHUNKS + 11)
    for which in range(2):
        for t in (1, 2):
            ro_copy(t, which).wait()
        for t in range(3):
            rb_copy(t, which).wait_recv()
    tail_b.wait()
    tail_o.wait()
    rx.wait()
    ox.wait()

    def finish(k, _):
        x_copy(k).wait_send()
        c1_copy(k).wait()
        c2_copy(k).wait()
        y_copy(k).wait_send()
        return 0

    lax.fori_loop(0, CHUNKS, finish, 0)
    for m in range(3):
        wys[m].wait_send()
        wzs[m].wait_send()
    hx.wait_send()
    hc.wait_send()
    hd.wait_send()


def expert_call(hg, g4, w0, wg, wu, wd):
    anyspace = pl.BlockSpec(memory_space=pl.ANY)
    dma = pltpu.SemaphoreType.DMA
    vmem = lambda *s: pltpu.VMEM(s, bf16)
    shapes = [(ROWS, WIDE)] * 3 + [(ROWS, MODEL_WIDTH)] * 3
    shapes += [(3, 8, HALF, FF), (2, 3, MODEL_WIDTH, FF)] + [(CHUNKS, CHUNK, FF)] * 3
    scratch = [
        vmem(4 * ROWS, WIDE),
        vmem(4 * ROWS, MODEL_WIDTH),
        vmem(2, 3, MODEL_WIDTH, FF),
        vmem(2, 3, 4 * ROWS, FF),
        vmem(4 * ROWS, PAD),
        vmem(2, ROWS, 512),
        vmem(2, ROWS, 512),
        vmem(ROWS, WIDE),
        vmem(ROWS, MODEL_WIDTH),
        vmem(2, 384, FF),
        vmem(2, CHUNK, FF),
        vmem(2, CHUNK, FF),
        vmem(4, CHUNK, FF),
        vmem(2, CHUNK, FF),
        vmem(4, CHUNK, FF),
        vmem(2, CHUNK, FF),
        vmem(4, CHUNK, FF),
        dma((9,)), dma((3,)), dma((3,)), dma((3,)), dma((3,)), dma((3,)), dma((3,)),
        dma((2,)), dma((CHUNKS,)), dma((CHUNKS,)), dma((2,)), dma((2,)),
        dma((CHUNKS,)), dma((CHUNKS,)), dma((2,)), dma((CHUNKS,)), dma((CHUNKS,)), dma((2,)),
        dma((CHUNKS,)), dma((CHUNKS,)), dma((4,)), dma((CHUNKS,)), dma((CHUNKS,)),
        dma((CHUNKS,)), dma((CHUNKS,)), dma((CHUNKS,)), dma((CHUNKS,)),
        dma((2, 3)), dma((2, 3)), dma((2,)), dma((2,)), dma((8,)), dma((8,)), dma((2, 4)),
    ]
    return pl.pallas_call(
        expert_kernel,
        out_shape=[jax.ShapeDtypeStruct(s, bf16) for s in shapes],
        in_specs=[anyspace] * 6,
        out_specs=[anyspace] * len(shapes),
        scratch_shapes=scratch,
        compiler_params=pltpu.CompilerParams(
            collective_id=2, has_side_effects=True, vmem_limit_bytes=66 * 1000 * 1000
        ),
        name="experts",
    )(hg, g4, w0, wg, wu, wd)[:7]


BLOCKS = 7
WIDTH = 512
SIXTH = 192


def attention_kernel(
    d, sm, out, smo, ca, ya, xa, za, zb, sa, VA, VB, PP, VY, QQ, VX, VS, VZ, VT, VF, FN, SA, SB, SC,
    loc, c_s, c_r, ld, y_s, y_r, ldy, x_s, x_r, ldx, z1_s, z1_r, ldz, z2_s, z2_r, ldf, z3_s, z3_r,
    fo, xg_s, xg_r, c1_s, c1_r, c2_s, c2_r, s_s, s_r, sl,
):
    z, x, c, y = place()
    mid = (z == 1) | (z == 2)
    ydev, xdev, cdev = at(z, x, c, 1 - y), at(z, 1 - x, c, y), at(z, x, 1 - c, y)
    zdev = at(z + 1 - 2 * (z % 2), x, c, y)
    mdev = at(3 - z, x, c, y)
    greet((ydev, xdev, cdev, zdev, mdev))

    def c_copy(k):
        return remote(
            d.at[k, :, pl.ds((1 - c) * 384, 384)], ca.at[k], c_s.at[k], c_r.at[k], cdev
        )

    def load_a(k):
        return pltpu.make_async_copy(
            d.at[k, :, pl.ds(c * 384, 384)], VA.at[k % 2], ld.at[0, k % 2]
        )

    def load_b(k):
        return pltpu.make_async_copy(ca.at[k], VB.at[k % 2], ld.at[1, k % 2])

    def y_copy(k):
        return remote(PP.at[k % 4, 1 - y], ya.at[k], y_s.at[k], y_r.at[k], ydev)

    def load_y(k):
        return pltpu.make_async_copy(ya.at[k], VY.at[k % 2], ldy.at[k % 2])

    def x_copy(k):
        return remote(
            QQ.at[k % 4, pl.ds((1 - x) * SIXTH, SIXTH)], xa.at[k], x_s.at[k], x_r.at[k], xdev
        )

    def load_x(k):
        return pltpu.make_async_copy(xa.at[k], VX.at[k % 2], ldx.at[k % 2])

    def z1_copy(k):
        return remote(VS.at[k % 8], za.at[k], z1_s.at[k], z1_r.at[k], zdev)

    def load_z(k):
        return pltpu.make_async_copy(za.at[k], VZ.at[k % 2], ldz.at[k % 2])

    def z2_copy(k):
        return remote(VT.at[k % 4], zb.at[k], z2_s.at[k], z2_r.at[k], mdev)

    def load_f(k):
        return pltpu.make_async_copy(zb.at[k], VF.at[k % 2], ldf.at[k % 2])

    def spot(k, xx, cc):
        return out.at[k, pl.ds(cc * 384 + xx * SIXTH, SIXTH)]

    def z3_copy(k):
        return remote(FN.at[k % 4], spot(k, x, c), z3_s.at[k], z3_r.at[k], zdev)

    def store_f(k):
        return pltpu.make_async_copy(FN.at[k % 4], spot(k, x, c), fo.at[k % 4])

    def xg_copy(k):
        return remote(spot(k, x, c), spot(k, x, c), xg_s.at[k], xg_r.at[k], xdev)

    def c1_copy(k):
        return remote(spot(k, x, c), spot(k, x, c), c1_s.at[k], c1_r.at[k], cdev)

    def c2_copy(k):
        return remote(spot(k, 1 - x, c), spot(k, 1 - x, c), c2_s.at[k], c2_r.at[k], cdev)

    def when(k, cond=None):
        ok = (k >= 0) & (k < BLOCKS)
        return pl.when(ok if cond is None else ok & cond)

    def slot(s):
        @when(s - 13)
        def _():
            xg_copy(s - 13).wait_recv()
            c2_copy(s - 13).start()

        @when(s - 12, mid)
        def _():
            store_f(s - 12).wait()
            z3_copy(s - 12).wait_send()

        @when(s - 12, jnp.logical_not(mid))
        def _():
            z3_copy(s - 12).wait_recv()
            z1_copy(s - 12).wait_send()

        @when(s - 12)
        def _():
            xg_copy(s - 12).start()
            c1_copy(s - 12).start()

        @when(s - 10, mid)
        def _():
            k = s - 10
            load_f(k).wait()
            z2_copy(k).wait_send()
            FN[k % 4] = (VT[k % 4].astype(f32) + VF[k % 2].astype(f32)).astype(bf16)
            z3_copy(k).start()
            store_f(k).start()

        @when(s - 9, mid)
        def _():
            z2_copy(s - 9).wait_recv()
            load_f(s - 9).start()

        @when(s - 8, mid)
        def _():
            k = s - 8
            load_z(k).wait()
            VT[k % 4] = (VS[k % 8].astype(f32) + VZ[k % 2].astype(f32)).astype(bf16)
            z2_copy(k).start()

        @when(s - 7, mid)
        def _():
            z1_copy(s - 7).wait_recv()
            load_z(s - 7).start()

        @when(s - 6)
        def _():
            k = s - 6
            load_x(k).wait()
            x_copy(k).wait_send()
            mine = pl.ds(pl.multiple_of(x * SIXTH, SIXTH), SIXTH)
            VS[k % 8] = (QQ[k % 4, mine, :].astype(f32) + VX[k % 2].astype(f32)).astype(bf16)

        @when(s - 6, jnp.logical_not(mid))
        def _():
            z1_copy(s - 6).start()

        @when(s - 5)
        def _():
            x_copy(s - 5).wait_recv()
            load_x(s - 5).start()

        @when(s - 4)
        def _():
            k = s - 4
            load_y(k).wait()
            y_copy(k).wait_send()
            QQ[k % 4] = (PP[k % 4, y].astype(f32) + VY[k % 2].astype(f32)).astype(bf16)
            x_copy(k).start()

        @when(s - 3)
        def _():
            y_copy(s - 3).wait_recv()
            load_y(s - 3).start()

        @when(s - 1)
        def _():
            k = s - 1
            load_a(k).wait()
            load_b(k).wait()
            PP[k % 4] = (VA[k % 2].astype(f32) + VB[k % 2].astype(f32)).astype(bf16)
            y_copy(k).start()

        @when(s)
        def _():
            c_copy(s).wait_recv()
            load_a(s).start()
            load_b(s).start()

    for k in range(BLOCKS):
        c_copy(k).start()

    first = pltpu.make_async_copy(sm, SA, sl.at[0])
    first.start()
    first.wait()

    def swap(i, device):
        copy = remote(SC, sa.at[i], s_s.at[i], s_r.at[i], device)
        copy.start()
        return copy

    def arrive(i):
        load = pltpu.make_async_copy(sa.at[i], SB, sl.at[0])
        load.start()
        load.wait()
        return SB[...].astype(f32)

    SC[...] = SA[...]
    hop = swap(0, cdev)
    hop.wait()
    SC[...] = (SC[...].astype(f32) + arrive(0)).astype(bf16)
    lax.fori_loop(0, 3, lambda s, _: (slot(s), 0)[1], 0)
    hop = swap(1, xdev)
    hop.wait()
    SC[...] = (SC[...].astype(f32) + arrive(1)).astype(bf16)
    lax.fori_loop(3, 5, lambda s, _: (slot(s), 0)[1], 0)
    hop = swap(2, ydev)
    hop.wait()
    SC[...] = (SC[...].astype(f32) + arrive(2)).astype(bf16)
    lax.fori_loop(5, 7, lambda s, _: (slot(s), 0)[1], 0)
    hop = swap(3, zdev)
    hop.wait()
    SC[...] = (SC[...].astype(f32) + arrive(3)).astype(bf16)
    lax.fori_loop(7, 9, lambda s, _: (slot(s), 0)[1], 0)
    hop = swap(4, mdev)
    hop.wait()
    SA[...] = (SC[...].astype(f32) + arrive(4)).astype(bf16)
    last = pltpu.make_async_copy(SA, smo, sl.at[1])
    last.start()
    lax.fori_loop(9, BLOCKS + 13, lambda s, _: (slot(s), 0)[1], 0)
    last.wait()

    def finish(k, _):
        c_copy(k).wait_send()
        xg_copy(k).wait_send()
        c1_copy(k).wait()
        c2_copy(k).wait()
        return 0

    lax.fori_loop(0, BLOCKS, finish, 0)


def attention_call(d, sm):
    anyspace = pl.BlockSpec(memory_space=pl.ANY)
    dma = pltpu.SemaphoreType.DMA
    vmem = lambda *s: pltpu.VMEM(s, bf16)
    n = BLOCKS
    shapes = [(n, HALF, WIDTH), (2, 16, HALF), (n, 2, 384, WIDTH), (n, 384, WIDTH)]
    shapes += [(n, SIXTH, WIDTH)] * 3 + [(5, 2, 16, HALF)]
    scratch = [
        vmem(2, 2, 384, WIDTH), vmem(2, 2, 384, WIDTH), vmem(4, 2, 384, WIDTH),
        vmem(2, 384, WIDTH), vmem(4, 384, WIDTH), vmem(2, SIXTH, WIDTH), vmem(8, SIXTH, WIDTH),
        vmem(2, SIXTH, WIDTH), vmem(4, SIXTH, WIDTH), vmem(2, SIXTH, WIDTH), vmem(4, SIXTH, WIDTH),
        vmem(2, 16, HALF), vmem(2, 16, HALF), vmem(2, 16, HALF),
        dma((1,)), dma((n,)), dma((n,)), dma((2, 2)), dma((n,)), dma((n,)), dma((2,)),
        dma((n,)), dma((n,)), dma((2,)), dma((n,)), dma((n,)), dma((2,)), dma((n,)), dma((n,)),
        dma((2,)), dma((n,)), dma((n,)), dma((4,)), dma((n,)), dma((n,)), dma((n,)), dma((n,)),
        dma((n,)), dma((n,)), dma((5,)), dma((5,)), dma((2,)),
    ]
    return pl.pallas_call(
        attention_kernel,
        out_shape=[jax.ShapeDtypeStruct(s, bf16) for s in shapes],
        in_specs=[anyspace] * 2,
        out_specs=[anyspace] * len(shapes),
        scratch_shapes=scratch,
        compiler_params=pltpu.CompilerParams(
            collective_id=3, has_side_effects=True, vmem_limit_bytes=40 * 1000 * 1000
        ),
        name="attention_sums",
    )(d, sm)[:2]


def attention_forward(hidden, segments, gain_one, w_q, w_k, w_v, w_o, gain_two):
    sequence_length = hidden.shape[0]
    group = QUERY_HEADS // KEY_VALUE_HEADS
    head_scale = HEAD_SIZE ** (-0.5)
    cosine, sine = tables(sequence_length, HEAD_SIZE)
    normed_f, scale_one = normalize(hidden, gain_one)
    h1 = normed_f.astype(bf16)
    qr = jnp.dot(h1, w_q, preferred_element_type=f32)
    kr = jnp.dot(h1, w_k, preferred_element_type=f32)
    values = jnp.dot(h1, w_v, preferred_element_type=f32).astype(bf16)
    values = values.reshape(sequence_length, KEY_VALUE_HEADS, HEAD_SIZE)
    qr = qr.reshape(sequence_length, QUERY_HEADS, HEAD_SIZE)
    kr = kr.reshape(sequence_length, KEY_VALUE_HEADS, HEAD_SIZE)
    queries = apply_rotary(qr, cosine, sine).astype(bf16)
    queries = queries.reshape(sequence_length, KEY_VALUE_HEADS, group, HEAD_SIZE)
    keys = apply_rotary(kr, cosine, sine).astype(bf16)
    position = jnp.arange(sequence_length)
    allowed = (position[None, :] <= position[:, None]) & (segments[:, None] == segments[None, :])
    scores = jnp.einsum("qkgd,skd->kgqs", queries, keys, preferred_element_type=f32) * head_scale
    scores = jnp.where(allowed, scores, -1e30)
    top_score = jnp.max(scores, axis=-1, keepdims=True)
    exp_scores = jnp.exp(scores - top_score)
    sum_exp = jnp.sum(exp_scores, axis=-1, keepdims=True)
    log_total = top_score + jnp.log(sum_exp)
    probs = (exp_scores / sum_exp).astype(bf16)
    mixed = jnp.einsum("kgqs,skd->qkgd", probs, values, preferred_element_type=f32)
    mixed = mixed.reshape(sequence_length, QUERY_HEADS * HEAD_SIZE).astype(bf16)
    middle = hidden + jnp.dot(mixed, w_o, preferred_element_type=f32)
    normed_two_f, scale_two = normalize(middle, gain_two)
    h2 = normed_two_f.astype(bf16)
    kept = (scale_one, h1, queries, keys, values, allowed, log_total, mixed, middle, scale_two)
    return h2, kept


def router_forward(h2, w_router, routes):
    logits = jnp.dot(h2, w_router, preferred_element_type=f32)
    probs = softmax_rows(logits)
    experts = w_router.shape[1]
    chosen = jnp.any(
        routes[:, :, None] == jnp.arange(experts, dtype=jnp.int32)[None, None, :], axis=1
    )
    picked = jnp.where(chosen, probs, 0.0)
    total = jnp.sum(picked, axis=-1, keepdims=True)
    return probs, chosen, total, picked / total


def router_backward(h2, w_router, probs, chosen, total, gates, gate_grads):
    gate_grads = jnp.where(chosen, gate_grads, 0.0)
    weighted = jnp.sum(gate_grads * gates, axis=-1, keepdims=True)
    prob_grad = jnp.where(chosen, (gate_grads - weighted) / total, 0.0)
    logit_grad = probs * (prob_grad - jnp.sum(prob_grad * probs, axis=-1, keepdims=True))
    logit_grad = logit_grad.astype(bf16)
    return contract(h2, logit_grad, 0, 0), contract(logit_grad, w_router, 1, 1)


def attention_backward(hidden, kept, gain_one, w_q, w_k, w_v, w_o, gain_two, upstream, dh2):
    scale_one, h1, queries, keys, values, allowed, log_total, mixed, middle, scale_two = kept
    sequence_length = hidden.shape[0]
    group = QUERY_HEADS // KEY_VALUE_HEADS
    head_scale = HEAD_SIZE ** (-0.5)
    cosine, sine = tables(sequence_length, HEAD_SIZE)
    middle_norm_grad, gain_two_grad = norm_back(middle, scale_two, gain_two, dh2)
    middle_grad = upstream + middle_norm_grad
    branch_grad = middle_grad.astype(bf16)
    out_proj_sum = contract(mixed, branch_grad, 0, 0)
    mixed_grad = contract(branch_grad, w_o, 1, 1).astype(bf16)
    mixed_grad = mixed_grad.reshape(sequence_length, KEY_VALUE_HEADS, group, HEAD_SIZE)
    probs = jnp.exp(
        jnp.einsum("qkgd,skd->kgqs", queries, keys, preferred_element_type=f32) * head_scale
        - log_total
    )
    probs = jnp.where(allowed, probs, 0.0)
    prob_back = jnp.einsum("qkgd,skd->kgqs", mixed_grad, values, preferred_element_type=f32)
    score_grad = probs * (prob_back - jnp.sum(prob_back * probs, axis=-1, keepdims=True))
    score_grad = score_grad.astype(bf16)
    dq = jnp.einsum("kgqs,skd->qkgd", score_grad, keys, preferred_element_type=f32) * head_scale
    dq = dq.reshape(sequence_length, QUERY_HEADS, HEAD_SIZE)
    dq = apply_rotary(dq, cosine, -sine).astype(bf16)
    dq = dq.reshape(sequence_length, QUERY_HEADS * HEAD_SIZE)
    dk = jnp.einsum("kgqs,qkgd->skd", score_grad, queries, preferred_element_type=f32) * head_scale
    dk = apply_rotary(dk, cosine, -sine).astype(bf16)
    dk = dk.reshape(sequence_length, KEY_VALUE_HEADS * HEAD_SIZE)
    dv = jnp.einsum("kgqs,qkgd->skd", probs.astype(bf16), mixed_grad, preferred_element_type=f32)
    dv = dv.astype(bf16).reshape(sequence_length, KEY_VALUE_HEADS * HEAD_SIZE)
    query_sum = contract(h1, dq, 0, 0)
    key_sum = contract(h1, dk, 0, 0)
    value_sum = contract(h1, dv, 0, 0)
    dh1 = contract(dq, w_q, 1, 1) + contract(dk, w_k, 1, 1) + contract(dv, w_v, 1, 1)
    hidden_norm_grad, gain_one_grad = norm_back(hidden, scale_one, gain_one, dh1)
    hidden_grad = (middle_grad + hidden_norm_grad).astype(bf16)
    return hidden_grad, (
        gain_one_grad,
        query_sum,
        key_sum,
        value_sum,
        out_proj_sum,
        gain_two_grad,
    )


def reduce_over_all(value, dimension):
    value = lax.psum_scatter(
        value.astype(bf16), "shard", scatter_dimension=dimension, tiled=True
    ).astype(f32)
    return lax.psum(value.astype(bf16), "rep").astype(f32)


def local(
    hidden_in,
    segment_ids,
    routes,
    out_grad,
    norm1_gain,
    w_query,
    key_weight,
    value_weight,
    w_out,
    norm2_gain,
    w_router,
    w_gate,
    w_up,
    w_down,
):
    small = jnp.concatenate(
        [norm1_gain[None], norm2_gain[None], w_router.T, jnp.zeros((6, HALF), bf16)], axis=0
    )
    w_q, w_k, w_v, w_o, small, g4, w0 = gather_call(
        w_query, key_weight, value_weight, w_out, small, out_grad, w_gate, w_up, w_down
    )
    whole = lambda w: w.reshape(MODEL_WIDTH, w.shape[-1])
    w_q, w_k, w_v, w_o = whole(w_q), whole(w_k), whole(w_v), whole(w_o)
    small = small.transpose(1, 0, 2).reshape(16, MODEL_WIDTH)
    gain_one, gain_two = small[0].astype(f32), small[1].astype(f32)
    router = small[2:10].T
    hidden = hidden_in.astype(f32)
    h2, kept = attention_forward(
        hidden, segment_ids[0], gain_one, w_q, w_k, w_v, w_o, gain_two
    )
    probs, chosen, total, gates = router_forward(h2, router, routes)
    high = gates.astype(bf16)
    low = (gates - high.astype(f32)).astype(bf16)
    hg = jnp.concatenate([h2, high, low, jnp.zeros((ROWS, PAD - 16), bf16)], axis=1)
    r_own, r_core, r_x, o_own, o_core, o_x, grads = expert_call(
        hg, g4.reshape(4 * ROWS, MODEL_WIDTH), w0, w_gate, w_up, w_down
    )
    add = lambda a, b, c: a.astype(f32) + b.astype(f32) + c.astype(f32)
    middle = kept[8]
    hidden_out = (middle + add(o_own, o_core, o_x)).astype(bf16)
    returned = add(r_own, r_core, r_x)
    gate_grads = returned[:, 1536:1544] + returned[:, 1544:1552]
    router_sum, routed = router_backward(h2, router, probs, chosen, total, gates, gate_grads)
    dh2 = routed + returned[:, :MODEL_WIDTH]
    hidden_grad, sums = attention_backward(
        hidden, kept, gain_one, w_q, w_k, w_v, w_o, gain_two, out_grad.astype(f32), dh2
    )
    gain_one_sum, query_sum, key_sum, value_sum, out_sum, gain_two_sum = sums
    d = jnp.concatenate([query_sum, key_sum, value_sum, out_sum], axis=1).astype(bf16)
    d = d.reshape(2, HALF, BLOCKS, WIDTH).transpose(2, 0, 1, 3)
    sm = jnp.concatenate(
        [gain_one_sum[None], gain_two_sum[None], router_sum.T, jnp.zeros((6, MODEL_WIDTH), f32)],
        axis=0,
    )
    sm = sm.astype(bf16).reshape(16, 2, HALF).transpose(1, 0, 2)
    d, sm = attention_call(d, sm)
    d = d.transpose(1, 0, 2).reshape(HALF, BLOCKS * WIDTH).astype(f32)
    sm = lax.dynamic_index_in_dim(sm, lax.axis_index("shard"), 0, keepdims=False).astype(f32)
    attn = (sm[0], d[:, :1536], d[:, 1536:1792], d[:, 1792:2048], d[:, 2048:], sm[1], sm[2:10].T)
    grads = [grads[m].astype(f32) for m in range(3)]
    return (hidden_out, hidden_grad, *attn, *grads)


def local_any(
    hidden_in,
    segment_ids,
    routes,
    out_grad,
    norm1_gain,
    w_query,
    key_weight,
    value_weight,
    w_out,
    norm2_gain,
    w_router,
    w_gate,
    w_up,
    w_down,
):
    wide = lambda w, axis: lax.all_gather(w, "shard", axis=axis, tiled=True)
    gain_one, gain_two = wide(norm1_gain, 0).astype(f32), wide(norm2_gain, 0).astype(f32)
    w_q, w_k, w_v, w_o = (wide(w, 0) for w in (w_query, key_weight, value_weight, w_out))
    router = wide(w_router, 0)
    hidden = hidden_in.astype(f32)
    h2, kept = attention_forward(
        hidden, segment_ids[0], gain_one, w_q, w_k, w_v, w_o, gain_two
    )
    probs, chosen, total, gates = router_forward(h2, router, routes)
    full = [wide(w, 1) for w in (w_gate, w_up, w_down)]

    def expert(carry, inputs):
        mixed, dh2 = carry
        gate_weight, up_weight, down_weight, gate = inputs
        gate = gate[:, None]
        ug = jnp.dot(h2, gate_weight, preferred_element_type=f32)
        uu = jnp.dot(h2, up_weight, preferred_element_type=f32)
        dh = jnp.dot(out_grad, down_weight, preferred_element_type=f32)
        sigma = jax.nn.sigmoid(ug)
        silu = ug * sigma
        hid = silu * uu
        gate_grad = jnp.sum(hid * dh, axis=1)
        hidden_rows = (hid * gate).astype(bf16)
        dug = (dh * gate * uu * sigma * (1.0 + ug * (1.0 - sigma))).astype(bf16)
        duu = (dh * gate * silu).astype(bf16)
        mixed = mixed + contract(hidden_rows, down_weight, 1, 1)
        dh2 = dh2 + contract(dug, gate_weight, 1, 1) + contract(duu, up_weight, 1, 1)
        sums = (contract(h2, dug, 0, 0), contract(h2, duu, 0, 0))
        sums = sums + (contract(out_grad, hidden_rows, 0, 0),)
        return (mixed, dh2), (gate_grad, *(s.astype(bf16) for s in sums))

    zeros = jnp.zeros(hidden.shape, f32)
    (mixed, dh2), (gate_grads, *sums) = lax.scan(expert, (zeros, zeros), (*full, gates.T))
    hidden_out = (kept[8] + mixed).astype(bf16)
    router_sum, routed = router_backward(h2, router, probs, chosen, total, gates, gate_grads.T)
    hidden_grad, attn = attention_backward(
        hidden, kept, gain_one, w_q, w_k, w_v, w_o, gain_two, out_grad.astype(f32), routed + dh2
    )
    attn = [reduce_over_all(value, 0) for value in attn + (router_sum,)]
    grads = [reduce_over_all(value, 1) for value in sums]
    return (hidden_out, hidden_grad, *attn, *grads)


def solution(mesh):
    rows, vector, matrix = P(("rep", "shard"), None), P("shard"), P("shard", None)
    stack = P(None, "shard", None)
    in_specs = (
        rows, rows, rows, rows, vector, matrix, matrix, matrix, matrix, vector, matrix,
        stack, stack, stack,
    )
    out_specs = (
        rows, rows, vector, matrix, matrix, matrix, matrix, vector, matrix, stack, stack, stack,
    )
    fits = dict(mesh.shape) == {"rep": 16, "shard": 2}
    body = local if fits else local_any
    return jax.shard_map(body, mesh=mesh, in_specs=in_specs, out_specs=out_specs, check_vma=False)
```

```python
import functools

import jax
import jax.numpy as jnp
from jax import lax
from jax.experimental import pallas as pl
from jax.experimental.pallas import tpu as pltpu
from jax.sharding import PartitionSpec as P

MODEL_WIDTH = 1536
QUERY_HEADS = 12
KEY_VALUE_HEADS = 2
HEAD_SIZE = 128
TOPK = 4
FF = 768
HALF = 768
ROWS = 512
PAD = 128
WIDE = MODEL_WIDTH + PAD
CHUNK = 96
PER = HALF // CHUNK
CHUNKS = 6 * PER

epsilon = 1e-06
rope_base = 1000000.0
MESH = pl.DeviceIdType.MESH
bf16 = jnp.bfloat16
f32 = jnp.float32


def tables(sequence_length, row_width):
    frequency = rope_base ** (-2.0 * jnp.arange(row_width // 2, dtype=jnp.float32) / row_width)
    angles = jnp.arange(sequence_length, dtype=jnp.float32)[:, None] * frequency[None, :]
    angles = jnp.concatenate([angles, angles], axis=-1)
    return (jnp.cos(angles)[:, None, :], jnp.sin(angles)[:, None, :])


def apply_rotary(values, rotary_cosine, rotary_sine):
    half_width = values.shape[-1] // 2
    turned = jnp.concatenate([-values[..., half_width:], values[..., :half_width]], axis=-1)
    return values * rotary_cosine + turned * rotary_sine


def contract(left_side, right_side, left_dim, right_dim):
    return lax.dot_general(
        left_side,
        right_side,
        (((left_dim,), (right_dim,)), ((), ())),
        preferred_element_type=jnp.float32,
    )


def normalize(values, gain_vector):
    scale_rows = lax.rsqrt(jnp.mean(values * values, axis=-1, keepdims=True) + epsilon)
    return (values * scale_rows * gain_vector, scale_rows)


def norm_back(values, scale_rows, gain_vector, upstream):
    scaled = upstream * gain_vector
    gain_grad = jnp.sum(upstream * values * scale_rows, axis=0)
    inner_sum = jnp.sum(scaled * values, axis=-1, keepdims=True)
    return (scaled * scale_rows - values * scale_rows**3 * inner_sum / values.shape[-1], gain_grad)


def softmax_rows(values):
    top_value = jnp.max(values, axis=-1, keepdims=True)
    exp_values = jnp.exp(values - top_value)
    return exp_values / jnp.sum(exp_values, axis=-1, keepdims=True)


def place():
    rep = lax.axis_index("rep")
    y = lax.axis_index("shard")
    return rep // 4, (rep // 2) % 2, rep % 2, y


def at(z, x, c, y):
    return ((z * 2 + x) * 2 + c, y)


def remote(src, dst, send, recv, device):
    return pltpu.make_async_remote_copy(
        src_ref=src,
        dst_ref=dst,
        send_sem=send,
        recv_sem=recv,
        device_id=device,
        device_id_type=MESH,
    )


def greet(partners):
    barrier = pltpu.get_barrier_semaphore()
    for device in partners:
        pl.semaphore_signal(barrier, inc=1, device_id=device, device_id_type=MESH)
    pl.semaphore_wait(barrier, len(partners))


def gather_kernel(
    wq, wk, wv, wo, sm, g, wg, wu, wd,
    wqf, wkf, wvf, wof, smf, g4, w0,
    bq, bk, bv, bo, bs, bg, loc, y_s, y_r, x_s, x_r, c_s, c_r, d_s, d_r, z_s, z_r,
):
    z, x, c, y = place()
    ydev, xdev, cdev = at(z, x, c, 1 - y), at(z, 1 - x, c, y), at(z, x, 1 - c, y)
    zdev = at(z + 1 - 2 * (z % 2), x, c, y)
    greet((ydev, xdev, cdev, zdev))
    parts, fulls, experts = (wq, wk, wv, wo), (wqf, wkf, wvf, wof), (wg, wu, wd)
    piece = HALF // 4
    mine = pl.ds((2 * x + c) * piece, piece)
    theirs = pl.ds((2 * (1 - x) + c) * piece, piece)
    expert = 2 * (2 * x + c)
    h = z % 2
    ys, xs, cs, ds, zs = [], [], [], [], []
    for a in range(4):
        ys.append(remote(parts[a].at[mine], fulls[a].at[y, mine], y_s.at[a], y_r.at[a], ydev))
        ys[a].start()
    ys.append(remote(sm, smf.at[y], y_s.at[4], y_r.at[4], ydev))
    ys[4].start()
    xs_g = remote(g, g4.at[2], x_s.at[4], x_r.at[4], xdev)
    cs_g = remote(g, g4.at[1], c_s.at[4], c_r.at[4], cdev)
    cs_g.start()
    for m in range(3):
        ys.append(
            remote(
                experts[m].at[expert, pl.ds(h * 384, 384)],
                w0.at[m, pl.ds(h * 384, 384)],
                y_s.at[5 + m],
                y_r.at[5 + m],
                ydev,
            )
        )
        ys[5 + m].start()
    pairs = [(parts[a], (bq, bk, bv, bo)[a], fulls[a].at[y]) for a in range(4)]
    pairs += [(sm, bs, smf.at[y]), (g, bg, g4.at[0])]
    loads = [pltpu.make_async_copy(p[0], p[1], loc.at[i]) for i, p in enumerate(pairs)]
    locs = [pltpu.make_async_copy(p[1], p[2], loc.at[6 + i]) for i, p in enumerate(pairs)]
    for copy in loads:
        copy.start()
    for i in range(6):
        loads[i].wait()
        locs[i].start()
    for a in range(4):
        ys[a].wait_recv()
        xs.append(
            remote(
                fulls[a].at[1 - y, mine], fulls[a].at[1 - y, mine], x_s.at[a], x_r.at[a], xdev
            )
        )
        cs.append(
            remote(
                fulls[a].at[1 - y, mine], fulls[a].at[1 - y, mine], c_s.at[a], c_r.at[a], cdev
            )
        )
        xs[a].start()
        cs[a].start()
    xs_g.start()
    for a in range(4):
        xs[a].wait_recv()
        ds.append(
            remote(
                fulls[a].at[1 - y, theirs], fulls[a].at[1 - y, theirs], d_s.at[a], d_r.at[a], cdev
            )
        )
        ds[a].start()
    for m in range(3):
        ys[5 + m].wait_recv()
        rows = pl.ds(h * 384, 384)
        zs.append(remote(w0.at[m, rows], w0.at[m, rows], z_s.at[m], z_r.at[m], zdev))
        zs[m].start()
    xs_g.wait_recv()
    ds_g = remote(g4.at[2], g4.at[3], d_s.at[4], d_r.at[4], cdev)
    ds_g.start()
    ys[4].wait_recv()
    for copy in ys:
        copy.wait_send()
    for copy in xs + [xs_g]:
        copy.wait_send()
    xs_g = None
    for copy in cs + [cs_g] + ds + [ds_g] + zs:
        copy.wait()
    for copy in locs:
        copy.wait()


def gather_call(wq, wk, wv, wo, sm, g, wg, wu, wd):
    anyspace = pl.BlockSpec(memory_space=pl.ANY)
    shapes = [
        (2, HALF, MODEL_WIDTH),
        (2, HALF, 256),
        (2, HALF, 256),
        (2, HALF, MODEL_WIDTH),
        (2, 16, HALF),
        (4, ROWS, MODEL_WIDTH),
        (3, HALF, FF),
    ]
    dma = pltpu.SemaphoreType.DMA
    return pl.pallas_call(
        gather_kernel,
        out_shape=[jax.ShapeDtypeStruct(s, bf16) for s in shapes],
        in_specs=[anyspace] * 9,
        out_specs=[anyspace] * 7,
        scratch_shapes=[
            pltpu.VMEM(s, bf16)
            for s in (
                (HALF, MODEL_WIDTH), (HALF, 256), (HALF, 256), (HALF, MODEL_WIDTH), (16, HALF),
                (ROWS, MODEL_WIDTH),
            )
        ]
        + [dma((12,)), dma((8,)), dma((8,))] + [dma((5,))] * 6 + [dma((3,))] * 2,
        compiler_params=pltpu.CompilerParams(collective_id=1, has_side_effects=True),
        name="gather_weights",
    )(wq, wk, wv, wo, sm, g, wg, wu, wd)


def nt_dot(a, b):
    return lax.dot_general(a, b, (((1,), (1,)), ((), ())), preferred_element_type=f32)


def tn_dot(a, b):
    return lax.dot_general(a, b, (((0,), (0,)), ((), ())), preferred_element_type=f32)


def turn_table(sine):
    sign = jnp.where(jnp.arange(HEAD_SIZE) < HEAD_SIZE // 2, -1.0, 1.0)
    return sine[:, 0, :] * sign[None, :]


def router_rows(h2, router_rows_t, routes):
    logits = nt_dot(h2, router_rows_t)
    lane = lax.broadcasted_iota(jnp.int32, logits.shape, 1)
    real = lane < 8
    logits = jnp.where(real, logits, -1e30)
    top = jnp.max(logits, axis=1, keepdims=True)
    exp_values = jnp.where(real, jnp.exp(logits - top), 0.0)
    probs = exp_values / jnp.sum(exp_values, axis=1, keepdims=True)
    chosen = lane == routes[:, 0:1]
    for k in range(1, 4):
        chosen = chosen | (lane == routes[:, k : k + 1])
    picked = jnp.where(chosen, probs, 0.0)
    total = jnp.sum(picked, axis=1, keepdims=True)
    return probs, chosen, total, picked / total


def middle_backward(returned, h2, rt, routes, y1, g, gain_two, DL, DY, DA, GS):
    GS[...] = jnp.zeros_like(GS)

    def step(b, _):
        rows = pl.ds(pl.multiple_of(b * 128, 128), 128)
        probs, chosen, total, gates = router_rows(h2(rows), rt[...], routes[rows, :])
        back = returned(rows)
        packed = back[:, MODEL_WIDTH:]
        gate_grads = jnp.where(chosen, packed + pltpu.roll(packed, PAD - 8, 1), 0.0)
        weighted = jnp.sum(gate_grads * gates, axis=1, keepdims=True)
        prob_grad = jnp.where(chosen, (gate_grads - weighted) / total, 0.0)
        inner = jnp.sum(prob_grad * probs, axis=1, keepdims=True)
        logit_grad = (probs * (prob_grad - inner)).astype(bf16)
        DL[rows, :] = logit_grad
        dh2 = back[:, :MODEL_WIDTH] + jnp.dot(logit_grad, rt[...], preferred_element_type=f32)
        v = y1[rows, :]
        r = lax.rsqrt(jnp.mean(v * v, axis=1, keepdims=True) + epsilon)
        GS[...] = GS[...] + jnp.sum(dh2 * v * r, axis=0, keepdims=True)
        scaled = dh2 * gain_two[...]
        along = jnp.sum(scaled * v, axis=1, keepdims=True)
        dy = g[rows, :].astype(f32) + (scaled * r - v * (r * r * r * along / MODEL_WIDTH))
        DY[rows, :] = dy
        DA[rows, :] = dy.astype(bf16)
        return 0

    lax.fori_loop(0, ROWS // 128, step, 0)


def heads_backward(Q, K, V, DOB, BIAS, LSE, COS, SIN, DQKV, DK, DV, tick):
    scale = HEAD_SIZE ** (-0.5)
    DK[...] = jnp.zeros_like(DK)
    DV[...] = jnp.zeros_like(DV)
    for group in range(2):
        shared = pl.ds(group * HEAD_SIZE, HEAD_SIZE)

        def head(n, _, group=group, shared=shared):
            columns = pl.ds(pl.multiple_of((group * 6 + n) * HEAD_SIZE, HEAD_SIZE), HEAD_SIZE)
            lane = lax.broadcasted_iota(jnp.int32, (ROWS, PAD), 1)
            lse = jnp.sum(
                jnp.where(lane == group * 6 + n, LSE[...], 0.0), axis=1, keepdims=True
            )
            for block in range(2):
                rows, keys = pl.ds(block * 256, 256), pl.ds(0, 256 * (block + 1))
                q, dob = Q[rows, columns], DOB[rows, columns]
                k, v = K[keys, shared], V[keys, shared]
                logits = nt_dot(q, k) * scale + BIAS[rows, keys]
                p = jnp.exp(logits - lse[block * 256 : block * 256 + 256])
                dp = nt_dot(dob, v)
                inner = jnp.sum(dp * p, axis=1, keepdims=True)
                ds = (p * (dp - inner)).astype(bf16)
                dq = jnp.dot(ds, k, preferred_element_type=f32) * scale
                dq = dq * COS[rows, :] - pltpu.roll(dq, 64, 1) * SIN[rows, :]
                DQKV[rows, columns] = dq.astype(bf16)
                DK[group, keys, :] = DK[group, keys, :] + tn_dot(ds, q)
                DV[group, keys, :] = DV[group, keys, :] + tn_dot(p.astype(bf16), dob)
            return 0

        for n in range(0, 6, 3):
            lax.fori_loop(n, n + 3, head, 0)
            tick()
        dk = DK[group] * scale
        dk = dk * COS[...] - pltpu.roll(dk, 64, 1) * SIN[...]
        DQKV[:, pl.ds(1536 + group * HEAD_SIZE, HEAD_SIZE)] = dk.astype(bf16)
        DQKV[:, pl.ds(1792 + group * HEAD_SIZE, HEAD_SIZE)] = DV[group].astype(bf16)


def first_backward(DH1, X, DY, gain_one, HG, GS):
    GS[...] = jnp.zeros_like(GS)

    def step(b, _):
        rows = pl.ds(pl.multiple_of(b * 128, 128), 128)
        v, up = X[rows, :].astype(f32), DH1[rows, :]
        r = lax.rsqrt(jnp.mean(v * v, axis=1, keepdims=True) + epsilon)
        GS[...] = GS[...] + jnp.sum(up * v * r, axis=0, keepdims=True)
        scaled = up * gain_one[...]
        along = jnp.sum(scaled * v, axis=1, keepdims=True)
        back = scaled * r - v * (r * r * r * along / MODEL_WIDTH)
        HG[rows, :] = (DY[rows, :] + back).astype(bf16)
        return 0

    lax.fori_loop(0, ROWS // 128, step, 0)


def mask_bias(seg_column, seg_row, BIAS):
    row = lax.broadcasted_iota(jnp.int32, (ROWS, ROWS), 0)
    column = lax.broadcasted_iota(jnp.int32, (ROWS, ROWS), 1)
    same = seg_column[:, 0:1] == seg_row[0:1, :]
    BIAS[...] = jnp.where((column <= row) & same, 0.0, -1e30)


BLOCKS = 7
PARTS = 2 * BLOCKS
WIDTH = 512
QUARTER = 96
EXPERT_SLOTS = CHUNKS + 14
PART_SLOTS = PARTS + 13


def layer_kernel(
    hg, g4, w0, wg, wu, wd, y1, xin, h1, q, k, v, ob, lse, cos, sin, rt, routes, gain1, gain2,
    segc, segr, wq, wk, wv, wo,
    o_own, o_core, o_x, out, aout, smo, hgrad,
    r_core, r_x, gr, ya, za, zb, d, ca, yb, xb, zc, zd, sa,
    H, W, DG, CR, CO, VA, VB, VS, VZ, VT, VF, FN, SM, SB,
    loc, h_s, h_r, wy_s, wy_r, wz_s, wz_r, stg_sem, y_s, y_r, ld_a, ld_b,
    z1_s, z1_r, ld_z, z2_s, z2_r, ld_f, z3_s, z3_r, fo, x_s, x_r, c1_s, c1_r, c2_s, c2_r,
    z4_s, z4_r, rc_s, rc_r, rx_s, rx_r, rd_s, rd_r, ro,
    ac_s, ac_r, ald, ay_s, ay_r, aldy, ax_s, ax_r, aldx, az1_s, az1_r, aldz, az2_s, az2_r, aldf,
    az3_s, az3_r, afo, axg_s, axg_r, ac1_s, ac1_r, ac2_s, ac2_r, s_s, s_r, sl, att,
):
    z, x, c, y = place()
    mid = (z == 1) | (z == 2)
    end = jnp.logical_not(mid)
    ydev, xdev, cdev = at(z, x, c, 1 - y), at(z, 1 - x, c, y), at(z, x, 1 - c, y)
    zdev = at(z + 1 - 2 * (z % 2), x, c, y)
    mdev = at(3 - z, x, c, y)
    greet((ydev, xdev, cdev, zdev, mdev))
    shards = (wg, wu, wd)
    e0 = 2 * (2 * x + c)
    other = 2 * (2 * (1 - x) + c)
    h = z % 2
    local_copy = pltpu.make_async_copy

    hx = remote(hg, H.at[pl.ds(2 * ROWS, ROWS)], h_s.at[0], h_r.at[0], xdev)
    hc = remote(hg, H.at[pl.ds(ROWS, ROWS)], h_s.at[1], h_r.at[1], cdev)
    hx.start()
    hc.start()

    def parts_of(n):
        return n // (3 * PER), (n // PER) % 3, n % PER

    def y_copy(n):
        j, m, i = parts_of(n)
        src = gr.at[j, m, pl.ds((1 - y) * HALF + i * CHUNK, CHUNK)]
        return remote(src, ya.at[n], y_s.at[n], y_r.at[n], ydev)

    def spot(n, expert):
        j, m, i = parts_of(n)
        return out.at[m, expert + j, pl.ds(i * CHUNK, CHUNK)]

    def load_a(n):
        j, m, i = parts_of(n)
        src = gr.at[j, m, pl.ds(y * HALF + i * CHUNK, CHUNK)]
        return local_copy(src, VA.at[n % 2], ld_a.at[n % 2])

    def load_b(n):
        return local_copy(ya.at[n], VB.at[n % 2], ld_b.at[n % 2])

    def load_z(n):
        return local_copy(za.at[n], VZ.at[n % 2], ld_z.at[n % 2])

    def load_f(n):
        return local_copy(zb.at[n], VF.at[n % 2], ld_f.at[n % 2])

    def z1_copy(n):
        return remote(VS.at[n % 4], za.at[n], z1_s.at[n], z1_r.at[n], zdev)

    def z2_copy(n):
        return remote(VT.at[n % 4], zb.at[n], z2_s.at[n], z2_r.at[n], mdev)

    def z3_copy(n):
        return remote(FN.at[n % 4], spot(n, e0), z3_s.at[n], z3_r.at[n], zdev)

    def z4_copy(n):
        return remote(spot(n, other), spot(n, other), z4_s.at[n], z4_r.at[n], zdev)

    def store_f(n):
        return local_copy(FN.at[n % 4], spot(n, e0), fo.at[n % 4])

    def x_copy(n):
        return remote(spot(n, e0), spot(n, e0), x_s.at[n], x_r.at[n], xdev)

    def c1_copy(n):
        return remote(spot(n, e0), spot(n, e0), c1_s.at[n], c1_r.at[n], cdev)

    def c2_copy(n):
        return remote(spot(n, other), spot(n, other), c2_s.at[n], c2_r.at[n], cdev)

    def crosses(n):
        return (n % 2 == 0) | ((n % 4 == 1) & mid) | ((n % 4 == 3) & end)

    def when(n, cond=None):
        ok = (n >= 0) & (n < CHUNKS)
        return pl.when(ok if cond is None else ok & cond)

    def slot(s):
        @when(s - 13, jnp.logical_not(crosses(s - 13 + 4 * CHUNKS)))
        def _():
            z4_copy(s - 13).wait_recv()
            c2_copy(s - 13).start()

        crossed = crosses(s - 11 + 4 * CHUNKS)

        @when(s - 11, crossed)
        def _():
            x_copy(s - 11).wait_recv()
            c2_copy(s - 11).start()

        @when(s - 11, crossed & ((s + 1) % 2 == 1))
        def _():
            z4_copy(s - 11).start()

        @when(s - 9, mid)
        def _():
            store_f(s - 9).wait()
            z3_copy(s - 9).wait_send()

        @when(s - 9, end)
        def _():
            z3_copy(s - 9).wait_recv()

        @when(s - 9, crosses(s - 9 + 4 * CHUNKS))
        def _():
            x_copy(s - 9).start()

        @when(s - 9)
        def _():
            c1_copy(s - 9).start()

        @when(s - 7, mid)
        def _():
            n = s - 7
            load_f(n).wait()
            z2_copy(n).wait_send()
            FN[n % 4] = (VT[n % 4].astype(f32) + VF[n % 2].astype(f32)).astype(bf16)
            z3_copy(n).start()
            store_f(n).start()

        @when(s - 6, mid)
        def _():
            z2_copy(s - 6).wait_recv()
            load_f(s - 6).start()

        @when(s - 4, mid)
        def _():
            n = s - 4
            load_z(n).wait()
            VT[n % 4] = (VS[n % 4].astype(f32) + VZ[n % 2].astype(f32)).astype(bf16)
            z2_copy(n).start()

        @when(s - 3, mid)
        def _():
            z1_copy(s - 3).wait_recv()
            load_z(s - 3).start()

        @when(s - 5, end)
        def _():
            z1_copy(s - 5).wait_send()

        @when(s - 1)
        def _():
            n = s - 1
            load_a(n).wait()
            load_b(n).wait()
            VS[n % 4] = (VA[n % 2].astype(f32) + VB[n % 2].astype(f32)).astype(bf16)

        @when(s - 1, end)
        def _():
            z1_copy(s - 1).start()

        @when(s)
        def _():
            y_copy(s).wait_recv()
            load_a(s).start()
            load_b(s).start()

    def slots(first, last):
        def step(s, _):
            slot(s)
            return 0

        lax.fori_loop(first, last, step, 0)

    third, second = pl.ds(3 * ROWS, ROWS), pl.ds(2 * ROWS, ROWS)
    first, zeroth = pl.ds(ROWS, ROWS), pl.ds(0, ROWS)

    def experts(G, ACT, STG, RS, OS):
        own = [
            local_copy(hg, H.at[pl.ds(0, ROWS)], loc.at[0]),
            local_copy(g4, G, loc.at[1]),
            local_copy(w0, W.at[0, :, pl.ds((1 - y) * HALF, HALF)], loc.at[2]),
        ]
        for m in range(3):
            own.append(
                local_copy(shards[m].at[e0 + 1], W.at[1, m, pl.ds(y * HALF, HALF)], loc.at[3 + m])
            )
        for m in range(3):
            own.append(
                local_copy(shards[m].at[e0], W.at[0, m, pl.ds(y * HALF, HALF)], loc.at[6 + m])
            )
        wys = []
        for m in range(3):
            wys.append(
                remote(
                    shards[m].at[e0 + 1, pl.ds(h * 384, 384)],
                    W.at[1, m, pl.ds(y * HALF + h * 384, 384)],
                    wy_s.at[m],
                    wy_r.at[m],
                    ydev,
                )
            )
            wys[m].start()
        for copy in own:
            copy.start()

        def gate_of(j, rows):
            lane = lax.broadcasted_iota(jnp.int32, (2 * ROWS, PAD), 1)
            packed = H[rows, MODEL_WIDTH:].astype(f32)
            picked = (lane == e0 + j) | (lane == e0 + j + 8)
            return jnp.sum(jnp.where(picked, packed, 0.0), axis=1, keepdims=True), lane

        def forward(j, begin, base=None):
            rows = pl.ds(begin, 2 * ROWS)
            gate, lane = gate_of(j, rows)

            def step(t, total):
                columns = pl.ds(pl.multiple_of(t * 256, 256), 256)
                ug = jnp.dot(
                    H[rows, :MODEL_WIDTH], W[j, 0, :, columns], preferred_element_type=f32
                )
                uu = jnp.dot(
                    H[rows, :MODEL_WIDTH], W[j, 1, :, columns], preferred_element_type=f32
                )
                dh = jnp.dot(G[rows, :], W[j, 2, :, columns], preferred_element_type=f32)
                sigma = jax.nn.sigmoid(ug)
                silu = ug * sigma
                hid = silu * uu
                ACT[j, 0, rows, columns] = (hid * gate).astype(bf16)
                dhg = dh * gate
                ACT[j, 1, rows, columns] = (
                    dhg * uu * sigma * (1.0 + ug * (1.0 - sigma))
                ).astype(bf16)
                ACT[j, 2, rows, columns] = (dhg * silu).astype(bf16)
                if base is not None:
                    slot(base + t)
                return total + jnp.sum(hid * dh, axis=1, keepdims=True)

            total = lax.fori_loop(0, FF // 256, step, jnp.zeros((2 * ROWS, 1), f32))
            high = total.astype(bf16).astype(f32)
            low = total - high
            here = jnp.where(lane == e0 + j, high, jnp.where(lane == e0 + j + 8, low, 0.0))
            if j == 0:
                DG[rows, :] = here.astype(bf16)
            else:
                DG[rows, :] = (DG[rows, :].astype(f32) + here).astype(bf16)

        def back_rows(rows, ns):
            o = nt_dot(ACT[0, 0, rows, :], W[0, 2, ns, :])
            o = o + nt_dot(ACT[1, 0, rows, :], W[1, 2, ns, :])
            e = nt_dot(ACT[0, 1, rows, :], W[0, 0, ns, :])
            e = e + nt_dot(ACT[0, 2, rows, :], W[0, 1, ns, :])
            e = e + nt_dot(ACT[1, 1, rows, :], W[1, 0, ns, :])
            e = e + nt_dot(ACT[1, 2, rows, :], W[1, 1, ns, :])
            return o, e

        def weight_tile(j, m, left, half, i, place_in):
            begin = half * HALF + i * 384
            lhs = left[:, pl.ds(pl.multiple_of(begin, 128), 384)]
            STG[place_in] = tn_dot(lhs, ACT[j, (m + 1) % 3]).astype(bf16)
            copy = local_copy(
                STG.at[place_in], gr.at[j, m, pl.ds(begin, 384)], stg_sem.at[place_in]
            )
            copy.start()
            return copy

        def weight_grads(j, base=None):
            done = 0
            for left, m0, steps in ((H, 0, 4), (G, 2, 2)):

                def step(n, _, left=left, m0=m0, done=done):
                    m, i = m0 + n // 2, n % 2
                    away = weight_tile(j, m, left, 1 - y, i, 0)
                    here = weight_tile(j, m, left, y, i, 1)
                    away.wait()
                    begin = (j * 3 + m) * PER + i * (384 // CHUNK)
                    for p in range(384 // CHUNK):
                        y_copy(begin + p).start()
                    if base is not None:
                        slot(base + done + n)
                    here.wait()
                    return 0

                lax.fori_loop(0, steps, step, 0)
                done += steps

        def rc_copy(t, which):
            ns = pl.ds(pl.multiple_of(t * 512, 512), 512)
            src, dst = ((RS, CR), (OS, CO))[which]
            return remote(
                src.at[t % 2], dst.at[:, ns], rc_s.at[which, t], rc_r.at[which, t], cdev
            )

        def rb_copy(t, which):
            ns = pl.ds(pl.multiple_of(t * 512, 512), 512)
            src, dst = ((RS, r_core), (OS, o_core))[which]
            return remote(
                src.at[t % 2], dst.at[:, ns], rd_s.at[1 + which * 3 + t],
                rd_r.at[1 + which * 3 + t], cdev,
            )

        def ro_copy(t):
            ns = pl.ds(pl.multiple_of(t * 512, 512), 512)
            return local_copy(OS.at[t % 2], o_own.at[:, ns], ro.at[t])

        own[1].wait()
        own[2].wait()
        own[0].wait()
        for m in range(3):
            own[6 + m].wait()
        hc.wait_recv()
        forward(0, 0)
        hx.wait_recv()
        hd = remote(H.at[second], H.at[third], h_s.at[2], h_r.at[2], cdev)
        hd.start()
        wzs = []
        for m in range(3):
            wys[m].wait_recv()
            rows = pl.ds((1 - y) * HALF + h * 384, 384)
            wzs.append(remote(W.at[1, m, rows], W.at[1, m, rows], wz_s.at[m], wz_r.at[m], zdev))
            wzs[m].start()
        hd.wait_recv()
        forward(0, 2 * ROWS)
        weight_grads(0)
        for m in range(3):
            wzs[m].wait_recv()
            own[3 + m].wait()
        forward(1, 0, 0)
        forward(1, 2 * ROWS, 3)

        def third_step(t, _):
            ns = pl.ds(pl.multiple_of(t * 512, 512), 512)

            @pl.when(t == 2)
            def _():
                rc_copy(0, 0).wait_send()
                rc_copy(0, 1).wait_send()

            o, e = back_rows(third, ns)
            RS[t % 2] = e.astype(bf16)
            OS[t % 2] = o.astype(bf16)
            rc_copy(t, 0).start()
            rc_copy(t, 1).start()
            slot(6 + t)
            return 0

        lax.fori_loop(0, 3, third_step, 0)
        dg_copy = remote(
            DG.at[third], CR.at[:, pl.ds(MODEL_WIDTH, PAD)], rd_s.at[0], rd_r.at[0], cdev
        )
        dg_copy.start()

        def second_step(t, _):
            ns = pl.ds(pl.multiple_of(t * 512, 512), 512)
            o, e = back_rows(second, ns)
            rc_copy(t, 0).wait_recv()
            rc_copy(t, 1).wait_recv()
            CR[:, ns] = (CR[:, ns].astype(f32) + e).astype(bf16)
            CO[:, ns] = (CO[:, ns].astype(f32) + o).astype(bf16)
            slot(9 + t)
            return 0

        lax.fori_loop(0, 3, second_step, 0)
        dg_copy.wait_recv()
        CR[:, MODEL_WIDTH:] = CR[:, MODEL_WIDTH:] + DG[second, :]
        rx.start()
        weight_grads(1, 12)
        for which in range(2):
            for t in (1, 2):
                rc_copy(t, which).wait_send()
        dg_copy.wait_send()
        tail_b.start()

        def first_step(t, _):
            ns = pl.ds(pl.multiple_of(t * 512, 512), 512)

            @pl.when(t == 2)
            def _():
                rb_copy(0, 0).wait_send()
                rb_copy(0, 1).wait_send()

            o, e = back_rows(first, ns)
            RS[t % 2] = e.astype(bf16)
            OS[t % 2] = o.astype(bf16)
            rb_copy(t, 0).start()
            rb_copy(t, 1).start()
            slot(18 + t)
            return 0

        lax.fori_loop(0, 3, first_step, 0)
        for t in (1, 2):
            rb_copy(t, 0).wait_send()
            rb_copy(t, 1).wait_send()

        def zeroth_step(t, _):
            ns = pl.ds(pl.multiple_of(t * 512, 512), 512)
            o, e = back_rows(zeroth, ns)

            @pl.when(t == 2)
            def _():
                ro_copy(0).wait()

            H[first, ns] = e.astype(bf16)
            OS[t % 2] = o.astype(bf16)
            ro_copy(t).start()
            slot(21 + t)
            return 0

        lax.fori_loop(0, 3, zeroth_step, 0)
        H[first, MODEL_WIDTH:] = DG[zeroth, :]
        for t in range(3):
            rb_copy(t, 0).wait_recv()
            rb_copy(t, 1).wait_recv()
        for t in (1, 2):
            ro_copy(t).wait()
        for m in range(3):
            wys[m].wait_send()
            wzs[m].wait_send()
        hx.wait_send()
        hc.wait_send()
        hd.wait_send()
        rx.wait_send()

    rx = remote(CR, r_x, rx_s.at[0], rx_r.at[0], xdev)
    ox = remote(CO, o_x, rx_s.at[1], rx_r.at[1], xdev)
    tail_b = remote(
        DG.at[first], r_core.at[:, pl.ds(MODEL_WIDTH, PAD)], rd_s.at[7], rd_r.at[7], cdev
    )
    vm = pltpu.VMEM
    pl.run_scoped(
        experts,
        vm((4 * ROWS, MODEL_WIDTH), bf16),
        vm((2, 3, 4 * ROWS, FF), bf16),
        vm((2, 384, FF), bf16),
        vm((2, ROWS, 512), bf16),
        vm((2, ROWS, 512), bf16),
    )
    ox.start()
    tail_b.wait()

    def attention(
        Y1, DY, GB, XB, H1, OB, QB, KB, VV, DA, DOB, DQKV, BIAS, LSE, COS, SIN, RT, RO, G1, G2,
        SC, SR, DL, GS, DK, DV, HG, STG,
        AA, AB, PP, VY, QQ, VX, AS, AZ, AT, AF, AN,
    ):
        pairs = [
            (y1, Y1), (g4.at[pl.ds(0, ROWS)], GB), (xin, XB), (h1, H1), (ob, OB), (q, QB), (k, KB),
            (v, VV), (lse, LSE), (cos, COS), (sin, SIN), (rt, RT), (routes, RO), (gain1, G1),
            (gain2, G2), (segc, SC), (segr, SR), (r_core, H.at[second]),
        ]
        for half in range(2):
            rows = pl.ds(half * HALF, HALF)
            for n, w in ((0, wq), (1, wo)):
                for part in range(2):
                    columns = pl.ds(part * HALF, HALF)
                    pairs.append((w.at[half, :, columns], W.at[n, part, rows]))
            pairs.append((wk.at[half], W.at[0, 2, rows, pl.ds(0, 256)]))
            pairs.append((wv.at[half], W.at[0, 2, rows, pl.ds(256, 256)]))
        loads = [local_copy(p[0], p[1], att.at[n]) for n, p in enumerate(pairs)]
        for copy in loads:
            copy.start()
        slots(24, 26)
        for copy in loads:
            copy.wait()
        mask_bias(SC, SR, BIAS)
        slots(26, 28)
        rx.wait_recv()
        last = local_copy(r_x, H.at[third], att.at[len(pairs)])
        last.start()
        last.wait()

        def rows_of(n):
            q_, i = n // 2, n % 2
            return q_, i * 384

        def ac_copy(n):
            b, begin = rows_of(n)
            src = d.at[b, :, pl.ds(begin + (1 - c) * 192, 192)]
            return remote(src, ca.at[n], ac_s.at[n], ac_r.at[n], cdev)

        def aload_a(n):
            b, begin = rows_of(n)
            return local_copy(d.at[b, :, pl.ds(begin + c * 192, 192)], AA.at[n % 2], ald.at[0, n % 2])

        def aload_b(n):
            return local_copy(ca.at[n], AB.at[n % 2], ald.at[1, n % 2])

        def ay_copy(n):
            return remote(PP.at[n % 4, 1 - y], yb.at[n], ay_s.at[n], ay_r.at[n], ydev)

        def aload_y(n):
            return local_copy(yb.at[n], VY.at[n % 2], aldy.at[n % 2])

        def ax_copy(n):
            src = QQ.at[n % 4, pl.ds((1 - x) * QUARTER, QUARTER)]
            return remote(src, xb.at[n], ax_s.at[n], ax_r.at[n], xdev)

        def aload_x(n):
            return local_copy(xb.at[n], VX.at[n % 2], aldx.at[n % 2])

        def az1_copy(n):
            return remote(AS.at[n % 8], zc.at[n], az1_s.at[n], az1_r.at[n], zdev)

        def aload_z(n):
            return local_copy(zc.at[n], AZ.at[n % 2], aldz.at[n % 2])

        def az2_copy(n):
            return remote(AT.at[n % 4], zd.at[n], az2_s.at[n], az2_r.at[n], mdev)

        def aload_f(n):
            return local_copy(zd.at[n], AF.at[n % 2], aldf.at[n % 2])

        def aspot(n, xx, cc):
            b, begin = rows_of(n)
            columns = pl.ds(pl.multiple_of(b * WIDTH, WIDTH), WIDTH)
            return aout.at[pl.ds(begin + cc * 192 + xx * QUARTER, QUARTER), columns]

        def az3_copy(n):
            return remote(AN.at[n % 4], aspot(n, x, c), az3_s.at[n], az3_r.at[n], zdev)

        def astore(n):
            return local_copy(AN.at[n % 4], aspot(n, x, c), afo.at[n % 4])

        def axg_copy(n):
            return remote(aspot(n, x, c), aspot(n, x, c), axg_s.at[n], axg_r.at[n], xdev)

        def ac1_copy(n):
            return remote(aspot(n, x, c), aspot(n, x, c), ac1_s.at[n], ac1_r.at[n], cdev)

        def ac2_copy(n):
            return remote(aspot(n, 1 - x, c), aspot(n, 1 - x, c), ac2_s.at[n], ac2_r.at[n], cdev)

        def awhen(n, cond=None):
            ok = (n >= 0) & (n < PARTS)
            return pl.when(ok if cond is None else ok & cond)

        def aslot(s):
            @awhen(s - 13)
            def _():
                axg_copy(s - 13).wait_recv()
                ac2_copy(s - 13).start()

            @awhen(s - 12, mid)
            def _():
                astore(s - 12).wait()
                az3_copy(s - 12).wait_send()

            @awhen(s - 12, end)
            def _():
                az3_copy(s - 12).wait_recv()
                az1_copy(s - 12).wait_send()

            @awhen(s - 12)
            def _():
                axg_copy(s - 12).start()
                ac1_copy(s - 12).start()

            @awhen(s - 10, mid)
            def _():
                n = s - 10
                aload_f(n).wait()
                az2_copy(n).wait_send()
                AN[n % 4] = (AT[n % 4].astype(f32) + AF[n % 2].astype(f32)).astype(bf16)
                az3_copy(n).start()
                astore(n).start()

            @awhen(s - 9, mid)
            def _():
                az2_copy(s - 9).wait_recv()
                aload_f(s - 9).start()

            @awhen(s - 8, mid)
            def _():
                n = s - 8
                aload_z(n).wait()
                AT[n % 4] = (AS[n % 8].astype(f32) + AZ[n % 2].astype(f32)).astype(bf16)
                az2_copy(n).start()

            @awhen(s - 7, mid)
            def _():
                az1_copy(s - 7).wait_recv()
                aload_z(s - 7).start()

            @awhen(s - 6)
            def _():
                n = s - 6
                aload_x(n).wait()
                ax_copy(n).wait_send()
                mine = pl.ds(pl.multiple_of(x * QUARTER, 16), QUARTER)
                AS[n % 8] = (QQ[n % 4, mine, :].astype(f32) + VX[n % 2].astype(f32)).astype(bf16)

            @awhen(s - 6, end)
            def _():
                az1_copy(s - 6).start()

            @awhen(s - 5)
            def _():
                ax_copy(s - 5).wait_recv()
                aload_x(s - 5).start()

            @awhen(s - 4)
            def _():
                n = s - 4
                aload_y(n).wait()
                ay_copy(n).wait_send()
                QQ[n % 4] = (PP[n % 4, y].astype(f32) + VY[n % 2].astype(f32)).astype(bf16)
                ax_copy(n).start()

            @awhen(s - 3)
            def _():
                ay_copy(s - 3).wait_recv()
                aload_y(s - 3).start()

            @awhen(s - 1)
            def _():
                n = s - 1
                aload_a(n).wait()
                aload_b(n).wait()
                PP[n % 4] = (AA[n % 2].astype(f32) + AB[n % 2].astype(f32)).astype(bf16)
                ay_copy(n).start()

            @awhen(s)
            def _():
                ac_copy(s).wait_recv()
                aload_a(s).start()
                aload_b(s).start()

        def emit(b, left, right):
            copies = []
            for half in range(2):
                STG[half] = tn_dot(left[:, pl.ds(half * HALF, HALF)], right).astype(bf16)
                copies.append(local_copy(STG.at[half], d.at[b, half], stg_sem.at[half]))
                copies[half].start()
            for copy in copies:
                copy.wait()
            ac_copy(2 * b).start()
            ac_copy(2 * b + 1).start()

        def returned(rows):
            begin = rows.start
            one = H[pl.ds(pl.multiple_of(begin + ROWS, 128), 128), :].astype(f32)
            two = H[pl.ds(pl.multiple_of(begin + 2 * ROWS, 128), 128), :].astype(f32)
            three = H[pl.ds(pl.multiple_of(begin + 3 * ROWS, 128), 128), :].astype(f32)
            return one + two + three

        middle_backward(
            returned, lambda rows: H[rows, :MODEL_WIDTH], RT, RO, Y1, GB, G2, DL, DY, DA, GS
        )
        for half in range(2):
            columns = pl.ds(half * HALF, HALF)
            SM[half, 1:2, :] = GS[:, columns].astype(bf16)
            router = tn_dot(DL[...], H[zeroth, columns])
            SM[half, 2:10, :] = router[0:8].astype(bf16)
            SM[half, 10:16, :] = jnp.zeros((6, HALF), bf16)

        def out_block(b, _):
            emit(b, OB, DA[:, pl.ds(pl.multiple_of(b * WIDTH, WIDTH), WIDTH)])
            slot(28 + b)
            return 0

        lax.fori_loop(0, 3, out_block, 0)

        def dob_tile(t, _):
            ns = pl.ds(pl.multiple_of(t * 512, 512), 512)
            tile = nt_dot(DA[:, :HALF], W[1, 0, ns, :]) + nt_dot(DA[:, HALF:], W[1, 1, ns, :])
            DOB[:, ns] = tile.astype(bf16)
            slot(31 + t)
            return 0

        lax.fori_loop(0, 3, dob_tile, 0)
        state = [34, 0]

        def tick():
            first_slot, first_part = state

            def step(n, _):
                slot(first_slot + n)
                return 0

            lax.fori_loop(0, 2, step, 0)
            if first_part < 6:
                lax.fori_loop(0, 2, lambda n, _: (aslot(first_part + n), 0)[1], 0)
            state[0] += 2
            state[1] = min(state[1] + 2, 6)

        heads_backward(QB, KB, VV, DOB, BIAS, LSE, COS, SIN, DQKV, DK, DV, tick)
        done, parts_done = state

        def qkv_block(b, _):
            emit(3 + b, H1, DQKV[:, pl.ds(pl.multiple_of(b * WIDTH, WIDTH), WIDTH)])
            slot(done + b)
            return 0

        lax.fori_loop(0, 4, qkv_block, 0)
        done += 4

        def dh1_tile(t, _):
            ns = pl.ds(pl.multiple_of(t * 512, 512), 512)
            tile = nt_dot(DQKV[:, :HALF], W[0, 0, ns, :])
            tile = tile + nt_dot(DQKV[:, HALF:MODEL_WIDTH], W[0, 1, ns, :])
            Y1[:, ns] = tile + nt_dot(DQKV[:, MODEL_WIDTH:], W[0, 2, ns, :512])
            slot(done + t)
            aslot(parts_done + t)
            return 0

        lax.fori_loop(0, 3, dh1_tile, 0)
        done, parts_done = done + 3, parts_done + 3
        first_backward(Y1, XB, DY, G1, HG, GS)
        for half in range(2):
            SM[half, 0:1, :] = GS[:, pl.ds(half * HALF, HALF)].astype(bf16)
        result = local_copy(HG, hgrad, att.at[len(pairs) + 1])
        result.start()

        for i, device in enumerate((cdev, xdev, ydev, zdev, mdev)):
            hop = remote(SM, sa.at[i], s_s.at[i], s_r.at[i], device)
            hop.start()
            slot(done)
            aslot(parts_done)
            done, parts_done = done + 1, parts_done + 1
            hop.wait()
            load = local_copy(sa.at[i], SB, sl.at[0])
            load.start()
            load.wait()
            SM[...] = (SM[...].astype(f32) + SB[...].astype(f32)).astype(bf16)
        small = local_copy(SM, smo, sl.at[1])
        small.start()

        last_slot = max(EXPERT_SLOTS - done, PART_SLOTS - parts_done)

        def drain(n, _):
            slot(done + n)
            aslot(parts_done + n)
            return 0

        lax.fori_loop(0, last_slot, drain, 0)
        small.wait()
        result.wait()

        def finish_part(n, _):
            ac_copy(n).wait_send()
            axg_copy(n).wait_send()
            ac1_copy(n).wait()
            ac2_copy(n).wait()
            return 0

        lax.fori_loop(0, PARTS, finish_part, 0)

    part = lambda *shape: vm(shape, bf16)
    pl.run_scoped(
        attention,
        vm((ROWS, MODEL_WIDTH), f32), vm((ROWS, MODEL_WIDTH), f32),
        part(ROWS, MODEL_WIDTH), part(ROWS, MODEL_WIDTH), part(ROWS, MODEL_WIDTH),
        part(ROWS, MODEL_WIDTH), part(ROWS, MODEL_WIDTH), part(ROWS, 256), part(ROWS, 256),
        part(ROWS, MODEL_WIDTH), part(ROWS, MODEL_WIDTH), part(ROWS, 2048),
        vm((ROWS, ROWS), f32), vm((ROWS, PAD), f32), vm((ROWS, PAD), f32), vm((ROWS, PAD), f32),
        part(PAD, MODEL_WIDTH), vm((ROWS, PAD), jnp.int32), vm((1, MODEL_WIDTH), f32),
        vm((1, MODEL_WIDTH), f32), vm((ROWS, PAD), jnp.int32), vm((8, ROWS), jnp.int32),
        part(ROWS, PAD), vm((1, MODEL_WIDTH), f32), vm((2, ROWS, PAD), f32),
        vm((2, ROWS, PAD), f32), part(ROWS, MODEL_WIDTH), part(2, HALF, WIDTH),
        part(2, 2, 192, WIDTH), part(2, 2, 192, WIDTH), part(4, 2, 192, WIDTH),
        part(2, 192, WIDTH), part(4, 192, WIDTH), part(2, QUARTER, WIDTH), part(8, QUARTER, WIDTH),
        part(2, QUARTER, WIDTH), part(4, QUARTER, WIDTH), part(2, QUARTER, WIDTH),
        part(4, QUARTER, WIDTH),
    )
    ox.wait()

    def finish(n, _):
        @pl.when(crosses(n))
        def _():
            x_copy(n).wait_send()

        @pl.when(crosses(n) & (n % 2 == 1))
        def _():
            z4_copy(n).wait_send()

        c1_copy(n).wait()
        c2_copy(n).wait()
        y_copy(n).wait_send()
        return 0

    lax.fori_loop(0, CHUNKS, finish, 0)


def layer_call(*arrays):
    anyspace = pl.BlockSpec(memory_space=pl.ANY)
    dma = pltpu.SemaphoreType.DMA
    vmem = lambda *s: pltpu.VMEM(s, bf16)
    n = PARTS
    shapes = [(ROWS, MODEL_WIDTH)] * 3
    shapes += [(3, 8, HALF, FF), (HALF, BLOCKS * WIDTH), (2, 16, HALF), (ROWS, MODEL_WIDTH)]
    shapes += [(ROWS, WIDE)] * 2 + [(2, 3, MODEL_WIDTH, FF)] + [(CHUNKS, CHUNK, FF)] * 3
    shapes += [(BLOCKS, 2, HALF, WIDTH), (n, 2, 192, WIDTH), (n, 192, WIDTH)]
    shapes += [(n, QUARTER, WIDTH)] * 3 + [(5, 2, 16, HALF)]
    many, few = dma((CHUNKS,)), dma((n,))
    scratch = [
        vmem(4 * ROWS, WIDE), vmem(2, 3, MODEL_WIDTH, FF), vmem(4 * ROWS, PAD), vmem(ROWS, WIDE),
        vmem(ROWS, MODEL_WIDTH), vmem(2, CHUNK, FF), vmem(2, CHUNK, FF), vmem(4, CHUNK, FF),
        vmem(2, CHUNK, FF), vmem(4, CHUNK, FF), vmem(2, CHUNK, FF), vmem(4, CHUNK, FF),
        vmem(2, 16, HALF), vmem(2, 16, HALF),
        dma((9,)), dma((3,)), dma((3,)), dma((3,)), dma((3,)), dma((3,)), dma((3,)),
        dma((2,)), many, many, dma((2,)), dma((2,)),
        many, many, dma((2,)), many, many, dma((2,)),
        many, many, dma((4,)), many, many, many, many, many, many, many, many,
        dma((2, 3)), dma((2, 3)), dma((2,)), dma((2,)), dma((8,)), dma((8,)), dma((3,)),
        few, few, dma((2, 2)), few, few, dma((2,)), few, few, dma((2,)), few, few, dma((2,)),
        few, few, dma((2,)), few, few, dma((4,)), few, few, few, few, few, few,
        dma((5,)), dma((5,)), dma((2,)), dma((32,)),
    ]
    return pl.pallas_call(
        layer_kernel,
        out_shape=[jax.ShapeDtypeStruct(s, bf16) for s in shapes],
        in_specs=[anyspace] * len(arrays),
        out_specs=[anyspace] * len(shapes),
        scratch_shapes=scratch,
        compiler_params=pltpu.CompilerParams(
            collective_id=2, has_side_effects=True, vmem_limit_bytes=66 * 1000 * 1000
        ),
        name="layer",
    )(*arrays)[:7]


def attention_forward(hidden, segments, gain_one, w_q, w_k, w_v, w_o, gain_two):
    sequence_length = hidden.shape[0]
    group = QUERY_HEADS // KEY_VALUE_HEADS
    head_scale = HEAD_SIZE ** (-0.5)
    cosine, sine = tables(sequence_length, HEAD_SIZE)
    normed_f, scale_one = normalize(hidden, gain_one)
    h1 = normed_f.astype(bf16)
    qr = jnp.dot(h1, w_q, preferred_element_type=f32)
    kr = jnp.dot(h1, w_k, preferred_element_type=f32)
    values = jnp.dot(h1, w_v, preferred_element_type=f32).astype(bf16)
    values = values.reshape(sequence_length, KEY_VALUE_HEADS, HEAD_SIZE)
    qr = qr.reshape(sequence_length, QUERY_HEADS, HEAD_SIZE)
    kr = kr.reshape(sequence_length, KEY_VALUE_HEADS, HEAD_SIZE)
    queries = apply_rotary(qr, cosine, sine).astype(bf16)
    queries = queries.reshape(sequence_length, KEY_VALUE_HEADS, group, HEAD_SIZE)
    keys = apply_rotary(kr, cosine, sine).astype(bf16)
    position = jnp.arange(sequence_length)
    allowed = (position[None, :] <= position[:, None]) & (segments[:, None] == segments[None, :])
    scores = jnp.einsum("qkgd,skd->kgqs", queries, keys, preferred_element_type=f32) * head_scale
    scores = jnp.where(allowed, scores, -1e30)
    top_score = jnp.max(scores, axis=-1, keepdims=True)
    exp_scores = jnp.exp(scores - top_score)
    sum_exp = jnp.sum(exp_scores, axis=-1, keepdims=True)
    log_total = top_score + jnp.log(sum_exp)
    probs = (exp_scores / sum_exp).astype(bf16)
    mixed = jnp.einsum("kgqs,skd->qkgd", probs, values, preferred_element_type=f32)
    mixed = mixed.reshape(sequence_length, QUERY_HEADS * HEAD_SIZE).astype(bf16)
    middle = hidden + jnp.dot(mixed, w_o, preferred_element_type=f32)
    normed_two_f, scale_two = normalize(middle, gain_two)
    h2 = normed_two_f.astype(bf16)
    kept = (scale_one, h1, queries, keys, values, allowed, log_total, mixed, middle, scale_two)
    return h2, kept


def router_forward(h2, w_router, routes):
    logits = jnp.dot(h2, w_router, preferred_element_type=f32)
    probs = softmax_rows(logits)
    experts = w_router.shape[1]
    chosen = jnp.any(
        routes[:, :, None] == jnp.arange(experts, dtype=jnp.int32)[None, None, :], axis=1
    )
    picked = jnp.where(chosen, probs, 0.0)
    total = jnp.sum(picked, axis=-1, keepdims=True)
    return probs, chosen, total, picked / total


def router_backward(h2, w_router, probs, chosen, total, gates, gate_grads):
    gate_grads = jnp.where(chosen, gate_grads, 0.0)
    weighted = jnp.sum(gate_grads * gates, axis=-1, keepdims=True)
    prob_grad = jnp.where(chosen, (gate_grads - weighted) / total, 0.0)
    logit_grad = probs * (prob_grad - jnp.sum(prob_grad * probs, axis=-1, keepdims=True))
    logit_grad = logit_grad.astype(bf16)
    return contract(h2, logit_grad, 0, 0), contract(logit_grad, w_router, 1, 1)


def attention_backward(hidden, kept, gain_one, w_q, w_k, w_v, w_o, gain_two, upstream, dh2):
    scale_one, h1, queries, keys, values, allowed, log_total, mixed, middle, scale_two = kept
    sequence_length = hidden.shape[0]
    group = QUERY_HEADS // KEY_VALUE_HEADS
    head_scale = HEAD_SIZE ** (-0.5)
    cosine, sine = tables(sequence_length, HEAD_SIZE)
    middle_norm_grad, gain_two_grad = norm_back(middle, scale_two, gain_two, dh2)
    middle_grad = upstream + middle_norm_grad
    branch_grad = middle_grad.astype(bf16)
    out_proj_sum = contract(mixed, branch_grad, 0, 0)
    mixed_grad = contract(branch_grad, w_o, 1, 1).astype(bf16)
    mixed_grad = mixed_grad.reshape(sequence_length, KEY_VALUE_HEADS, group, HEAD_SIZE)
    probs = jnp.exp(
        jnp.einsum("qkgd,skd->kgqs", queries, keys, preferred_element_type=f32) * head_scale
        - log_total
    )
    probs = jnp.where(allowed, probs, 0.0)
    prob_back = jnp.einsum("qkgd,skd->kgqs", mixed_grad, values, preferred_element_type=f32)
    score_grad = probs * (prob_back - jnp.sum(prob_back * probs, axis=-1, keepdims=True))
    score_grad = score_grad.astype(bf16)
    dq = jnp.einsum("kgqs,skd->qkgd", score_grad, keys, preferred_element_type=f32) * head_scale
    dq = dq.reshape(sequence_length, QUERY_HEADS, HEAD_SIZE)
    dq = apply_rotary(dq, cosine, -sine).astype(bf16)
    dq = dq.reshape(sequence_length, QUERY_HEADS * HEAD_SIZE)
    dk = jnp.einsum("kgqs,qkgd->skd", score_grad, queries, preferred_element_type=f32) * head_scale
    dk = apply_rotary(dk, cosine, -sine).astype(bf16)
    dk = dk.reshape(sequence_length, KEY_VALUE_HEADS * HEAD_SIZE)
    dv = jnp.einsum("kgqs,qkgd->skd", probs.astype(bf16), mixed_grad, preferred_element_type=f32)
    dv = dv.astype(bf16).reshape(sequence_length, KEY_VALUE_HEADS * HEAD_SIZE)
    query_sum = contract(h1, dq, 0, 0)
    key_sum = contract(h1, dk, 0, 0)
    value_sum = contract(h1, dv, 0, 0)
    dh1 = contract(dq, w_q, 1, 1) + contract(dk, w_k, 1, 1) + contract(dv, w_v, 1, 1)
    hidden_norm_grad, gain_one_grad = norm_back(hidden, scale_one, gain_one, dh1)
    hidden_grad = (middle_grad + hidden_norm_grad).astype(bf16)
    return hidden_grad, (
        gain_one_grad,
        query_sum,
        key_sum,
        value_sum,
        out_proj_sum,
        gain_two_grad,
    )


def reduce_over_all(value, dimension):
    value = lax.psum_scatter(
        value.astype(bf16), "shard", scatter_dimension=dimension, tiled=True
    ).astype(f32)
    return lax.psum(value.astype(bf16), "rep").astype(f32)


def local(
    hidden_in,
    segment_ids,
    routes,
    out_grad,
    norm1_gain,
    w_query,
    key_weight,
    value_weight,
    w_out,
    norm2_gain,
    w_router,
    w_gate,
    w_up,
    w_down,
):
    small = jnp.concatenate(
        [norm1_gain[None], norm2_gain[None], w_router.T, jnp.zeros((6, HALF), bf16)], axis=0
    )
    w_q, w_k, w_v, w_o, small, g4, w0 = gather_call(
        w_query, key_weight, value_weight, w_out, small, out_grad, w_gate, w_up, w_down
    )
    whole = lambda w: w.reshape(MODEL_WIDTH, w.shape[-1])
    weights = (w_q, w_k, w_v, w_o)
    w_q, w_k, w_v, w_o = whole(w_q), whole(w_k), whole(w_v), whole(w_o)
    small = small.transpose(1, 0, 2).reshape(16, MODEL_WIDTH)
    gain_one, gain_two = small[0].astype(f32), small[1].astype(f32)
    router = small[2:10].T
    hidden = hidden_in.astype(f32)
    h2, kept = attention_forward(
        hidden, segment_ids[0], gain_one, w_q, w_k, w_v, w_o, gain_two
    )
    probs, chosen, total, gates = router_forward(h2, router, routes)
    high = gates.astype(bf16)
    low = (gates - high.astype(f32)).astype(bf16)
    hg = jnp.concatenate([h2, high, low, jnp.zeros((ROWS, PAD - 16), bf16)], axis=1)
    scale_one, h1, queries, keys, values, allowed, log_total, mixed, middle, scale_two = kept
    cosine, sine = tables(ROWS, HEAD_SIZE)
    lanes = lambda v: jnp.pad(v, ((0, 0), (0, PAD - v.shape[1])))
    segments = segment_ids[0]
    o_own, o_core, o_x, grads, d, sm, hidden_grad = layer_call(
        hg,
        g4.reshape(4 * ROWS, MODEL_WIDTH),
        w0,
        w_gate,
        w_up,
        w_down,
        middle,
        hidden_in,
        h1,
        queries.reshape(ROWS, MODEL_WIDTH),
        keys.reshape(ROWS, 256),
        values.reshape(ROWS, 256),
        mixed,
        lanes(log_total.reshape(QUERY_HEADS, ROWS).T),
        cosine[:, 0, :],
        turn_table(sine),
        jnp.pad(small[2:10], ((0, PAD - 8), (0, 0))),
        lanes(routes),
        gain_one[None],
        gain_two[None],
        jnp.broadcast_to(segments[:, None], (ROWS, PAD)),
        jnp.broadcast_to(segments[None, :], (8, ROWS)),
        *weights,
    )
    add = lambda a, b, c: a.astype(f32) + b.astype(f32) + c.astype(f32)
    hidden_out = (middle + add(o_own, o_core, o_x)).astype(bf16)
    sm = lax.dynamic_index_in_dim(sm, lax.axis_index("shard"), 0, keepdims=False).astype(f32)
    d = d.astype(f32)
    attn = (sm[0], d[:, 1536:3072], d[:, 3072:3328], d[:, 3328:], d[:, :1536], sm[1], sm[2:10].T)
    grads = [grads[m].astype(f32) for m in range(3)]
    return (hidden_out, hidden_grad, *attn, *grads)


def local_any(
    hidden_in,
    segment_ids,
    routes,
    out_grad,
    norm1_gain,
    w_query,
    key_weight,
    value_weight,
    w_out,
    norm2_gain,
    w_router,
    w_gate,
    w_up,
    w_down,
):
    wide = lambda w, axis: lax.all_gather(w, "shard", axis=axis, tiled=True)
    gain_one, gain_two = wide(norm1_gain, 0).astype(f32), wide(norm2_gain, 0).astype(f32)
    w_q, w_k, w_v, w_o = (wide(w, 0) for w in (w_query, key_weight, value_weight, w_out))
    router = wide(w_router, 0)
    hidden = hidden_in.astype(f32)
    h2, kept = attention_forward(
        hidden, segment_ids[0], gain_one, w_q, w_k, w_v, w_o, gain_two
    )
    probs, chosen, total, gates = router_forward(h2, router, routes)
    full = [wide(w, 1) for w in (w_gate, w_up, w_down)]

    def expert(carry, inputs):
        mixed, dh2 = carry
        gate_weight, up_weight, down_weight, gate = inputs
        gate = gate[:, None]
        ug = jnp.dot(h2, gate_weight, preferred_element_type=f32)
        uu = jnp.dot(h2, up_weight, preferred_element_type=f32)
        dh = jnp.dot(out_grad, down_weight, preferred_element_type=f32)
        sigma = jax.nn.sigmoid(ug)
        silu = ug * sigma
        hid = silu * uu
        gate_grad = jnp.sum(hid * dh, axis=1)
        hidden_rows = (hid * gate).astype(bf16)
        dug = (dh * gate * uu * sigma * (1.0 + ug * (1.0 - sigma))).astype(bf16)
        duu = (dh * gate * silu).astype(bf16)
        mixed = mixed + contract(hidden_rows, down_weight, 1, 1)
        dh2 = dh2 + contract(dug, gate_weight, 1, 1) + contract(duu, up_weight, 1, 1)
        sums = (contract(h2, dug, 0, 0), contract(h2, duu, 0, 0))
        sums = sums + (contract(out_grad, hidden_rows, 0, 0),)
        return (mixed, dh2), (gate_grad, *(s.astype(bf16) for s in sums))

    zeros = jnp.zeros(hidden.shape, f32)
    (mixed, dh2), (gate_grads, *sums) = lax.scan(expert, (zeros, zeros), (*full, gates.T))
    hidden_out = (kept[8] + mixed).astype(bf16)
    router_sum, routed = router_backward(h2, router, probs, chosen, total, gates, gate_grads.T)
    hidden_grad, attn = attention_backward(
        hidden, kept, gain_one, w_q, w_k, w_v, w_o, gain_two, out_grad.astype(f32), routed + dh2
    )
    attn = [reduce_over_all(value, 0) for value in attn + (router_sum,)]
    grads = [reduce_over_all(value, 1) for value in sums]
    return (hidden_out, hidden_grad, *attn, *grads)


def solution(mesh):
    rows, vector, matrix = P(("rep", "shard"), None), P("shard"), P("shard", None)
    stack = P(None, "shard", None)
    in_specs = (
        rows, rows, rows, rows, vector, matrix, matrix, matrix, matrix, vector, matrix,
        stack, stack, stack,
    )
    out_specs = (
        rows, rows, vector, matrix, matrix, matrix, matrix, vector, matrix, stack, stack, stack,
    )
    fits = dict(mesh.shape) == {"rep": 16, "shard": 2}
    body = local if fits else local_any
    return jax.shard_map(body, mesh=mesh, in_specs=in_specs, out_specs=out_specs, check_vma=False)
```

```python
import functools

import jax
import jax.numpy as jnp
from jax import lax
from jax.experimental import pallas as pl
from jax.experimental.pallas import tpu as pltpu
from jax.sharding import PartitionSpec as P

MODEL_WIDTH = 1536
QUERY_HEADS = 12
KEY_VALUE_HEADS = 2
HEAD_SIZE = 128
TOPK = 4
FF = 768
HALF = 768
ROWS = 512
PAD = 128
WIDE = MODEL_WIDTH + PAD
CHUNK = 96
PER = HALF // CHUNK
CHUNKS = 6 * PER

epsilon = 1e-06
rope_base = 1000000.0
MESH = pl.DeviceIdType.MESH
bf16 = jnp.bfloat16
f32 = jnp.float32


def tables(sequence_length, row_width):
    frequency = rope_base ** (-2.0 * jnp.arange(row_width // 2, dtype=jnp.float32) / row_width)
    angles = jnp.arange(sequence_length, dtype=jnp.float32)[:, None] * frequency[None, :]
    angles = jnp.concatenate([angles, angles], axis=-1)
    return (jnp.cos(angles)[:, None, :], jnp.sin(angles)[:, None, :])


def apply_rotary(values, rotary_cosine, rotary_sine):
    half_width = values.shape[-1] // 2
    turned = jnp.concatenate([-values[..., half_width:], values[..., :half_width]], axis=-1)
    return values * rotary_cosine + turned * rotary_sine


def contract(left_side, right_side, left_dim, right_dim):
    return lax.dot_general(
        left_side,
        right_side,
        (((left_dim,), (right_dim,)), ((), ())),
        preferred_element_type=jnp.float32,
    )


def normalize(values, gain_vector):
    scale_rows = lax.rsqrt(jnp.mean(values * values, axis=-1, keepdims=True) + epsilon)
    return (values * scale_rows * gain_vector, scale_rows)


def norm_back(values, scale_rows, gain_vector, upstream):
    scaled = upstream * gain_vector
    gain_grad = jnp.sum(upstream * values * scale_rows, axis=0)
    inner_sum = jnp.sum(scaled * values, axis=-1, keepdims=True)
    return (scaled * scale_rows - values * scale_rows**3 * inner_sum / values.shape[-1], gain_grad)


def softmax_rows(values):
    top_value = jnp.max(values, axis=-1, keepdims=True)
    exp_values = jnp.exp(values - top_value)
    return exp_values / jnp.sum(exp_values, axis=-1, keepdims=True)


def place():
    rep = lax.axis_index("rep")
    y = lax.axis_index("shard")
    return rep // 4, (rep // 2) % 2, rep % 2, y


def at(z, x, c, y):
    return ((z * 2 + x) * 2 + c, y)


def remote(src, dst, send, recv, device):
    return pltpu.make_async_remote_copy(
        src_ref=src,
        dst_ref=dst,
        send_sem=send,
        recv_sem=recv,
        device_id=device,
        device_id_type=MESH,
    )


def greet(partners):
    barrier = pltpu.get_barrier_semaphore()
    for device in partners:
        pl.semaphore_signal(barrier, inc=1, device_id=device, device_id_type=MESH)
    pl.semaphore_wait(barrier, len(partners))


def nt_dot(a, b):
    return lax.dot_general(a, b, (((1,), (1,)), ((), ())), preferred_element_type=f32)


def tn_dot(a, b):
    return lax.dot_general(a, b, (((0,), (0,)), ((), ())), preferred_element_type=f32)


def turn_table(sine):
    sign = jnp.where(jnp.arange(HEAD_SIZE) < HEAD_SIZE // 2, -1.0, 1.0)
    return sine[:, 0, :] * sign[None, :]


def router_rows(h2, router_rows_t, routes):
    logits = nt_dot(h2, router_rows_t)
    lane = lax.broadcasted_iota(jnp.int32, logits.shape, 1)
    real = lane < 8
    logits = jnp.where(real, logits, -1e30)
    top = jnp.max(logits, axis=1, keepdims=True)
    exp_values = jnp.where(real, jnp.exp(logits - top), 0.0)
    probs = exp_values / jnp.sum(exp_values, axis=1, keepdims=True)
    chosen = lane == routes[:, 0:1]
    for k in range(1, 4):
        chosen = chosen | (lane == routes[:, k : k + 1])
    picked = jnp.where(chosen, probs, 0.0)
    total = jnp.sum(picked, axis=1, keepdims=True)
    return probs, chosen, total, picked / total


def middle_backward(returned, h2, rt, routes, y1, g, gain_two, DL, DY, DA, GS):
    GS[...] = jnp.zeros_like(GS)

    def step(b, _):
        rows = pl.ds(pl.multiple_of(b * 128, 128), 128)
        probs, chosen, total, gates = router_rows(h2(rows), rt[...], routes[rows, :])
        back = returned(rows)
        packed = back[:, MODEL_WIDTH:]
        gate_grads = jnp.where(chosen, packed + pltpu.roll(packed, PAD - 8, 1), 0.0)
        weighted = jnp.sum(gate_grads * gates, axis=1, keepdims=True)
        prob_grad = jnp.where(chosen, (gate_grads - weighted) / total, 0.0)
        inner = jnp.sum(prob_grad * probs, axis=1, keepdims=True)
        logit_grad = (probs * (prob_grad - inner)).astype(bf16)
        DL[rows, :] = logit_grad
        dh2 = back[:, :MODEL_WIDTH] + jnp.dot(logit_grad, rt[...], preferred_element_type=f32)
        v = y1[rows, :]
        r = lax.rsqrt(jnp.mean(v * v, axis=1, keepdims=True) + epsilon)
        GS[...] = GS[...] + jnp.sum(dh2 * v * r, axis=0, keepdims=True)
        scaled = dh2 * gain_two[...]
        along = jnp.sum(scaled * v, axis=1, keepdims=True)
        dy = g[rows, :].astype(f32) + (scaled * r - v * (r * r * r * along / MODEL_WIDTH))
        DY[rows, :] = dy
        DA[rows, :] = dy.astype(bf16)
        return 0

    lax.fori_loop(0, ROWS // 128, step, 0)


def heads_backward(Q, K, V, DOB, BIAS, LSE, COS, SIN, DQKV, DK, DV, tick):
    scale = HEAD_SIZE ** (-0.5)
    DK[...] = jnp.zeros_like(DK)
    DV[...] = jnp.zeros_like(DV)
    for group in range(2):
        shared = pl.ds(group * HEAD_SIZE, HEAD_SIZE)

        def head(n, _, group=group, shared=shared):
            columns = pl.ds(pl.multiple_of((group * 6 + n) * HEAD_SIZE, HEAD_SIZE), HEAD_SIZE)
            lane = lax.broadcasted_iota(jnp.int32, (ROWS, PAD), 1)
            lse = jnp.sum(
                jnp.where(lane == group * 6 + n, LSE[...], 0.0), axis=1, keepdims=True
            )
            for block in range(2):
                rows, keys = pl.ds(block * 256, 256), pl.ds(0, 256 * (block + 1))
                q, dob = Q[rows, columns], DOB[rows, columns]
                k, v = K[keys, shared], V[keys, shared]
                logits = nt_dot(q, k) * scale + BIAS[rows, keys]
                p = jnp.exp(logits - lse[block * 256 : block * 256 + 256])
                dp = nt_dot(dob, v)
                inner = jnp.sum(dp * p, axis=1, keepdims=True)
                ds = (p * (dp - inner)).astype(bf16)
                dq = jnp.dot(ds, k, preferred_element_type=f32) * scale
                dq = dq * COS[rows, :] - pltpu.roll(dq, 64, 1) * SIN[rows, :]
                DQKV[rows, columns] = dq.astype(bf16)
                DK[group, keys, :] = DK[group, keys, :] + tn_dot(ds, q)
                DV[group, keys, :] = DV[group, keys, :] + tn_dot(p.astype(bf16), dob)
            return 0

        for n in range(0, 6, 3):
            lax.fori_loop(n, n + 3, head, 0)
            tick()
        dk = DK[group] * scale
        dk = dk * COS[...] - pltpu.roll(dk, 64, 1) * SIN[...]
        DQKV[:, pl.ds(1536 + group * HEAD_SIZE, HEAD_SIZE)] = dk.astype(bf16)
        DQKV[:, pl.ds(1792 + group * HEAD_SIZE, HEAD_SIZE)] = DV[group].astype(bf16)


def first_backward(DH1, X, DY, gain_one, HG, GS):
    GS[...] = jnp.zeros_like(GS)

    def step(b, _):
        rows = pl.ds(pl.multiple_of(b * 128, 128), 128)
        v, up = X[rows, :].astype(f32), DH1[rows, :]
        r = lax.rsqrt(jnp.mean(v * v, axis=1, keepdims=True) + epsilon)
        GS[...] = GS[...] + jnp.sum(up * v * r, axis=0, keepdims=True)
        scaled = up * gain_one[...]
        along = jnp.sum(scaled * v, axis=1, keepdims=True)
        back = scaled * r - v * (r * r * r * along / MODEL_WIDTH)
        HG[rows, :] = (DY[rows, :] + back).astype(bf16)
        return 0

    lax.fori_loop(0, ROWS // 128, step, 0)


def mask_bias(seg_column, seg_row, BIAS):
    row = lax.broadcasted_iota(jnp.int32, (ROWS, ROWS), 0)
    column = lax.broadcasted_iota(jnp.int32, (ROWS, ROWS), 1)
    same = seg_column[:, 0:1] == seg_row[0:1, :]
    BIAS[...] = jnp.where((column <= row) & same, 0.0, -1e30)


BLOCKS = 7
PARTS = 2 * BLOCKS
WIDTH = 512
QUARTER = 96
SLACK = 3
AT_ZL, AT_FL, AT_X = 1 + SLACK, 2 + 2 * SLACK, 3 + 3 * SLACK
AT_CX, AT_CZ = AT_X + 16, AT_X + 20
EXPERT_SLOTS = CHUNKS + AT_CZ + 1
PART_SLOTS = PARTS + 25


def layer_kernel(
    xin, g, wq, wk, wv, wo, sm, wg, wu, wd, cos, sin, routes, segc, segr,
    o_own, o_core, o_x, out, aout, smo, hgrad, y1,
    h1, q, k, v, ob, lse, wqo, wko, wvo, woo, smf, gl,
    r_core, r_x, gr, ya, za, zb, d, ca, yb, xb, zc, zd, sa,
    H, W, DG, CR, CO, VA, VB, VS, VZ, VT, VF, FN, SM, SB, RT, G1, G2,
    fl_s, wa_s, wa_r, wx_s, wx_r, wc_s, wc_r, wd_s, wd_r, wz_s, wz_r, hx_s, hx_r, hc_s, hc_r,
    hd_s, hd_r, own_s, st_s,
    loc, stg_sem, y_s, y_r, ld_a, ld_b,
    z1_s, z1_r, ld_z, z2_s, z2_r, ld_f, z3_s, z3_r, fo, x_s, x_r, c1_s, c1_r, c2_s, c2_r,
    z4_s, z4_r, rc_s, rc_r, rx_s, rx_r, rd_s, rd_r, ro,
    ac_s, ac_r, ald, ay_s, ay_r, aldy, ax_s, ax_r, aldx, az1_s, az1_r, aldz, az2_s, az2_r, aldf,
    az3_s, az3_r, afo, axg_s, axg_r, ac1_s, ac1_r, ac2_s, ac2_r, s_s, s_r, sl, att,
):
    z, x, c, y = place()
    mid = (z == 1) | (z == 2)
    end = jnp.logical_not(mid)
    ydev, xdev, cdev = at(z, x, c, 1 - y), at(z, 1 - x, c, y), at(z, x, 1 - c, y)
    zdev = at(z + 1 - 2 * (z % 2), x, c, y)
    mdev = at(3 - z, x, c, y)
    greet((ydev, xdev, cdev, zdev, mdev))
    shards = (wg, wu, wd)
    e0 = 2 * (2 * x + c)
    other = 2 * (2 * (1 - x) + c)
    h = z % 2
    local_copy = pltpu.make_async_copy
    vm = pltpu.VMEM
    part = lambda *shape: vm(shape, bf16)

    kinds = ((wk, wko), (wv, wvo), (wq, wqo), (wo, woo))
    piece = HALF // 4
    mine = pl.ds((2 * x + c) * piece, piece)
    theirs = pl.ds((2 * (1 - x) + c) * piece, piece)
    wa = [remote(p[0].at[mine], p[1].at[mine], wa_s.at[n], wa_r.at[n], ydev) for n, p in enumerate(kinds)]
    wa.append(remote(sm, smf, wa_s.at[4], wa_r.at[4], ydev))
    wx = [remote(p[1].at[mine], p[1].at[mine], wx_s.at[n], wx_r.at[n], xdev) for n, p in enumerate(kinds)]
    wc = [remote(p[1].at[mine], p[1].at[mine], wc_s.at[n], wc_r.at[n], cdev) for n, p in enumerate(kinds)]
    wt = [
        remote(p[1].at[theirs], p[1].at[theirs], wd_s.at[n], wd_r.at[n], cdev)
        for n, p in enumerate(kinds)
    ]
    gx = remote(g, gl.at[1], wx_s.at[4], wx_r.at[4], xdev)
    gc = remote(g, gl.at[0], wc_s.at[4], wc_r.at[4], cdev)
    gt = remote(gl.at[1], gl.at[2], wd_s.at[4], wd_r.at[4], cdev)

    def wy(n):
        j, m = n // 3, n % 3
        return remote(
            shards[m].at[e0 + j, pl.ds(h * 384, 384)],
            W.at[j, m, pl.ds(y * HALF + h * 384, 384)],
            wa_s.at[5 + n],
            wa_r.at[5 + n],
            ydev,
        )

    def wz(n):
        rows = pl.ds((1 - y) * HALF + h * 384, 384)
        ref = W.at[n // 3, n % 3, rows]
        return remote(ref, ref, wz_s.at[n], wz_r.at[n], zdev)

    def own_half(n):
        j, m = n // 3, n % 3
        return local_copy(shards[m].at[e0 + j], W.at[j, m, pl.ds(y * HALF, HALF)], own_s.at[n])

    def pass_on(n):
        wy(n).wait_recv()
        wz(n).start()

    def hx(b):
        src = H.at[pl.ds(b * 256, 256)]
        return remote(src, H.at[pl.ds(2 * ROWS + b * 256, 256)], hx_s.at[b], hx_r.at[b], xdev)

    def hc(b):
        src = H.at[pl.ds(b * 256, 256)]
        return remote(src, H.at[pl.ds(ROWS + b * 256, 256)], hc_s.at[b], hc_r.at[b], cdev)

    def hd(b):
        src = H.at[pl.ds(2 * ROWS + b * 256, 256)]
        return remote(src, H.at[pl.ds(3 * ROWS + b * 256, 256)], hd_s.at[b], hd_r.at[b], cdev)

    wa[4].start()
    for n in range(4):
        wa[n].start()
    gc.start()
    for n in range(6):
        wy(n).start()

    def front(X, H1, WQ, WKV, WO, Q, K, V, OB, BIAS, LSE, COS, SIN, RO, SC, SR, SF, Y1):
        there = pl.ds(y * HALF, HALF)
        away = pl.ds((1 - y) * HALF, HALF)
        left, right = pl.ds(0, 256), pl.ds(256, 256)
        pairs = [
            (xin, X), (sm, SF.at[y]), (wk, WKV.at[there, left]), (wv, WKV.at[there, right]),
            (wq, WQ.at[there]), (wo, WO.at[there]), (cos, COS), (sin, SIN), (routes, RO),
            (segc, SC), (segr, SR),
        ]
        loads = [local_copy(p[0], p[1], fl_s.at[n]) for n, p in enumerate(pairs)]
        for copy in loads:
            copy.start()
        for n in range(6):
            own_half(n).start()
        late = [
            local_copy(wko, WKV.at[away, left], fl_s.at[11]),
            local_copy(wvo, WKV.at[away, right], fl_s.at[12]),
            local_copy(wqo, WQ.at[away], fl_s.at[13]),
            local_copy(woo, WO.at[away], fl_s.at[14]),
            local_copy(smf, SF.at[1 - y], fl_s.at[15]),
        ]
        wa[4].wait_recv()
        late[4].start()
        for n in (0, 1):
            loads[n].wait()
        late[4].wait()
        row = lax.broadcasted_iota(jnp.int32, (16, HALF), 0)
        RT[...] = jnp.zeros_like(RT)
        for half in range(2):
            columns = pl.ds(half * HALF, HALF)
            small = SF[half].astype(f32)
            RT[0:16, columns] = jnp.where(row < 8, small, 0.0).astype(bf16)
            G1[:, columns] = jnp.sum(jnp.where(row == 8, small, 0.0), axis=0, keepdims=True)
            G2[:, columns] = jnp.sum(jnp.where(row == 9, small, 0.0), axis=0, keepdims=True)

        def norm_step(b, _):
            rows = pl.ds(pl.multiple_of(b * 128, 128), 128)
            value = X[rows, :].astype(f32)
            r = lax.rsqrt(jnp.mean(value * value, axis=1, keepdims=True) + epsilon)
            H1[rows, :] = (value * r * G1[...]).astype(bf16)
            return 0

        lax.fori_loop(0, ROWS // 128, norm_step, 0)
        for n in range(2, 11):
            loads[n].wait()
        mask_bias(SC, SR, BIAS)
        for n in range(4):
            wa[n].wait_recv()
            wx[n].start()
            wc[n].start()
        gx.start()
        for n in range(3):
            wx[n].wait_recv()
            wt[n].start()
        for n in range(3):
            wc[n].wait_recv()
            wt[n].wait_recv()
            late[n].start()
        for n in range(3):
            late[n].wait()

        def rotate(u):
            return u * COS[...] + pltpu.roll(u, 64, 1) * SIN[...]

        def query_step(t, _):
            begin = pl.multiple_of(t * 512, 512)
            tile = jnp.dot(H1[...], WQ[:, pl.ds(begin, 512)], preferred_element_type=f32)
            for n in range(4):
                u = tile[:, n * HEAD_SIZE : (n + 1) * HEAD_SIZE]
                Q[:, pl.ds(begin + n * HEAD_SIZE, HEAD_SIZE)] = rotate(u).astype(bf16)
            return 0

        tile = jnp.dot(H1[...], WKV[...], preferred_element_type=f32)
        for n in range(2):
            columns = pl.ds(n * HEAD_SIZE, HEAD_SIZE)
            u = tile[:, n * HEAD_SIZE : (n + 1) * HEAD_SIZE]
            K[:, columns] = rotate(u).astype(bf16)
        V[...] = tile[:, 256:].astype(bf16)
        lax.fori_loop(0, 3, query_step, 0)
        wx[3].wait_recv()
        wt[3].start()
        pass_on(0)
        LSE[...] = jnp.zeros_like(LSE)
        scale = HEAD_SIZE ** (-0.5)
        for b in range(2):
            rows, keys = pl.ds(b * 256, 256), pl.ds(0, 256 * (b + 1))

            def head(n, _, rows=rows, keys=keys):
                columns = pl.ds(pl.multiple_of(n * HEAD_SIZE, HEAD_SIZE), HEAD_SIZE)
                shared = pl.ds(pl.multiple_of(n // 6 * HEAD_SIZE, HEAD_SIZE), HEAD_SIZE)
                logits = nt_dot(Q[rows, columns], K[keys, shared]) * scale + BIAS[rows, keys]
                top = jnp.max(logits, axis=1, keepdims=True)
                p = jnp.exp(logits - top)
                total = jnp.sum(p, axis=1, keepdims=True)
                lane = lax.broadcasted_iota(jnp.int32, (256, PAD), 1)
                LSE[rows, :] = jnp.where(lane == n, top + jnp.log(total), LSE[rows, :])
                p = (p * (1.0 / total)).astype(bf16)
                mixed = jnp.dot(p, V[keys, shared], preferred_element_type=f32)
                OB[rows, columns] = mixed.astype(bf16)
                return 0

            lax.fori_loop(0, QUERY_HEADS, head, 0)
            if b == 0:
                wc[3].wait_recv()
                wt[3].wait_recv()
                late[3].start()
                pass_on(1)
                late[3].wait()
            for t in range(3):
                ns = pl.ds(t * 512, 512)
                Y1[rows, ns] = X[rows, ns].astype(f32) + jnp.dot(
                    OB[rows, :], WO[:, ns], preferred_element_type=f32
                )
            for n in range(2):
                block = pl.ds(b * 256 + n * 128, 128)
                value = Y1[block, :]
                r = lax.rsqrt(jnp.mean(value * value, axis=1, keepdims=True) + epsilon)
                h2 = (value * r * G2[...]).astype(bf16)
                H[block, :MODEL_WIDTH] = h2
                gates = router_rows(h2, RT[...], RO[block, :])[3]
                high = gates.astype(bf16).astype(f32)
                H[block, MODEL_WIDTH:] = (high + pltpu.roll(gates - high, 8, 1)).astype(bf16)
            hx(b).start()
            hc(b).start()
        stores = [
            local_copy(p[0], p[1], st_s.at[n])
            for n, p in enumerate(
                ((Y1, y1), (H1, h1), (Q, q), (K, k), (V, v), (OB, ob), (LSE, lse))
            )
        ]
        for copy in stores:
            copy.start()
        pass_on(2)
        for copy in stores:
            copy.wait()

    pl.run_scoped(
        front,
        part(ROWS, MODEL_WIDTH), part(ROWS, MODEL_WIDTH), part(MODEL_WIDTH, MODEL_WIDTH),
        part(MODEL_WIDTH, 512), part(MODEL_WIDTH, MODEL_WIDTH), part(ROWS, MODEL_WIDTH),
        part(ROWS, 256), part(ROWS, 256), part(ROWS, MODEL_WIDTH), vm((ROWS, ROWS), f32),
        vm((ROWS, PAD), f32), vm((ROWS, PAD), f32), vm((ROWS, PAD), f32),
        vm((ROWS, PAD), jnp.int32), vm((ROWS, PAD), jnp.int32), vm((8, ROWS), jnp.int32),
        part(2, 16, HALF), vm((ROWS, MODEL_WIDTH), f32),
    )

    def parts_of(n):
        return n // (3 * PER), (n // PER) % 3, n % PER

    def y_copy(n):
        j, m, i = parts_of(n)
        src = gr.at[j, m, pl.ds((1 - y) * HALF + i * CHUNK, CHUNK)]
        return remote(src, ya.at[n], y_s.at[n], y_r.at[n], ydev)

    def spot(n, expert):
        j, m, i = parts_of(n)
        return out.at[m, expert + j, pl.ds(i * CHUNK, CHUNK)]

    def load_a(n):
        j, m, i = parts_of(n)
        src = gr.at[j, m, pl.ds(y * HALF + i * CHUNK, CHUNK)]
        return local_copy(src, VA.at[n % 2], ld_a.at[n % 2])

    def load_b(n):
        return local_copy(ya.at[n], VB.at[n % 2], ld_b.at[n % 2])

    def load_z(n):
        return local_copy(za.at[n], VZ.at[n % 2], ld_z.at[n % 2])

    def load_f(n):
        return local_copy(zb.at[n], VF.at[n % 2], ld_f.at[n % 2])

    def z1_copy(n):
        return remote(VS.at[n % 4], za.at[n], z1_s.at[n], z1_r.at[n], zdev)

    def z2_copy(n):
        return remote(VT.at[n % 4], zb.at[n], z2_s.at[n], z2_r.at[n], mdev)

    def z3_copy(n):
        return remote(FN.at[n % 4], spot(n, e0), z3_s.at[n], z3_r.at[n], zdev)

    def z4_copy(n):
        return remote(spot(n, other), spot(n, other), z4_s.at[n], z4_r.at[n], zdev)

    def store_f(n):
        return local_copy(FN.at[n % 4], spot(n, e0), fo.at[n % 4])

    def x_copy(n):
        return remote(spot(n, e0), spot(n, e0), x_s.at[n], x_r.at[n], xdev)

    def c1_copy(n):
        return remote(spot(n, e0), spot(n, e0), c1_s.at[n], c1_r.at[n], cdev)

    def c2_copy(n):
        return remote(spot(n, other), spot(n, other), c2_s.at[n], c2_r.at[n], cdev)

    def handed(n):
        return n % 2 == 1

    def crosses(n):
        return (n % 2 == 0) | ((n % 4 == 1) & mid) | ((n % 4 == 3) & end)

    def when(n, cond=None):
        ok = (n >= 0) & (n < CHUNKS)
        return pl.when(ok if cond is None else ok & cond)

    def slot(s):
        n = s - AT_CZ

        @when(n, jnp.logical_not(crosses(n + 4 * CHUNKS)))
        def _(n=n):
            z4_copy(n).wait_recv()
            c2_copy(n).start()

        n = s - AT_CX
        crossed = crosses(n + 4 * CHUNKS)

        @when(n, crossed)
        def _(n=n):
            x_copy(n).wait_recv()
            c2_copy(n).start()

        @when(n, crossed & handed(n + 4 * CHUNKS))
        def _(n=n):
            z4_copy(n).start()

        n = s - AT_X

        @when(n, mid)
        def _(n=n):
            store_f(n).wait()
            z3_copy(n).wait_send()

        @when(n, end)
        def _(n=n):
            z3_copy(n).wait_recv()

        @when(n, crosses(n + 4 * CHUNKS))
        def _(n=n):
            x_copy(n).start()

        @when(n)
        def _(n=n):
            c1_copy(n).start()

        n = s - AT_FL - 1

        @when(n, mid)
        def _(n=n):
            load_f(n).wait()
            z2_copy(n).wait_send()
            FN[n % 4] = (VT[n % 4].astype(f32) + VF[n % 2].astype(f32)).astype(bf16)
            z3_copy(n).start()
            store_f(n).start()

        n = s - AT_FL

        @when(n, mid)
        def _(n=n):
            z2_copy(n).wait_recv()
            load_f(n).start()

        n = s - AT_ZL - 1

        @when(n, mid)
        def _(n=n):
            load_z(n).wait()
            VT[n % 4] = (VS[n % 4].astype(f32) + VZ[n % 2].astype(f32)).astype(bf16)
            z2_copy(n).start()

        n = s - AT_ZL

        @when(n, mid)
        def _(n=n):
            z1_copy(n).wait_recv()
            load_z(n).start()

        n = s - 5

        @when(n, end)
        def _(n=n):
            z1_copy(n).wait_send()

        n = s - 1

        @when(n)
        def _(n=n):
            load_a(n).wait()
            load_b(n).wait()
            VS[n % 4] = (VA[n % 2].astype(f32) + VB[n % 2].astype(f32)).astype(bf16)

        @when(n, end)
        def _(n=n):
            z1_copy(n).start()

        @when(s)
        def _():
            y_copy(s).wait_recv()
            load_a(s).start()
            load_b(s).start()

    def slots(first, last):
        def step(s, _):
            slot(s)
            return 0

        lax.fori_loop(first, last, step, 0)

    third, second = pl.ds(3 * ROWS, ROWS), pl.ds(2 * ROWS, ROWS)
    first, zeroth = pl.ds(ROWS, ROWS), pl.ds(0, ROWS)

    def experts(G, ACT, STG, RS, OS):
        gain_rows = [
            local_copy(src, G.at[pl.ds(n * ROWS, ROWS)], loc.at[n])
            for n, src in enumerate((g, gl.at[0], gl.at[1], gl.at[2]))
        ]
        gain_rows[0].start()
        gc.wait_recv()
        gain_rows[1].start()

        def gate_of(j, rows):
            lane = lax.broadcasted_iota(jnp.int32, (2 * ROWS, PAD), 1)
            packed = H[rows, MODEL_WIDTH:].astype(f32)
            picked = (lane == e0 + j) | (lane == e0 + j + 8)
            return jnp.sum(jnp.where(picked, packed, 0.0), axis=1, keepdims=True), lane

        def forward(j, begin, base=None):
            rows = pl.ds(begin, 2 * ROWS)
            gate, lane = gate_of(j, rows)

            def step(t, total):
                columns = pl.ds(pl.multiple_of(t * 256, 256), 256)
                ug = jnp.dot(
                    H[rows, :MODEL_WIDTH], W[j, 0, :, columns], preferred_element_type=f32
                )
                uu = jnp.dot(
                    H[rows, :MODEL_WIDTH], W[j, 1, :, columns], preferred_element_type=f32
                )
                dh = jnp.dot(G[rows, :], W[j, 2, :, columns], preferred_element_type=f32)
                sigma = jax.nn.sigmoid(ug)
                silu = ug * sigma
                hid = silu * uu
                ACT[j, 0, rows, columns] = (hid * gate).astype(bf16)
                dhg = dh * gate
                ACT[j, 1, rows, columns] = (
                    dhg * uu * sigma * (1.0 + ug * (1.0 - sigma))
                ).astype(bf16)
                ACT[j, 2, rows, columns] = (dhg * silu).astype(bf16)
                if base is not None:
                    slot(base + t)
                return total + jnp.sum(hid * dh, axis=1, keepdims=True)

            total = lax.fori_loop(0, FF // 256, step, jnp.zeros((2 * ROWS, 1), f32))
            high = total.astype(bf16).astype(f32)
            low = total - high
            here = jnp.where(lane == e0 + j, high, jnp.where(lane == e0 + j + 8, low, 0.0))
            if j == 0:
                DG[rows, :] = here.astype(bf16)
            else:
                DG[rows, :] = (DG[rows, :].astype(f32) + here).astype(bf16)

        def back_rows(rows, ns):
            o = nt_dot(ACT[0, 0, rows, :], W[0, 2, ns, :])
            o = o + nt_dot(ACT[1, 0, rows, :], W[1, 2, ns, :])
            e = nt_dot(ACT[0, 1, rows, :], W[0, 0, ns, :])
            e = e + nt_dot(ACT[0, 2, rows, :], W[0, 1, ns, :])
            e = e + nt_dot(ACT[1, 1, rows, :], W[1, 0, ns, :])
            e = e + nt_dot(ACT[1, 2, rows, :], W[1, 1, ns, :])
            return o, e

        def store_tile(j, m, half, i, place_in):
            rows = pl.ds(half * HALF + i * 384, 384)
            return local_copy(STG.at[place_in], gr.at[j, m, rows], stg_sem.at[place_in])

        def weight_tile(j, m, left, half, i, place_in):
            begin = half * HALF + i * 384
            lhs = left[:, pl.ds(pl.multiple_of(begin, 128), 384)]
            STG[place_in] = tn_dot(lhs, ACT[j, (m + 1) % 3]).astype(bf16)
            copy = store_tile(j, m, half, i, place_in)
            copy.start()
            return copy

        def weight_grads(j, base=None):
            done = 0
            for left, m0, steps in ((H, 0, 4), (G, 2, 2)):

                def step(n, _, left=left, m0=m0, done=done):
                    m, i = m0 + n // 2, n % 2
                    away = weight_tile(j, m, left, 1 - y, i, 0)

                    @pl.when(n + done > 0)
                    def _():
                        store_tile(j, m, y, i, 1).wait()

                    weight_tile(j, m, left, y, i, 1)
                    away.wait()
                    begin = (j * 3 + m) * PER + i * (384 // CHUNK)
                    for p in range(384 // CHUNK):
                        y_copy(begin + p).start()
                    if base is not None:
                        slot(base + done + n)
                    return 0

                lax.fori_loop(0, steps, step, 0)
                done += steps
            store_tile(j, 2, y, 1, 1).wait()

        def rc_copy(t, which):
            ns = pl.ds(pl.multiple_of(t * 512, 512), 512)
            src, dst = ((RS, CR), (OS, CO))[which]
            return remote(
                src.at[t % 2], dst.at[:, ns], rc_s.at[which, t], rc_r.at[which, t], cdev
            )

        def rb_copy(t, which):
            ns = pl.ds(pl.multiple_of(t * 512, 512), 512)
            src, dst = ((RS, r_core), (OS, o_core))[which]
            return remote(
                src.at[t % 2], dst.at[:, ns], rd_s.at[1 + which * 3 + t],
                rd_r.at[1 + which * 3 + t], cdev,
            )

        def ro_copy(t):
            ns = pl.ds(pl.multiple_of(t * 512, 512), 512)
            return local_copy(OS.at[t % 2], o_own.at[:, ns], ro.at[t])

        for n in range(3):
            wz(n).wait_recv()
            own_half(n).wait()
        gain_rows[0].wait()
        gain_rows[1].wait()
        for b in range(2):
            hc(b).wait_recv()
        pass_on(3)
        forward(0, 0)
        gx.wait_recv()
        gt.start()
        gain_rows[2].start()
        pass_on(4)
        for b in range(2):
            hx(b).wait_recv()
            hd(b).start()
        pass_on(5)
        gt.wait_recv()
        gain_rows[3].start()
        for b in range(2):
            hd(b).wait_recv()
        gain_rows[2].wait()
        gain_rows[3].wait()
        forward(0, 2 * ROWS)
        weight_grads(0)
        for n in range(3, 6):
            wz(n).wait_recv()
            own_half(n).wait()
        forward(1, 2 * ROWS, 0)

        def third_step(t, _):
            ns = pl.ds(pl.multiple_of(t * 512, 512), 512)

            @pl.when(t == 2)
            def _():
                rc_copy(0, 0).wait_send()
                rc_copy(0, 1).wait_send()

            o, e = back_rows(third, ns)
            RS[t % 2] = e.astype(bf16)
            OS[t % 2] = o.astype(bf16)
            rc_copy(t, 0).start()
            rc_copy(t, 1).start()
            slot(3 + t)
            return 0

        lax.fori_loop(0, 3, third_step, 0)
        dg_copy = remote(
            DG.at[third], CR.at[:, pl.ds(MODEL_WIDTH, PAD)], rd_s.at[0], rd_r.at[0], cdev
        )
        dg_copy.start()

        def second_step(t, _):
            ns = pl.ds(pl.multiple_of(t * 512, 512), 512)
            o, e = back_rows(second, ns)
            rc_copy(t, 0).wait_recv()
            rc_copy(t, 1).wait_recv()
            CR[:, ns] = (CR[:, ns].astype(f32) + e).astype(bf16)
            CO[:, ns] = (CO[:, ns].astype(f32) + o).astype(bf16)
            slot(6 + t)
            return 0

        lax.fori_loop(0, 3, second_step, 0)
        dg_copy.wait_recv()
        CR[:, MODEL_WIDTH:] = CR[:, MODEL_WIDTH:] + DG[second, :]
        rx.start()
        forward(1, 0, 9)
        weight_grads(1, 12)
        for which in range(2):
            for t in (1, 2):
                rc_copy(t, which).wait_send()
        dg_copy.wait_send()
        tail_b.start()

        def first_step(t, _):
            ns = pl.ds(pl.multiple_of(t * 512, 512), 512)

            @pl.when(t == 2)
            def _():
                rb_copy(0, 0).wait_send()
                rb_copy(0, 1).wait_send()

            o, e = back_rows(first, ns)
            RS[t % 2] = e.astype(bf16)
            OS[t % 2] = o.astype(bf16)
            rb_copy(t, 0).start()
            rb_copy(t, 1).start()
            slot(18 + t)
            return 0

        lax.fori_loop(0, 3, first_step, 0)
        for t in (1, 2):
            rb_copy(t, 0).wait_send()
            rb_copy(t, 1).wait_send()

        def zeroth_step(t, _):
            ns = pl.ds(pl.multiple_of(t * 512, 512), 512)
            o, e = back_rows(zeroth, ns)

            @pl.when(t == 2)
            def _():
                ro_copy(0).wait()

            H[first, ns] = e.astype(bf16)
            OS[t % 2] = o.astype(bf16)
            ro_copy(t).start()
            slot(21 + t)
            return 0

        lax.fori_loop(0, 3, zeroth_step, 0)
        H[first, MODEL_WIDTH:] = DG[zeroth, :]
        for t in range(3):
            rb_copy(t, 0).wait_recv()
            rb_copy(t, 1).wait_recv()
        for t in (1, 2):
            ro_copy(t).wait()
        for n in range(6):
            wy(n).wait_send()
            wz(n).wait_send()
        for n in range(4):
            wa[n].wait_send()
            wx[n].wait_send()
            wc[n].wait_send()
            wt[n].wait_send()
        wa[4].wait_send()
        for copy in (gx, gc, gt):
            copy.wait_send()
        for b in range(2):
            hx(b).wait_send()
            hc(b).wait_send()
            hd(b).wait_send()
        rx.wait_send()

    rx = remote(CR, r_x, rx_s.at[0], rx_r.at[0], xdev)
    ox = remote(CO, o_x, rx_s.at[1], rx_r.at[1], xdev)
    tail_b = remote(
        DG.at[first], r_core.at[:, pl.ds(MODEL_WIDTH, PAD)], rd_s.at[7], rd_r.at[7], cdev
    )
    pl.run_scoped(
        experts,
        vm((4 * ROWS, MODEL_WIDTH), bf16),
        vm((2, 3, 4 * ROWS, FF), bf16),
        vm((2, 384, FF), bf16),
        vm((2, ROWS, 512), bf16),
        vm((2, ROWS, 512), bf16),
    )
    ox.start()
    tail_b.wait()

    def attention(
        Y1, DY, GB, XB, H1, OB, QB, KB, VV, DA, DOB, DQKV, BIAS, LSE, COS, SIN, RO,
        SC, SR, DL, GS, DK, DV, STG,
        AA, AB, PP, VY, QQ, VX, AS, AZ, AT, AF, AN,
    ):
        pairs = [
            (segc, SC), (segr, SR), (y1, Y1), (g, GB), (routes, RO), (r_core, H.at[second]),
            (ob, OB), (q, QB), (k, KB), (v, VV), (lse, LSE), (cos, COS), (sin, SIN), (h1, H1),
            (xin, XB),
        ]
        for n, ws in ((1, (wo, woo)), (0, (wq, wqo))):
            for w, rows in zip(ws, (pl.ds(y * HALF, HALF), pl.ds((1 - y) * HALF, HALF))):
                for side in range(2):
                    pairs.append((w.at[:, pl.ds(side * HALF, HALF)], W.at[n, side, rows]))
        for ws, columns in (((wk, wko), pl.ds(0, 256)), ((wv, wvo), pl.ds(256, 256))):
            for w, rows in zip(ws, (pl.ds(y * HALF, HALF), pl.ds((1 - y) * HALF, HALF))):
                pairs.append((w, W.at[0, 2, rows, columns]))
        loads = [local_copy(p[0], p[1], att.at[n]) for n, p in enumerate(pairs)]
        for copy in loads:
            copy.start()

        def need(first, last):
            for copy in loads[first:last]:
                copy.wait()

        slots(24, 26)
        need(0, 2)
        mask_bias(SC, SR, BIAS)
        slots(26, 28)
        need(2, 6)
        rx.wait_recv()
        last = local_copy(r_x, H.at[third], att.at[len(pairs)])
        last.start()
        last.wait()

        def rows_of(n):
            q_, i = n // 2, n % 2
            return q_, i * 384

        def ac_copy(n):
            b, begin = rows_of(n)
            src = d.at[b, :, pl.ds(begin + (1 - c) * 192, 192)]
            return remote(src, ca.at[n], ac_s.at[n], ac_r.at[n], cdev)

        def aload_a(n):
            b, begin = rows_of(n)
            return local_copy(d.at[b, :, pl.ds(begin + c * 192, 192)], AA.at[n % 2], ald.at[0, n % 2])

        def aload_b(n):
            return local_copy(ca.at[n], AB.at[n % 2], ald.at[1, n % 2])

        def ay_copy(n):
            return remote(PP.at[n % 4, 1 - y], yb.at[n], ay_s.at[n], ay_r.at[n], ydev)

        def aload_y(n):
            return local_copy(yb.at[n], VY.at[n % 2], aldy.at[n % 2])

        def ax_copy(n):
            src = QQ.at[n % 4, pl.ds((1 - x) * QUARTER, QUARTER)]
            return remote(src, xb.at[n], ax_s.at[n], ax_r.at[n], xdev)

        def aload_x(n):
            return local_copy(xb.at[n], VX.at[n % 2], aldx.at[n % 2])

        def az1_copy(n):
            return remote(AS.at[n % 8], zc.at[n], az1_s.at[n], az1_r.at[n], zdev)

        def aload_z(n):
            return local_copy(zc.at[n], AZ.at[n % 2], aldz.at[n % 2])

        def az2_copy(n):
            return remote(AT.at[n % 4], zd.at[n], az2_s.at[n], az2_r.at[n], mdev)

        def aload_f(n):
            return local_copy(zd.at[n], AF.at[n % 2], aldf.at[n % 2])

        def aspot(n, xx, cc):
            b, begin = rows_of(n)
            columns = pl.ds(pl.multiple_of(b * WIDTH, WIDTH), WIDTH)
            return aout.at[pl.ds(begin + cc * 192 + xx * QUARTER, QUARTER), columns]

        def az3_copy(n):
            return remote(AN.at[n % 4], aspot(n, x, c), az3_s.at[n], az3_r.at[n], zdev)

        def astore(n):
            return local_copy(AN.at[n % 4], aspot(n, x, c), afo.at[n % 4])

        def axg_copy(n):
            return remote(aspot(n, x, c), aspot(n, x, c), axg_s.at[n], axg_r.at[n], xdev)

        def ac1_copy(n):
            return remote(aspot(n, x, c), aspot(n, x, c), ac1_s.at[n], ac1_r.at[n], cdev)

        def ac2_copy(n):
            return remote(aspot(n, 1 - x, c), aspot(n, 1 - x, c), ac2_s.at[n], ac2_r.at[n], cdev)

        def awhen(n, cond=None):
            ok = (n >= 0) & (n < PARTS)
            return pl.when(ok if cond is None else ok & cond)

        def aslot(s):
            @awhen(s - 24)
            def _():
                axg_copy(s - 24).wait_recv()
                ac2_copy(s - 24).start()

            @awhen(s - 20, mid)
            def _():
                astore(s - 20).wait()
                az3_copy(s - 20).wait_send()

            @awhen(s - 20, end)
            def _():
                az3_copy(s - 20).wait_recv()

            @awhen(s - 20)
            def _():
                axg_copy(s - 20).start()
                ac1_copy(s - 20).start()

            @awhen(s - 17, mid)
            def _():
                n = s - 17
                aload_f(n).wait()
                az2_copy(n).wait_send()
                AN[n % 4] = (AT[n % 4].astype(f32) + AF[n % 2].astype(f32)).astype(bf16)
                az3_copy(n).start()
                astore(n).start()

            @awhen(s - 16, mid)
            def _():
                az2_copy(s - 16).wait_recv()
                aload_f(s - 16).start()

            @awhen(s - 13, mid)
            def _():
                n = s - 13
                aload_z(n).wait()
                AT[n % 4] = (AS[n % 8].astype(f32) + AZ[n % 2].astype(f32)).astype(bf16)
                az2_copy(n).start()

            @awhen(s - 13, end)
            def _():
                az1_copy(s - 13).wait_send()

            @awhen(s - 12, mid)
            def _():
                az1_copy(s - 12).wait_recv()
                aload_z(s - 12).start()

            @awhen(s - 9)
            def _():
                n = s - 9
                aload_x(n).wait()
                ax_copy(n).wait_send()
                mine = pl.ds(pl.multiple_of(x * QUARTER, 16), QUARTER)
                AS[n % 8] = (QQ[n % 4, mine, :].astype(f32) + VX[n % 2].astype(f32)).astype(bf16)

            @awhen(s - 9, end)
            def _():
                az1_copy(s - 9).start()

            @awhen(s - 8)
            def _():
                ax_copy(s - 8).wait_recv()
                aload_x(s - 8).start()

            @awhen(s - 5)
            def _():
                n = s - 5
                aload_y(n).wait()
                ay_copy(n).wait_send()
                QQ[n % 4] = (PP[n % 4, y].astype(f32) + VY[n % 2].astype(f32)).astype(bf16)
                ax_copy(n).start()

            @awhen(s - 4)
            def _():
                ay_copy(s - 4).wait_recv()
                aload_y(s - 4).start()

            @awhen(s - 1)
            def _():
                n = s - 1
                aload_a(n).wait()
                aload_b(n).wait()
                PP[n % 4] = (AA[n % 2].astype(f32) + AB[n % 2].astype(f32)).astype(bf16)
                ay_copy(n).start()

            @awhen(s)
            def _():
                ac_copy(s).wait_recv()
                aload_a(s).start()
                aload_b(s).start()

        def emit(b, left, right):
            copies = []
            for half in range(2):
                STG[half] = tn_dot(left[:, pl.ds(half * HALF, HALF)], right).astype(bf16)
                copies.append(local_copy(STG.at[half], d.at[b, half], stg_sem.at[half]))
                copies[half].start()
            for copy in copies:
                copy.wait()
            ac_copy(2 * b).start()
            ac_copy(2 * b + 1).start()

        def returned(rows):
            begin = rows.start
            one = H[pl.ds(pl.multiple_of(begin + ROWS, 128), 128), :].astype(f32)
            two = H[pl.ds(pl.multiple_of(begin + 2 * ROWS, 128), 128), :].astype(f32)
            three = H[pl.ds(pl.multiple_of(begin + 3 * ROWS, 128), 128), :].astype(f32)
            return one + two + three

        middle_backward(
            returned, lambda rows: H[rows, :MODEL_WIDTH], RT, RO, Y1, GB, G2, DL, DY, DA, GS
        )
        for half in range(2):
            columns = pl.ds(half * HALF, HALF)
            SM[half, 9:10, :] = GS[:, columns].astype(bf16)
            router = tn_dot(DL[...], H[zeroth, columns])
            SM[half, 0:8, :] = router[0:8].astype(bf16)
            SM[half, 10:16, :] = jnp.zeros((6, HALF), bf16)

        def out_block(b, _):
            emit(b, OB, DA[:, pl.ds(pl.multiple_of(b * WIDTH, WIDTH), WIDTH)])
            slot(28 + b)
            return 0

        need(6, 7)
        lax.fori_loop(0, 3, out_block, 0)
        need(15, 19)

        def dob_tile(t, _):
            ns = pl.ds(pl.multiple_of(t * 512, 512), 512)
            tile = nt_dot(DA[:, :HALF], W[1, 0, ns, :]) + nt_dot(DA[:, HALF:], W[1, 1, ns, :])
            DOB[:, ns] = tile.astype(bf16)
            slot(31 + t)
            return 0

        lax.fori_loop(0, 3, dob_tile, 0)
        need(7, 13)
        state = [34, 0]

        def tick():
            first_slot, first_part = state

            def step(n, _):
                slot(first_slot + n)
                return 0

            lax.fori_loop(0, 2, step, 0)
            if first_part < 6:
                lax.fori_loop(0, 2, lambda n, _: (aslot(first_part + n), 0)[1], 0)
            state[0] += 2
            state[1] = min(state[1] + 2, 6)

        heads_backward(QB, KB, VV, DOB, BIAS, LSE, COS, SIN, DQKV, DK, DV, tick)
        done, parts_done = state

        def qkv_block(b, _):
            emit(3 + b, H1, DQKV[:, pl.ds(pl.multiple_of(b * WIDTH, WIDTH), WIDTH)])
            slot(done + b)
            return 0

        need(13, 14)
        lax.fori_loop(0, 4, qkv_block, 0)
        need(14, 15)
        need(19, 27)
        done += 4

        def dh1_tile(t, _):
            ns = pl.ds(pl.multiple_of(t * 512, 512), 512)
            tile = nt_dot(DQKV[:, :HALF], W[0, 0, ns, :])
            tile = tile + nt_dot(DQKV[:, HALF:MODEL_WIDTH], W[0, 1, ns, :])
            Y1[:, ns] = tile + nt_dot(DQKV[:, MODEL_WIDTH:], W[0, 2, ns, :512])
            slot(done + t)
            aslot(parts_done + t)
            return 0

        lax.fori_loop(0, 3, dh1_tile, 0)
        done, parts_done = done + 3, parts_done + 3
        first_backward(Y1, XB, DY, G1, GB, GS)
        for half in range(2):
            SM[half, 8:9, :] = GS[:, pl.ds(half * HALF, HALF)].astype(bf16)
        result = local_copy(GB, hgrad, att.at[len(pairs) + 1])
        result.start()

        for i, device in enumerate((cdev, xdev, ydev, zdev, mdev)):
            hop = remote(SM, sa.at[i], s_s.at[i], s_r.at[i], device)
            hop.start()
            slot(done)
            aslot(parts_done)
            done, parts_done = done + 1, parts_done + 1
            hop.wait()
            load = local_copy(sa.at[i], SB, sl.at[0])
            load.start()
            load.wait()
            SM[...] = (SM[...].astype(f32) + SB[...].astype(f32)).astype(bf16)
        small = local_copy(SM, smo, sl.at[1])
        small.start()

        last_slot = max(EXPERT_SLOTS - done, PART_SLOTS - parts_done)

        def drain(n, _):
            slot(done + n)
            aslot(parts_done + n)
            return 0

        lax.fori_loop(0, last_slot, drain, 0)
        small.wait()
        result.wait()

        def finish_part(n, _):
            ac_copy(n).wait_send()
            axg_copy(n).wait_send()
            ac1_copy(n).wait()
            ac2_copy(n).wait()
            return 0

        lax.fori_loop(0, PARTS, finish_part, 0)

    pl.run_scoped(
        attention,
        vm((ROWS, MODEL_WIDTH), f32), vm((ROWS, MODEL_WIDTH), f32),
        part(ROWS, MODEL_WIDTH), part(ROWS, MODEL_WIDTH), part(ROWS, MODEL_WIDTH),
        part(ROWS, MODEL_WIDTH), part(ROWS, MODEL_WIDTH), part(ROWS, 256), part(ROWS, 256),
        part(ROWS, MODEL_WIDTH), part(ROWS, MODEL_WIDTH), part(ROWS, 2048),
        vm((ROWS, ROWS), f32), vm((ROWS, PAD), f32), vm((ROWS, PAD), f32), vm((ROWS, PAD), f32),
        vm((ROWS, PAD), jnp.int32), vm((ROWS, PAD), jnp.int32), vm((8, ROWS), jnp.int32),
        part(ROWS, PAD), vm((1, MODEL_WIDTH), f32), vm((2, ROWS, PAD), f32),
        vm((2, ROWS, PAD), f32), part(2, HALF, WIDTH),
        part(2, 2, 192, WIDTH), part(2, 2, 192, WIDTH), part(4, 2, 192, WIDTH),
        part(2, 192, WIDTH), part(4, 192, WIDTH), part(2, QUARTER, WIDTH), part(8, QUARTER, WIDTH),
        part(2, QUARTER, WIDTH), part(4, QUARTER, WIDTH), part(2, QUARTER, WIDTH),
        part(4, QUARTER, WIDTH),
    )
    ox.wait()

    def finish(n, _):
        @pl.when(crosses(n))
        def _():
            x_copy(n).wait_send()

        @pl.when(crosses(n) & handed(n))
        def _():
            z4_copy(n).wait_send()

        c1_copy(n).wait()
        c2_copy(n).wait()
        y_copy(n).wait_send()
        return 0

    lax.fori_loop(0, CHUNKS, finish, 0)


def layer_call(*arrays):
    anyspace = pl.BlockSpec(memory_space=pl.ANY)
    dma = pltpu.SemaphoreType.DMA
    vmem = lambda *s: pltpu.VMEM(s, bf16)
    n = PARTS
    wide, narrow = (ROWS, MODEL_WIDTH), (ROWS, 256)
    shapes = [wide] * 3
    shapes += [(3, 8, HALF, FF), (HALF, BLOCKS * WIDTH), (2, 16, HALF), wide]
    shapes += [(*wide, f32), wide, wide, narrow, narrow, wide, (ROWS, PAD, f32)]
    shapes += [(HALF, MODEL_WIDTH), (HALF, 256), (HALF, 256), (HALF, MODEL_WIDTH), (16, HALF)]
    shapes += [(3, ROWS, MODEL_WIDTH)]
    shapes += [(ROWS, WIDE)] * 2 + [(2, 3, MODEL_WIDTH, FF)] + [(CHUNKS, CHUNK, FF)] * 3
    shapes += [(BLOCKS, 2, HALF, WIDTH), (n, 2, 192, WIDTH), (n, 192, WIDTH)]
    shapes += [(n, QUARTER, WIDTH)] * 3 + [(5, 2, 16, HALF)]
    outputs = [
        jax.ShapeDtypeStruct(s[:-1], f32) if s[-1] is f32 else jax.ShapeDtypeStruct(s, bf16)
        for s in shapes
    ]
    many, few = dma((CHUNKS,)), dma((n,))
    scratch = [
        vmem(4 * ROWS, WIDE), vmem(2, 3, MODEL_WIDTH, FF), vmem(4 * ROWS, PAD), vmem(ROWS, WIDE),
        vmem(ROWS, MODEL_WIDTH), vmem(2, CHUNK, FF), vmem(2, CHUNK, FF), vmem(4, CHUNK, FF),
        vmem(2, CHUNK, FF), vmem(4, CHUNK, FF), vmem(2, CHUNK, FF), vmem(4, CHUNK, FF),
        vmem(2, 16, HALF), vmem(2, 16, HALF), vmem(PAD, MODEL_WIDTH),
        pltpu.VMEM((1, MODEL_WIDTH), f32), pltpu.VMEM((1, MODEL_WIDTH), f32),
        dma((16,)), dma((11,)), dma((11,)), dma((5,)), dma((5,)), dma((5,)), dma((5,)), dma((5,)),
        dma((5,)), dma((6,)), dma((6,)), dma((2,)), dma((2,)), dma((2,)), dma((2,)), dma((2,)),
        dma((2,)), dma((6,)), dma((7,)),
        dma((4,)), dma((2,)), many, many, dma((2,)), dma((2,)),
        many, many, dma((2,)), many, many, dma((2,)),
        many, many, dma((4,)), many, many, many, many, many, many, many, many,
        dma((2, 3)), dma((2, 3)), dma((2,)), dma((2,)), dma((8,)), dma((8,)), dma((3,)),
        few, few, dma((2, 2)), few, few, dma((2,)), few, few, dma((2,)), few, few, dma((2,)),
        few, few, dma((2,)), few, few, dma((4,)), few, few, few, few, few, few,
        dma((5,)), dma((5,)), dma((2,)), dma((32,)),
    ]
    return pl.pallas_call(
        layer_kernel,
        out_shape=outputs,
        in_specs=[anyspace] * len(arrays),
        out_specs=[anyspace] * len(shapes),
        scratch_shapes=scratch,
        compiler_params=pltpu.CompilerParams(
            collective_id=2, has_side_effects=True, vmem_limit_bytes=67 * 1000 * 1000
        ),
        name="layer",
    )(*arrays)[:8]


def attention_forward(hidden, segments, gain_one, w_q, w_k, w_v, w_o, gain_two):
    sequence_length = hidden.shape[0]
    group = QUERY_HEADS // KEY_VALUE_HEADS
    head_scale = HEAD_SIZE ** (-0.5)
    cosine, sine = tables(sequence_length, HEAD_SIZE)
    normed_f, scale_one = normalize(hidden, gain_one)
    h1 = normed_f.astype(bf16)
    qr = jnp.dot(h1, w_q, preferred_element_type=f32)
    kr = jnp.dot(h1, w_k, preferred_element_type=f32)
    values = jnp.dot(h1, w_v, preferred_element_type=f32).astype(bf16)
    values = values.reshape(sequence_length, KEY_VALUE_HEADS, HEAD_SIZE)
    qr = qr.reshape(sequence_length, QUERY_HEADS, HEAD_SIZE)
    kr = kr.reshape(sequence_length, KEY_VALUE_HEADS, HEAD_SIZE)
    queries = apply_rotary(qr, cosine, sine).astype(bf16)
    queries = queries.reshape(sequence_length, KEY_VALUE_HEADS, group, HEAD_SIZE)
    keys = apply_rotary(kr, cosine, sine).astype(bf16)
    position = jnp.arange(sequence_length)
    allowed = (position[None, :] <= position[:, None]) & (segments[:, None] == segments[None, :])
    scores = jnp.einsum("qkgd,skd->kgqs", queries, keys, preferred_element_type=f32) * head_scale
    scores = jnp.where(allowed, scores, -1e30)
    top_score = jnp.max(scores, axis=-1, keepdims=True)
    exp_scores = jnp.exp(scores - top_score)
    sum_exp = jnp.sum(exp_scores, axis=-1, keepdims=True)
    log_total = top_score + jnp.log(sum_exp)
    probs = (exp_scores / sum_exp).astype(bf16)
    mixed = jnp.einsum("kgqs,skd->qkgd", probs, values, preferred_element_type=f32)
    mixed = mixed.reshape(sequence_length, QUERY_HEADS * HEAD_SIZE).astype(bf16)
    middle = hidden + jnp.dot(mixed, w_o, preferred_element_type=f32)
    normed_two_f, scale_two = normalize(middle, gain_two)
    h2 = normed_two_f.astype(bf16)
    kept = (scale_one, h1, queries, keys, values, allowed, log_total, mixed, middle, scale_two)
    return h2, kept


def router_forward(h2, w_router, routes):
    logits = jnp.dot(h2, w_router, preferred_element_type=f32)
    probs = softmax_rows(logits)
    experts = w_router.shape[1]
    chosen = jnp.any(
        routes[:, :, None] == jnp.arange(experts, dtype=jnp.int32)[None, None, :], axis=1
    )
    picked = jnp.where(chosen, probs, 0.0)
    total = jnp.sum(picked, axis=-1, keepdims=True)
    return probs, chosen, total, picked / total


def router_backward(h2, w_router, probs, chosen, total, gates, gate_grads):
    gate_grads = jnp.where(chosen, gate_grads, 0.0)
    weighted = jnp.sum(gate_grads * gates, axis=-1, keepdims=True)
    prob_grad = jnp.where(chosen, (gate_grads - weighted) / total, 0.0)
    logit_grad = probs * (prob_grad - jnp.sum(prob_grad * probs, axis=-1, keepdims=True))
    logit_grad = logit_grad.astype(bf16)
    return contract(h2, logit_grad, 0, 0), contract(logit_grad, w_router, 1, 1)


def attention_backward(hidden, kept, gain_one, w_q, w_k, w_v, w_o, gain_two, upstream, dh2):
    scale_one, h1, queries, keys, values, allowed, log_total, mixed, middle, scale_two = kept
    sequence_length = hidden.shape[0]
    group = QUERY_HEADS // KEY_VALUE_HEADS
    head_scale = HEAD_SIZE ** (-0.5)
    cosine, sine = tables(sequence_length, HEAD_SIZE)
    middle_norm_grad, gain_two_grad = norm_back(middle, scale_two, gain_two, dh2)
    middle_grad = upstream + middle_norm_grad
    branch_grad = middle_grad.astype(bf16)
    out_proj_sum = contract(mixed, branch_grad, 0, 0)
    mixed_grad = contract(branch_grad, w_o, 1, 1).astype(bf16)
    mixed_grad = mixed_grad.reshape(sequence_length, KEY_VALUE_HEADS, group, HEAD_SIZE)
    probs = jnp.exp(
        jnp.einsum("qkgd,skd->kgqs", queries, keys, preferred_element_type=f32) * head_scale
        - log_total
    )
    probs = jnp.where(allowed, probs, 0.0)
    prob_back = jnp.einsum("qkgd,skd->kgqs", mixed_grad, values, preferred_element_type=f32)
    score_grad = probs * (prob_back - jnp.sum(prob_back * probs, axis=-1, keepdims=True))
    score_grad = score_grad.astype(bf16)
    dq = jnp.einsum("kgqs,skd->qkgd", score_grad, keys, preferred_element_type=f32) * head_scale
    dq = dq.reshape(sequence_length, QUERY_HEADS, HEAD_SIZE)
    dq = apply_rotary(dq, cosine, -sine).astype(bf16)
    dq = dq.reshape(sequence_length, QUERY_HEADS * HEAD_SIZE)
    dk = jnp.einsum("kgqs,qkgd->skd", score_grad, queries, preferred_element_type=f32) * head_scale
    dk = apply_rotary(dk, cosine, -sine).astype(bf16)
    dk = dk.reshape(sequence_length, KEY_VALUE_HEADS * HEAD_SIZE)
    dv = jnp.einsum("kgqs,qkgd->skd", probs.astype(bf16), mixed_grad, preferred_element_type=f32)
    dv = dv.astype(bf16).reshape(sequence_length, KEY_VALUE_HEADS * HEAD_SIZE)
    query_sum = contract(h1, dq, 0, 0)
    key_sum = contract(h1, dk, 0, 0)
    value_sum = contract(h1, dv, 0, 0)
    dh1 = contract(dq, w_q, 1, 1) + contract(dk, w_k, 1, 1) + contract(dv, w_v, 1, 1)
    hidden_norm_grad, gain_one_grad = norm_back(hidden, scale_one, gain_one, dh1)
    hidden_grad = (middle_grad + hidden_norm_grad).astype(bf16)
    return hidden_grad, (
        gain_one_grad,
        query_sum,
        key_sum,
        value_sum,
        out_proj_sum,
        gain_two_grad,
    )


def reduce_over_all(value, dimension):
    value = lax.psum_scatter(
        value.astype(bf16), "shard", scatter_dimension=dimension, tiled=True
    ).astype(f32)
    return lax.psum(value.astype(bf16), "rep").astype(f32)


def local(
    hidden_in,
    segment_ids,
    routes,
    out_grad,
    norm1_gain,
    w_query,
    key_weight,
    value_weight,
    w_out,
    norm2_gain,
    w_router,
    w_gate,
    w_up,
    w_down,
):
    small = jnp.concatenate(
        [w_router.T, norm1_gain[None], norm2_gain[None], jnp.zeros((6, HALF), bf16)], axis=0
    )
    cosine, sine = tables(ROWS, HEAD_SIZE)
    segments = segment_ids[0]
    o_own, o_core, o_x, grads, d, sm, hidden_grad, middle = layer_call(
        hidden_in,
        out_grad,
        w_query,
        key_weight,
        value_weight,
        w_out,
        small,
        w_gate,
        w_up,
        w_down,
        cosine[:, 0, :],
        turn_table(sine),
        jnp.pad(routes, ((0, 0), (0, PAD - TOPK))),
        jnp.broadcast_to(segments[:, None], (ROWS, PAD)),
        jnp.broadcast_to(segments[None, :], (8, ROWS)),
    )
    add = lambda a, b, c: a.astype(f32) + b.astype(f32) + c.astype(f32)
    hidden_out = (middle + add(o_own, o_core, o_x)).astype(bf16)
    sm = lax.dynamic_index_in_dim(sm, lax.axis_index("shard"), 0, keepdims=False).astype(f32)
    d = d.astype(f32)
    attn = (sm[8], d[:, 1536:3072], d[:, 3072:3328], d[:, 3328:], d[:, :1536], sm[9], sm[:8].T)
    grads = [grads[m].astype(f32) for m in range(3)]
    return (hidden_out, hidden_grad, *attn, *grads)


def local_any(
    hidden_in,
    segment_ids,
    routes,
    out_grad,
    norm1_gain,
    w_query,
    key_weight,
    value_weight,
    w_out,
    norm2_gain,
    w_router,
    w_gate,
    w_up,
    w_down,
):
    wide = lambda w, axis: lax.all_gather(w, "shard", axis=axis, tiled=True)
    gain_one, gain_two = wide(norm1_gain, 0).astype(f32), wide(norm2_gain, 0).astype(f32)
    w_q, w_k, w_v, w_o = (wide(w, 0) for w in (w_query, key_weight, value_weight, w_out))
    router = wide(w_router, 0)
    hidden = hidden_in.astype(f32)
    h2, kept = attention_forward(
        hidden, segment_ids[0], gain_one, w_q, w_k, w_v, w_o, gain_two
    )
    probs, chosen, total, gates = router_forward(h2, router, routes)
    full = [wide(w, 1) for w in (w_gate, w_up, w_down)]

    def expert(carry, inputs):
        mixed, dh2 = carry
        gate_weight, up_weight, down_weight, gate = inputs
        gate = gate[:, None]
        ug = jnp.dot(h2, gate_weight, preferred_element_type=f32)
        uu = jnp.dot(h2, up_weight, preferred_element_type=f32)
        dh = jnp.dot(out_grad, down_weight, preferred_element_type=f32)
        sigma = jax.nn.sigmoid(ug)
        silu = ug * sigma
        hid = silu * uu
        gate_grad = jnp.sum(hid * dh, axis=1)
        hidden_rows = (hid * gate).astype(bf16)
        dug = (dh * gate * uu * sigma * (1.0 + ug * (1.0 - sigma))).astype(bf16)
        duu = (dh * gate * silu).astype(bf16)
        mixed = mixed + contract(hidden_rows, down_weight, 1, 1)
        dh2 = dh2 + contract(dug, gate_weight, 1, 1) + contract(duu, up_weight, 1, 1)
        sums = (contract(h2, dug, 0, 0), contract(h2, duu, 0, 0))
        sums = sums + (contract(out_grad, hidden_rows, 0, 0),)
        return (mixed, dh2), (gate_grad, *(s.astype(bf16) for s in sums))

    zeros = jnp.zeros(hidden.shape, f32)
    (mixed, dh2), (gate_grads, *sums) = lax.scan(expert, (zeros, zeros), (*full, gates.T))
    hidden_out = (kept[8] + mixed).astype(bf16)
    router_sum, routed = router_backward(h2, router, probs, chosen, total, gates, gate_grads.T)
    hidden_grad, attn = attention_backward(
        hidden, kept, gain_one, w_q, w_k, w_v, w_o, gain_two, out_grad.astype(f32), routed + dh2
    )
    attn = [reduce_over_all(value, 0) for value in attn + (router_sum,)]
    grads = [reduce_over_all(value, 1) for value in sums]
    return (hidden_out, hidden_grad, *attn, *grads)


def solution(mesh):
    rows, vector, matrix = P(("rep", "shard"), None), P("shard"), P("shard", None)
    stack = P(None, "shard", None)
    in_specs = (
        rows, rows, rows, rows, vector, matrix, matrix, matrix, matrix, vector, matrix,
        stack, stack, stack,
    )
    out_specs = (
        rows, rows, vector, matrix, matrix, matrix, matrix, vector, matrix, stack, stack, stack,
    )
    fits = dict(mesh.shape) == {"rep": 16, "shard": 2}
    body = local if fits else local_any
    return jax.shard_map(body, mesh=mesh, in_specs=in_specs, out_specs=out_specs, check_vma=False)
```

```python
import functools

import jax
import jax.numpy as jnp
import numpy as np
from jax import lax
from jax.experimental import pallas as pl
from jax.experimental.pallas import tpu as pltpu
from jax.sharding import PartitionSpec as P

MODEL_WIDTH = 1536
QUERY_HEADS = 12
KEY_VALUE_HEADS = 2
HEAD_SIZE = 128
TOPK = 4
FF = 768
HALF = 768
ROWS = 512
PAD = 128
WIDE = MODEL_WIDTH + PAD
CHUNK = 96
PER = HALF // CHUNK
CHUNKS = 6 * PER

epsilon = 1e-06
rope_base = 1000000.0
MESH = pl.DeviceIdType.MESH
bf16 = jnp.bfloat16
f32 = jnp.float32


def tables(sequence_length, row_width):
    frequency = rope_base ** (-2.0 * jnp.arange(row_width // 2, dtype=jnp.float32) / row_width)
    angles = jnp.arange(sequence_length, dtype=jnp.float32)[:, None] * frequency[None, :]
    angles = jnp.concatenate([angles, angles], axis=-1)
    return (jnp.cos(angles)[:, None, :], jnp.sin(angles)[:, None, :])


def apply_rotary(values, rotary_cosine, rotary_sine):
    half_width = values.shape[-1] // 2
    turned = jnp.concatenate([-values[..., half_width:], values[..., :half_width]], axis=-1)
    return values * rotary_cosine + turned * rotary_sine


def contract(left_side, right_side, left_dim, right_dim):
    return lax.dot_general(
        left_side,
        right_side,
        (((left_dim,), (right_dim,)), ((), ())),
        preferred_element_type=jnp.float32,
    )


def normalize(values, gain_vector):
    scale_rows = lax.rsqrt(jnp.mean(values * values, axis=-1, keepdims=True) + epsilon)
    return (values * scale_rows * gain_vector, scale_rows)


def norm_back(values, scale_rows, gain_vector, upstream):
    scaled = upstream * gain_vector
    gain_grad = jnp.sum(upstream * values * scale_rows, axis=0)
    inner_sum = jnp.sum(scaled * values, axis=-1, keepdims=True)
    return (scaled * scale_rows - values * scale_rows**3 * inner_sum / values.shape[-1], gain_grad)


def softmax_rows(values):
    top_value = jnp.max(values, axis=-1, keepdims=True)
    exp_values = jnp.exp(values - top_value)
    return exp_values / jnp.sum(exp_values, axis=-1, keepdims=True)


def place():
    rep = lax.axis_index("rep")
    y = lax.axis_index("shard")
    return rep // 4, (rep // 2) % 2, rep % 2, y


def at(z, x, c, y):
    return ((z * 2 + x) * 2 + c, y)


def remote(src, dst, send, recv, device):
    return pltpu.make_async_remote_copy(
        src_ref=src,
        dst_ref=dst,
        send_sem=send,
        recv_sem=recv,
        device_id=device,
        device_id_type=MESH,
    )


def greet(partners):
    barrier = pltpu.get_barrier_semaphore()
    for device in partners:
        pl.semaphore_signal(barrier, inc=1, device_id=device, device_id_type=MESH)
    pl.semaphore_wait(barrier, len(partners))


def nt_dot(a, b):
    return lax.dot_general(a, b, (((1,), (1,)), ((), ())), preferred_element_type=f32)


def tn_dot(a, b):
    return lax.dot_general(a, b, (((0,), (0,)), ((), ())), preferred_element_type=f32)


def turn_tables(length):
    half = HEAD_SIZE // 2
    exponent = np.float32(-2.0) * np.arange(half, dtype=np.float32) / np.float32(HEAD_SIZE)
    frequency = np.float32(rope_base) ** exponent
    angles = np.arange(length, dtype=np.float32)[:, None] * frequency[None, :]
    cosine, sine = np.cos(angles), np.sin(angles)
    cosine = np.concatenate([cosine, cosine], axis=1)
    sine = np.concatenate([-sine, sine], axis=1)
    return jnp.asarray(cosine, f32), jnp.asarray(sine, f32)


def router_rows(h2, router_rows_t, routes):
    logits = nt_dot(h2, router_rows_t)
    lane = lax.broadcasted_iota(jnp.int32, logits.shape, 1)
    real = lane < 8
    logits = jnp.where(real, logits, -1e30)
    top = jnp.max(logits, axis=1, keepdims=True)
    exp_values = jnp.where(real, jnp.exp(logits - top), 0.0)
    probs = exp_values / jnp.sum(exp_values, axis=1, keepdims=True)
    chosen = lane == routes[:, 0:1]
    for k in range(1, 4):
        chosen = chosen | (lane == routes[:, k : k + 1])
    picked = jnp.where(chosen, probs, 0.0)
    total = jnp.sum(picked, axis=1, keepdims=True)
    return probs, chosen, total, picked / total


def middle_backward(returned, h2, rt, routes, y1, g, gain_two, DL, DY, DA, GS):
    GS[...] = jnp.zeros_like(GS)

    def step(b, _):
        rows = pl.ds(pl.multiple_of(b * 128, 128), 128)
        probs, chosen, total, gates = router_rows(h2(rows), rt[...], routes[rows, :])
        back = returned(rows)
        packed = back[:, MODEL_WIDTH:]
        gate_grads = jnp.where(chosen, packed + pltpu.roll(packed, PAD - 8, 1), 0.0)
        weighted = jnp.sum(gate_grads * gates, axis=1, keepdims=True)
        prob_grad = jnp.where(chosen, (gate_grads - weighted) / total, 0.0)
        inner = jnp.sum(prob_grad * probs, axis=1, keepdims=True)
        logit_grad = (probs * (prob_grad - inner)).astype(bf16)
        DL[rows, :] = logit_grad
        dh2 = back[:, :MODEL_WIDTH] + jnp.dot(logit_grad, rt[...], preferred_element_type=f32)
        v = y1[rows, :]
        r = lax.rsqrt(jnp.mean(v * v, axis=1, keepdims=True) + epsilon)
        GS[...] = GS[...] + jnp.sum(dh2 * v * r, axis=0, keepdims=True)
        scaled = dh2 * gain_two[...]
        along = jnp.sum(scaled * v, axis=1, keepdims=True)
        dy = g[rows, :].astype(f32) + (scaled * r - v * (r * r * r * along / MODEL_WIDTH))
        DY[rows, :] = dy
        DA[rows, :] = dy.astype(bf16)
        return 0

    lax.fori_loop(0, ROWS // 128, step, 0)


def heads_backward(Q, K, V, DOB, BIAS, LSE, COS, SIN, DQKV, DK, DV, tick):
    scale = HEAD_SIZE ** (-0.5)
    DK[...] = jnp.zeros_like(DK)
    DV[...] = jnp.zeros_like(DV)
    for group in range(2):
        shared = pl.ds(group * HEAD_SIZE, HEAD_SIZE)

        def head(n, _, group=group, shared=shared):
            columns = pl.ds(pl.multiple_of((group * 6 + n) * HEAD_SIZE, HEAD_SIZE), HEAD_SIZE)
            lane = lax.broadcasted_iota(jnp.int32, (ROWS, PAD), 1)
            lse = jnp.sum(
                jnp.where(lane == group * 6 + n, LSE[...], 0.0), axis=1, keepdims=True
            )
            for block in range(2):
                rows, keys = pl.ds(block * 256, 256), pl.ds(0, 256 * (block + 1))
                q, dob = Q[rows, columns], DOB[rows, columns]
                k, v = K[keys, shared], V[keys, shared]
                logits = nt_dot(q, k) * scale + BIAS[rows, keys]
                p = jnp.exp(logits - lse[block * 256 : block * 256 + 256])
                dp = nt_dot(dob, v)
                inner = jnp.sum(dp * p, axis=1, keepdims=True)
                ds = (p * (dp - inner)).astype(bf16)
                dq = jnp.dot(ds, k, preferred_element_type=f32) * scale
                dq = dq * COS[rows, :] - pltpu.roll(dq, 64, 1) * SIN[rows, :]
                DQKV[rows, columns] = dq.astype(bf16)
                DK[group, keys, :] = DK[group, keys, :] + tn_dot(ds, q)
                DV[group, keys, :] = DV[group, keys, :] + tn_dot(p.astype(bf16), dob)
            return 0

        for n in range(0, 6, 3):
            lax.fori_loop(n, n + 3, head, 0)
            tick(group * 6 + n + 3)
        dk = DK[group] * scale
        dk = dk * COS[...] - pltpu.roll(dk, 64, 1) * SIN[...]
        DQKV[:, pl.ds(1536 + group * HEAD_SIZE, HEAD_SIZE)] = dk.astype(bf16)
        DQKV[:, pl.ds(1792 + group * HEAD_SIZE, HEAD_SIZE)] = DV[group].astype(bf16)


def first_backward(DH1, X, DY, gain_one, HG, GS):
    GS[...] = jnp.zeros_like(GS)

    def step(b, _):
        rows = pl.ds(pl.multiple_of(b * 128, 128), 128)
        v, up = X[rows, :].astype(f32), DH1[rows, :]
        r = lax.rsqrt(jnp.mean(v * v, axis=1, keepdims=True) + epsilon)
        GS[...] = GS[...] + jnp.sum(up * v * r, axis=0, keepdims=True)
        scaled = up * gain_one[...]
        along = jnp.sum(scaled * v, axis=1, keepdims=True)
        back = scaled * r - v * (r * r * r * along / MODEL_WIDTH)
        HG[rows, :] = (DY[rows, :] + back).astype(bf16)
        return 0

    lax.fori_loop(0, ROWS // 128, step, 0)


def mask_bias(seg_row, BIAS):
    row = lax.broadcasted_iota(jnp.int32, (ROWS, ROWS), 0)
    column = lax.broadcasted_iota(jnp.int32, (ROWS, ROWS), 1)
    ids = seg_row[0:1, :].astype(f32)
    same = jnp.transpose(jnp.broadcast_to(ids, (PAD, ROWS)))[:, 0:1] == ids
    BIAS[...] = jnp.where((column <= row) & same, 0.0, -1e30)


BLOCKS = 7
PARTS = 2 * BLOCKS
WIDTH = 512
QUARTER = 96
SLACK = 3
AT_ZL, AT_FL, AT_X = 1 + SLACK, 2 + 2 * SLACK, 3 + 3 * SLACK
AT_CX, AT_CZ = AT_X + 8, AT_X + 12
EXPERT_SLOTS = CHUNKS + AT_CZ + 1
PART_SLOTS = PARTS + 18


def layer_kernel(
    xin, g, wq, wk, wv, wo, sm, wg, wu, wd, cos, sin, routes, segr,
    hout, out, aout, smo, hgrad,
    o_own, o_core, o_x, y1, h1, q, k, v, ob, lse, wqo, wko, wvo, woo, smf, gl,
    r_core, r_x, gr, ya, za, zb, d, ca, yb, xb, zc, zd, sa,
    H, W, DG, CR, CO, VA, VB, VS, VZ, VT, VF, FN, SM, SB, RT, G1, G2,
    fl_s, wa_s, wa_r, wx_s, wx_r, wc_s, wc_r, wd_s, wd_r, wz_s, wz_r, hx_s, hx_r, hc_s, hc_r,
    hd_s, hd_r, own_s, st_s,
    loc, stg_sem, y_s, y_r, ld_a, ld_b,
    z1_s, z1_r, ld_z, z2_s, z2_r, ld_f, z3_s, z3_r, fo, x_s, x_r, c1_s, c1_r, c2_s, c2_r,
    z4_s, z4_r, rc_s, rc_r, rx_s, rx_r, rd_s, rd_r, ro,
    ac_s, ac_r, ald, ay_s, ay_r, aldy, ax_s, ax_r, aldx, az1_s, az1_r, aldz, az2_s, az2_r, aldf,
    az3_s, az3_r, afo, axg_s, axg_r, ac1_s, ac1_r, ac2_s, ac2_r, s_s, s_r, sl, att,
):
    z, x, c, y = place()
    mid = (z == 1) | (z == 2)
    end = jnp.logical_not(mid)
    ydev, xdev, cdev = at(z, x, c, 1 - y), at(z, 1 - x, c, y), at(z, x, 1 - c, y)
    zdev = at(z + 1 - 2 * (z % 2), x, c, y)
    mdev = at(3 - z, x, c, y)
    greet((ydev, xdev, cdev, zdev, mdev))
    shards = (wg, wu, wd)
    e0 = 2 * (2 * x + c)
    other = 2 * (2 * (1 - x) + c)
    h = z % 2
    local_copy = pltpu.make_async_copy
    vm = pltpu.VMEM
    part = lambda *shape: vm(shape, bf16)

    piece = HALF // 4
    own_piece, x_piece = (2 * x + c) * piece, (2 * (1 - x) + c) * piece
    kinds = [(wk, wko, 0, piece), (wv, wvo, 0, piece)]
    kinds += [(wq, wqo, n * 64, 64) for n in range(3)] + [(wo, woo, n * 64, 64) for n in range(3)]

    def copies(from_input, begin, send, receive, device):
        made = []
        for n, (whole, landed, shift, count) in enumerate(kinds):
            rows = pl.ds(pl.multiple_of(begin + shift, 64), count)
            src = whole if from_input else landed
            made.append(remote(src.at[rows], landed.at[rows], send.at[n], receive.at[n], device))
        return made

    wa = copies(True, own_piece, wa_s, wa_r, ydev)
    wa.append(remote(sm, smf, wa_s.at[8], wa_r.at[8], ydev))
    wx = copies(False, own_piece, wx_s, wx_r, xdev)
    wc = copies(False, own_piece, wc_s, wc_r, cdev)
    wt = copies(False, x_piece, wd_s, wd_r, cdev)
    gx = remote(g, gl.at[1], wx_s.at[8], wx_r.at[8], xdev)
    gc = remote(g, gl.at[0], wc_s.at[8], wc_r.at[8], cdev)
    gt = remote(gl.at[1], gl.at[2], wd_s.at[8], wd_r.at[8], cdev)

    def wy(n):
        j, m = n // 3, n % 3
        return remote(
            shards[m].at[e0 + j, pl.ds(h * 384, 384)],
            W.at[j, m, pl.ds(y * HALF + h * 384, 384)],
            wa_s.at[9 + n],
            wa_r.at[9 + n],
            ydev,
        )

    def wz(n):
        rows = pl.ds((1 - y) * HALF + h * 384, 384)
        ref = W.at[n // 3, n % 3, rows]
        return remote(ref, ref, wz_s.at[n], wz_r.at[n], zdev)

    def own_half(n):
        j, m = n // 3, n % 3
        return local_copy(shards[m].at[e0 + j], W.at[j, m, pl.ds(y * HALF, HALF)], own_s.at[n])

    def pass_on(n):
        wy(n).wait_recv()
        wz(n).start()

    def hx(b):
        src = H.at[pl.ds(b * 256, 256)]
        return remote(src, H.at[pl.ds(2 * ROWS + b * 256, 256)], hx_s.at[b], hx_r.at[b], xdev)

    def hc(b):
        src = H.at[pl.ds(b * 256, 256)]
        return remote(src, H.at[pl.ds(ROWS + b * 256, 256)], hc_s.at[b], hc_r.at[b], cdev)

    def hd(b):
        src = H.at[pl.ds(2 * ROWS + b * 256, 256)]
        return remote(src, H.at[pl.ds(3 * ROWS + b * 256, 256)], hd_s.at[b], hd_r.at[b], cdev)

    wa[8].start()
    for n in range(8):
        wa[n].start()
    gc.start()
    for n in range(6):
        wy(n).start()

    def front(X, H1, WQ, WKV, WO, Q, K, V, OB, BIAS, LSE, COS, SIN, RO, SR, SF, Y1):
        there = pl.ds(y * HALF, HALF)
        away = pl.ds((1 - y) * HALF, HALF)
        left, right = pl.ds(0, 256), pl.ds(256, 256)
        pairs = [
            (xin, X), (sm, SF.at[y]), (wk, WKV.at[there, left]), (wv, WKV.at[there, right]),
            (wq, WQ.at[there]), (wo, WO.at[there]), (cos, COS), (sin, SIN), (routes, RO),
            (segr, SR),
        ]
        loads = [local_copy(p[0], p[1], fl_s.at[n]) for n, p in enumerate(pairs)]
        for copy in loads:
            copy.start()
        for n in range(6):
            own_half(n).start()
        late = [
            local_copy(wko, WKV.at[away, left], fl_s.at[11]),
            local_copy(wvo, WKV.at[away, right], fl_s.at[12]),
            local_copy(wqo, WQ.at[away], fl_s.at[13]),
            local_copy(woo, WO.at[away], fl_s.at[14]),
            local_copy(smf, SF.at[1 - y], fl_s.at[15]),
        ]
        wa[8].wait_recv()
        late[4].start()
        for n in (0, 1):
            loads[n].wait()
        late[4].wait()
        row = lax.broadcasted_iota(jnp.int32, (16, HALF), 0)
        RT[...] = jnp.zeros_like(RT)
        for half in range(2):
            columns = pl.ds(half * HALF, HALF)
            small = SF[half].astype(f32)
            RT[0:16, columns] = jnp.where(row < 8, small, 0.0).astype(bf16)
            G1[:, columns] = jnp.sum(jnp.where(row == 8, small, 0.0), axis=0, keepdims=True)
            G2[:, columns] = jnp.sum(jnp.where(row == 9, small, 0.0), axis=0, keepdims=True)

        def norm_step(b, _):
            rows = pl.ds(pl.multiple_of(b * 128, 128), 128)
            value = X[rows, :].astype(f32)
            r = lax.rsqrt(jnp.mean(value * value, axis=1, keepdims=True) + epsilon)
            H1[rows, :] = (value * r * G1[...]).astype(bf16)
            return 0

        lax.fori_loop(0, ROWS // 128, norm_step, 0)
        for n in range(2, 10):
            loads[n].wait()
        mask_bias(SR, BIAS)
        def onward(n):
            wa[n].wait_recv()
            wx[n].start()
            wc[n].start()

        def across(n):
            wx[n].wait_recv()
            wt[n].start()

        for n in range(3):
            onward(n)
        for n in range(3):
            across(n)
            onward(n + 3)
        for n in (3, 4):
            across(n)
            onward(n + 3)
        gx.start()
        for n in range(5):
            wc[n].wait_recv()
            wt[n].wait_recv()
        for n in range(3):
            late[n].start()
        for n in range(3):
            late[n].wait()

        def rotate(u):
            return u * COS[...] + pltpu.roll(u, 64, 1) * SIN[...]

        def query_step(t, _):
            begin = pl.multiple_of(t * 512, 512)
            tile = jnp.dot(H1[...], WQ[:, pl.ds(begin, 512)], preferred_element_type=f32)
            for n in range(4):
                u = tile[:, n * HEAD_SIZE : (n + 1) * HEAD_SIZE]
                Q[:, pl.ds(begin + n * HEAD_SIZE, HEAD_SIZE)] = rotate(u).astype(bf16)
            return 0

        tile = jnp.dot(H1[...], WKV[...], preferred_element_type=f32)
        for n in range(2):
            columns = pl.ds(n * HEAD_SIZE, HEAD_SIZE)
            u = tile[:, n * HEAD_SIZE : (n + 1) * HEAD_SIZE]
            K[:, columns] = rotate(u).astype(bf16)
        V[...] = tile[:, 256:].astype(bf16)
        lax.fori_loop(0, 3, query_step, 0)
        for n in (5, 6, 7):
            across(n)
        pass_on(0)
        LSE[...] = jnp.zeros_like(LSE)
        scale = HEAD_SIZE ** (-0.5)
        for b in range(2):
            rows, keys = pl.ds(b * 256, 256), pl.ds(0, 256 * (b + 1))

            def head(n, _, rows=rows, keys=keys):
                columns = pl.ds(pl.multiple_of(n * HEAD_SIZE, HEAD_SIZE), HEAD_SIZE)
                shared = pl.ds(pl.multiple_of(n // 6 * HEAD_SIZE, HEAD_SIZE), HEAD_SIZE)
                logits = nt_dot(Q[rows, columns], K[keys, shared]) * scale + BIAS[rows, keys]
                top = jnp.max(logits, axis=1, keepdims=True)
                p = jnp.exp(logits - top)
                total = jnp.sum(p, axis=1, keepdims=True)
                lane = lax.broadcasted_iota(jnp.int32, (256, PAD), 1)
                LSE[rows, :] = jnp.where(lane == n, top + jnp.log(total), LSE[rows, :])
                p = (p * (1.0 / total)).astype(bf16)
                mixed = jnp.dot(p, V[keys, shared], preferred_element_type=f32)
                OB[rows, columns] = mixed.astype(bf16)
                return 0

            lax.fori_loop(0, QUERY_HEADS, head, 0)
            if b == 0:
                for n in (5, 6, 7):
                    wc[n].wait_recv()
                    wt[n].wait_recv()
                late[3].start()
                pass_on(1)
                late[3].wait()
            for t in range(3):
                ns = pl.ds(t * 512, 512)
                Y1[rows, ns] = X[rows, ns].astype(f32) + jnp.dot(
                    OB[rows, :], WO[:, ns], preferred_element_type=f32
                )
            for n in range(2):
                block = pl.ds(b * 256 + n * 128, 128)
                value = Y1[block, :]
                r = lax.rsqrt(jnp.mean(value * value, axis=1, keepdims=True) + epsilon)
                h2 = (value * r * G2[...]).astype(bf16)
                H[block, :MODEL_WIDTH] = h2
                gates = router_rows(h2, RT[...], RO[block, :])[3]
                high = gates.astype(bf16).astype(f32)
                H[block, MODEL_WIDTH:] = (high + pltpu.roll(gates - high, 8, 1)).astype(bf16)
            hx(b).start()
            hc(b).start()
        stores = [
            local_copy(p[0], p[1], st_s.at[n])
            for n, p in enumerate(
                ((Y1, y1), (H1, h1), (Q, q), (K, k), (V, v), (OB, ob), (LSE, lse))
            )
        ]
        for copy in stores:
            copy.start()
        pass_on(2)
        for copy in stores:
            copy.wait()

    pl.run_scoped(
        front,
        part(ROWS, MODEL_WIDTH), part(ROWS, MODEL_WIDTH), part(MODEL_WIDTH, MODEL_WIDTH),
        part(MODEL_WIDTH, 512), part(MODEL_WIDTH, MODEL_WIDTH), part(ROWS, MODEL_WIDTH),
        part(ROWS, 256), part(ROWS, 256), part(ROWS, MODEL_WIDTH), vm((ROWS, ROWS), f32),
        vm((ROWS, PAD), f32), vm((ROWS, PAD), f32), vm((ROWS, PAD), f32),
        vm((ROWS, TOPK), jnp.int32), vm((1, ROWS), jnp.int32),
        part(2, 16, HALF), vm((ROWS, MODEL_WIDTH), f32),
    )

    def parts_of(n):
        return n // (3 * PER), (n // PER) % 3, n % PER

    def y_copy(n):
        j, m, i = parts_of(n)
        src = gr.at[j, m, pl.ds((1 - y) * HALF + i * CHUNK, CHUNK)]
        return remote(src, ya.at[n], y_s.at[n], y_r.at[n], ydev)

    def spot(n, expert):
        j, m, i = parts_of(n)
        return out.at[m, expert + j, pl.ds(i * CHUNK, CHUNK)]

    def load_a(n):
        j, m, i = parts_of(n)
        src = gr.at[j, m, pl.ds(y * HALF + i * CHUNK, CHUNK)]
        return local_copy(src, VA.at[n % 2], ld_a.at[n % 2])

    def load_b(n):
        return local_copy(ya.at[n], VB.at[n % 2], ld_b.at[n % 2])

    def load_z(n):
        return local_copy(za.at[n], VZ.at[n % 2], ld_z.at[n % 2])

    def load_f(n):
        return local_copy(zb.at[n], VF.at[n % 2], ld_f.at[n % 2])

    def z1_copy(n):
        return remote(VS.at[n % 4], za.at[n], z1_s.at[n], z1_r.at[n], zdev)

    def z2_copy(n):
        return remote(VT.at[n % 4], zb.at[n], z2_s.at[n], z2_r.at[n], mdev)

    def z3_copy(n):
        return remote(FN.at[n % 4], spot(n, e0), z3_s.at[n], z3_r.at[n], zdev)

    def z4_copy(n):
        return remote(spot(n, other), spot(n, other), z4_s.at[n], z4_r.at[n], zdev)

    def store_f(n):
        return local_copy(FN.at[n % 4], spot(n, e0), fo.at[n % 4])

    def x_copy(n):
        return remote(spot(n, e0), spot(n, e0), x_s.at[n], x_r.at[n], xdev)

    def c1_copy(n):
        return remote(spot(n, e0), spot(n, e0), c1_s.at[n], c1_r.at[n], cdev)

    def c2_copy(n):
        return remote(spot(n, other), spot(n, other), c2_s.at[n], c2_r.at[n], cdev)

    def handed(n):
        return n % 2 == 1

    def crosses(n):
        return (n % 2 == 0) | ((n % 4 == 1) & mid) | ((n % 4 == 3) & end)

    def when(n, cond=None):
        ok = (n >= 0) & (n < CHUNKS)
        return pl.when(ok if cond is None else ok & cond)

    def slot(s):
        n = s - AT_CZ

        @when(n, jnp.logical_not(crosses(n + 4 * CHUNKS)))
        def _(n=n):
            z4_copy(n).wait_recv()
            c2_copy(n).start()

        n = s - AT_CX
        crossed = crosses(n + 4 * CHUNKS)

        @when(n, crossed)
        def _(n=n):
            x_copy(n).wait_recv()
            c2_copy(n).start()

        @when(n, crossed & handed(n + 4 * CHUNKS))
        def _(n=n):
            z4_copy(n).start()

        n = s - AT_X

        @when(n, mid)
        def _(n=n):
            store_f(n).wait()
            z3_copy(n).wait_send()

        @when(n, end)
        def _(n=n):
            z3_copy(n).wait_recv()

        @when(n, crosses(n + 4 * CHUNKS))
        def _(n=n):
            x_copy(n).start()

        @when(n)
        def _(n=n):
            c1_copy(n).start()

        n = s - AT_FL - 1

        @when(n, mid)
        def _(n=n):
            load_f(n).wait()
            z2_copy(n).wait_send()
            FN[n % 4] = VT[n % 4] + VF[n % 2]
            z3_copy(n).start()
            store_f(n).start()

        n = s - AT_FL

        @when(n, mid)
        def _(n=n):
            z2_copy(n).wait_recv()
            load_f(n).start()

        n = s - AT_ZL - 1

        @when(n, mid)
        def _(n=n):
            load_z(n).wait()
            VT[n % 4] = VS[n % 4] + VZ[n % 2]
            z2_copy(n).start()

        n = s - AT_ZL

        @when(n, mid)
        def _(n=n):
            z1_copy(n).wait_recv()
            load_z(n).start()

        n = s - 5

        @when(n, end)
        def _(n=n):
            z1_copy(n).wait_send()

        n = s - 1

        @when(n)
        def _(n=n):
            load_a(n).wait()
            load_b(n).wait()
            VS[n % 4] = VA[n % 2] + VB[n % 2]

        @when(n, end)
        def _(n=n):
            z1_copy(n).start()

        @when(s)
        def _():
            y_copy(s).wait_recv()
            load_a(s).start()
            load_b(s).start()

    def slots(first, last):
        def step(s, _):
            slot(s)
            return 0

        lax.fori_loop(first, last, step, 0)

    third, second = pl.ds(3 * ROWS, ROWS), pl.ds(2 * ROWS, ROWS)
    first, zeroth = pl.ds(ROWS, ROWS), pl.ds(0, ROWS)

    def experts(G, ACT, STG, RS, OS):
        gain_rows = [
            local_copy(src, G.at[pl.ds(n * ROWS, ROWS)], loc.at[n])
            for n, src in enumerate((g, gl.at[0], gl.at[1], gl.at[2]))
        ]
        gain_rows[0].start()
        gc.wait_recv()
        gain_rows[1].start()

        def gate_of(j, rows):
            lane = lax.broadcasted_iota(jnp.int32, (2 * ROWS, PAD), 1)
            packed = H[rows, MODEL_WIDTH:].astype(f32)
            picked = (lane == e0 + j) | (lane == e0 + j + 8)
            return jnp.sum(jnp.where(picked, packed, 0.0), axis=1, keepdims=True), lane

        def forward(j, begin, base=None):
            rows = pl.ds(begin, 2 * ROWS)
            gate, lane = gate_of(j, rows)

            def step(t, total):
                columns = pl.ds(pl.multiple_of(t * 256, 256), 256)
                ug = jnp.dot(
                    H[rows, :MODEL_WIDTH], W[j, 0, :, columns], preferred_element_type=f32
                )
                uu = jnp.dot(
                    H[rows, :MODEL_WIDTH], W[j, 1, :, columns], preferred_element_type=f32
                )
                dh = jnp.dot(G[rows, :], W[j, 2, :, columns], preferred_element_type=f32)
                sigma = jax.nn.sigmoid(ug)
                silu = ug * sigma
                hid = silu * uu
                ACT[j, 0, rows, columns] = (hid * gate).astype(bf16)
                dhg = dh * gate
                ACT[j, 1, rows, columns] = (
                    dhg * uu * sigma * (1.0 + ug * (1.0 - sigma))
                ).astype(bf16)
                ACT[j, 2, rows, columns] = (dhg * silu).astype(bf16)
                if base is not None:
                    slot(base + t)
                return total + jnp.sum(hid * dh, axis=1, keepdims=True)

            total = lax.fori_loop(0, FF // 256, step, jnp.zeros((2 * ROWS, 1), f32))
            high = total.astype(bf16).astype(f32)
            low = total - high
            here = jnp.where(lane == e0 + j, high, jnp.where(lane == e0 + j + 8, low, 0.0))
            if j == 0:
                DG[rows, :] = here.astype(bf16)
            else:
                DG[rows, :] = (DG[rows, :].astype(f32) + here).astype(bf16)

        def back_rows(rows, ns):
            o = nt_dot(ACT[0, 0, rows, :], W[0, 2, ns, :])
            o = o + nt_dot(ACT[1, 0, rows, :], W[1, 2, ns, :])
            e = nt_dot(ACT[0, 1, rows, :], W[0, 0, ns, :])
            e = e + nt_dot(ACT[0, 2, rows, :], W[0, 1, ns, :])
            e = e + nt_dot(ACT[1, 1, rows, :], W[1, 0, ns, :])
            e = e + nt_dot(ACT[1, 2, rows, :], W[1, 1, ns, :])
            return o, e

        def store_tile(j, m, half, i, place_in):
            rows = pl.ds(half * HALF + i * 384, 384)
            return local_copy(STG.at[place_in], gr.at[j, m, rows], stg_sem.at[place_in])

        def weight_tile(j, m, left, half, i, place_in):
            begin = half * HALF + i * 384
            lhs = left[:, pl.ds(pl.multiple_of(begin, 128), 384)]
            STG[place_in] = tn_dot(lhs, ACT[j, (m + 1) % 3]).astype(bf16)
            copy = store_tile(j, m, half, i, place_in)
            copy.start()
            return copy

        def weight_grads(j, base=None):
            done = 0
            for left, m0, steps in ((H, 0, 4), (G, 2, 2)):

                def step(n, _, left=left, m0=m0, done=done):
                    m, i = m0 + n // 2, n % 2
                    away = weight_tile(j, m, left, 1 - y, i, 0)

                    @pl.when(n + done > 0)
                    def _():
                        store_tile(j, m, y, i, 1).wait()

                    weight_tile(j, m, left, y, i, 1)
                    away.wait()
                    begin = (j * 3 + m) * PER + i * (384 // CHUNK)
                    for p in range(384 // CHUNK):
                        y_copy(begin + p).start()
                    if base is not None:
                        slot(base + done + n)
                    return 0

                lax.fori_loop(0, steps, step, 0)
                done += steps
            store_tile(j, 2, y, 1, 1).wait()

        def rc_copy(t, which):
            ns = pl.ds(pl.multiple_of(t * 512, 512), 512)
            src, dst = ((RS, CR), (OS, CO))[which]
            return remote(
                src.at[t % 2], dst.at[:, ns], rc_s.at[which, t], rc_r.at[which, t], cdev
            )

        def rb_copy(t, which):
            ns = pl.ds(pl.multiple_of(t * 512, 512), 512)
            src, dst = ((RS, r_core), (OS, o_core))[which]
            return remote(
                src.at[t % 2], dst.at[:, ns], rd_s.at[1 + which * 3 + t],
                rd_r.at[1 + which * 3 + t], cdev,
            )

        def ro_copy(t):
            ns = pl.ds(pl.multiple_of(t * 512, 512), 512)
            return local_copy(OS.at[t % 2], o_own.at[:, ns], ro.at[t])

        for n in range(3):
            wz(n).wait_recv()
            own_half(n).wait()
        gain_rows[0].wait()
        gain_rows[1].wait()
        for b in range(2):
            hc(b).wait_recv()
        pass_on(3)
        forward(0, 0)
        gx.wait_recv()
        gt.start()
        gain_rows[2].start()
        pass_on(4)
        for b in range(2):
            hx(b).wait_recv()
            hd(b).start()
        gt.wait_recv()
        gain_rows[3].start()
        for b in range(2):
            hd(b).wait_recv()
        gain_rows[2].wait()
        gain_rows[3].wait()
        forward(0, 2 * ROWS)
        pass_on(5)
        weight_grads(0)
        for n in range(3, 6):
            wz(n).wait_recv()
            own_half(n).wait()
        forward(1, 2 * ROWS, 0)

        def third_step(t, _):
            ns = pl.ds(pl.multiple_of(t * 512, 512), 512)

            @pl.when(t == 2)
            def _():
                rc_copy(0, 0).wait_send()
                rc_copy(0, 1).wait_send()

            o, e = back_rows(third, ns)
            RS[t % 2] = e.astype(bf16)
            OS[t % 2] = o.astype(bf16)
            rc_copy(t, 0).start()
            rc_copy(t, 1).start()
            slot(3 + t)
            return 0

        lax.fori_loop(0, 3, third_step, 0)
        dg_copy = remote(
            DG.at[third], CR.at[:, pl.ds(MODEL_WIDTH, PAD)], rd_s.at[0], rd_r.at[0], cdev
        )
        dg_copy.start()

        def second_step(t, _):
            ns = pl.ds(pl.multiple_of(t * 512, 512), 512)
            o, e = back_rows(second, ns)
            rc_copy(t, 0).wait_recv()
            rc_copy(t, 1).wait_recv()
            CR[:, ns] = (CR[:, ns].astype(f32) + e).astype(bf16)
            CO[:, ns] = (CO[:, ns].astype(f32) + o).astype(bf16)
            slot(6 + t)
            return 0

        lax.fori_loop(0, 3, second_step, 0)
        dg_copy.wait_recv()
        CR[:, MODEL_WIDTH:] = CR[:, MODEL_WIDTH:] + DG[second, :]
        rx.start()
        forward(1, 0, 9)
        weight_grads(1, 12)
        for which in range(2):
            for t in (1, 2):
                rc_copy(t, which).wait_send()
        dg_copy.wait_send()
        tail_b.start()

        def first_step(t, _):
            ns = pl.ds(pl.multiple_of(t * 512, 512), 512)

            @pl.when(t == 2)
            def _():
                rb_copy(0, 0).wait_send()
                rb_copy(0, 1).wait_send()

            o, e = back_rows(first, ns)
            RS[t % 2] = e.astype(bf16)
            OS[t % 2] = o.astype(bf16)
            rb_copy(t, 0).start()
            rb_copy(t, 1).start()
            slot(18 + t)
            return 0

        lax.fori_loop(0, 3, first_step, 0)
        for t in (1, 2):
            rb_copy(t, 0).wait_send()
            rb_copy(t, 1).wait_send()

        def zeroth_step(t, _):
            ns = pl.ds(pl.multiple_of(t * 512, 512), 512)
            o, e = back_rows(zeroth, ns)

            @pl.when(t == 2)
            def _():
                ro_copy(0).wait()

            H[first, ns] = e.astype(bf16)
            OS[t % 2] = o.astype(bf16)
            ro_copy(t).start()
            slot(21 + t)
            return 0

        lax.fori_loop(0, 3, zeroth_step, 0)
        H[first, MODEL_WIDTH:] = DG[zeroth, :]
        for t in range(3):
            rb_copy(t, 0).wait_recv()
            rb_copy(t, 1).wait_recv()
        for t in (1, 2):
            ro_copy(t).wait()
        for n in range(6):
            wy(n).wait_send()
            wz(n).wait_send()
        for n in range(8):
            wa[n].wait_send()
            wx[n].wait_send()
            wc[n].wait_send()
            wt[n].wait_send()
        wa[8].wait_send()
        for copy in (gx, gc, gt):
            copy.wait_send()
        for b in range(2):
            hx(b).wait_send()
            hc(b).wait_send()
            hd(b).wait_send()
        rx.wait_send()

    rx = remote(CR, r_x, rx_s.at[0], rx_r.at[0], xdev)
    ox = remote(CO, o_x, rx_s.at[1], rx_r.at[1], xdev)
    tail_b = remote(
        DG.at[first], r_core.at[:, pl.ds(MODEL_WIDTH, PAD)], rd_s.at[7], rd_r.at[7], cdev
    )
    pl.run_scoped(
        experts,
        vm((4 * ROWS, MODEL_WIDTH), bf16),
        vm((2, 3, 4 * ROWS, FF), bf16),
        vm((2, 384, FF), bf16),
        vm((2, ROWS, 512), bf16),
        vm((2, ROWS, 512), bf16),
    )
    ox.start()
    tail_b.wait()

    def attention(
        Y1, DY, GB, XB, H1, OB, QB, KB, VV, DA, DOB, DQKV, BIAS, LSE, COS, SIN, RO,
        SR, DL, GS, DK, DV, STG,
        AA, AB, PP, VY, QQ, VX, AS, AZ, AT, AF, AN,
    ):
        pairs = [
            (segr, SR), (y1, Y1), (g, GB), (routes, RO), (r_core, H.at[second]),
            (ob, OB), (q, QB), (k, KB), (v, VV), (lse, LSE), (cos, COS), (sin, SIN), (h1, H1),
            (xin, XB),
        ]
        for n, ws in ((1, (wo, woo)), (0, (wq, wqo))):
            for w, rows in zip(ws, (pl.ds(y * HALF, HALF), pl.ds((1 - y) * HALF, HALF))):
                for side in range(2):
                    pairs.append((w.at[:, pl.ds(side * HALF, HALF)], W.at[n, side, rows]))
        for ws, columns in (((wk, wko), pl.ds(0, 256)), ((wv, wvo), pl.ds(256, 256))):
            for w, rows in zip(ws, (pl.ds(y * HALF, HALF), pl.ds((1 - y) * HALF, HALF))):
                pairs.append((w, W.at[0, 2, rows, columns]))
        loads = [local_copy(p[0], p[1], att.at[n]) for n, p in enumerate(pairs)]
        for copy in loads:
            copy.start()

        def need(first, last):
            for copy in loads[first:last]:
                copy.wait()

        slots(24, 26)
        need(0, 1)
        mask_bias(SR, BIAS)
        slots(26, 28)
        need(1, 5)
        rx.wait_recv()
        last = local_copy(r_x, H.at[third], att.at[len(pairs)])
        last.start()
        last.wait()

        def rows_of(n):
            q_, i = n // 2, n % 2
            return q_, i * 384

        def ac_copy(n):
            b, begin = rows_of(n)
            src = d.at[b, :, pl.ds(begin + (1 - c) * 192, 192)]
            return remote(src, ca.at[n], ac_s.at[n], ac_r.at[n], cdev)

        def aload_a(n):
            b, begin = rows_of(n)
            return local_copy(d.at[b, :, pl.ds(begin + c * 192, 192)], AA.at[n % 2], ald.at[0, n % 2])

        def aload_b(n):
            return local_copy(ca.at[n], AB.at[n % 2], ald.at[1, n % 2])

        def ay_copy(n):
            return remote(PP.at[n % 4, 1 - y], yb.at[n], ay_s.at[n], ay_r.at[n], ydev)

        def aload_y(n):
            return local_copy(yb.at[n], VY.at[n % 2], aldy.at[n % 2])

        def ax_copy(n):
            src = QQ.at[n % 4, pl.ds((1 - x) * QUARTER, QUARTER)]
            return remote(src, xb.at[n], ax_s.at[n], ax_r.at[n], xdev)

        def aload_x(n):
            return local_copy(xb.at[n], VX.at[n % 2], aldx.at[n % 2])

        def az1_copy(n):
            return remote(AS.at[n % 8], zc.at[n], az1_s.at[n], az1_r.at[n], zdev)

        def aload_z(n):
            return local_copy(zc.at[n], AZ.at[n % 2], aldz.at[n % 2])

        def az2_copy(n):
            return remote(AT.at[n % 4], zd.at[n], az2_s.at[n], az2_r.at[n], mdev)

        def aload_f(n):
            return local_copy(zd.at[n], AF.at[n % 2], aldf.at[n % 2])

        def aspot(n, xx, cc):
            b, begin = rows_of(n)
            columns = pl.ds(pl.multiple_of(b * WIDTH, WIDTH), WIDTH)
            return aout.at[pl.ds(begin + cc * 192 + xx * QUARTER, QUARTER), columns]

        def az3_copy(n):
            return remote(AN.at[n % 4], aspot(n, x, c), az3_s.at[n], az3_r.at[n], zdev)

        def astore(n):
            return local_copy(AN.at[n % 4], aspot(n, x, c), afo.at[n % 4])

        def axg_copy(n):
            return remote(aspot(n, x, c), aspot(n, x, c), axg_s.at[n], axg_r.at[n], xdev)

        def ac1_copy(n):
            return remote(aspot(n, x, c), aspot(n, x, c), ac1_s.at[n], ac1_r.at[n], cdev)

        def ac2_copy(n):
            return remote(aspot(n, 1 - x, c), aspot(n, 1 - x, c), ac2_s.at[n], ac2_r.at[n], cdev)

        def awhen(n, cond=None):
            ok = (n >= 0) & (n < PARTS)
            return pl.when(ok if cond is None else ok & cond)

        def aslot(s):
            @awhen(s - 17)
            def _():
                axg_copy(s - 17).wait_recv()
                ac2_copy(s - 17).start()

            @awhen(s - 15, mid)
            def _():
                astore(s - 15).wait()
                az3_copy(s - 15).wait_send()

            @awhen(s - 15, end)
            def _():
                az3_copy(s - 15).wait_recv()

            @awhen(s - 15)
            def _():
                axg_copy(s - 15).start()
                ac1_copy(s - 15).start()

            @awhen(s - 13, mid)
            def _():
                n = s - 13
                aload_f(n).wait()
                az2_copy(n).wait_send()
                AN[n % 4] = AT[n % 4] + AF[n % 2]
                az3_copy(n).start()
                astore(n).start()

            @awhen(s - 12, mid)
            def _():
                az2_copy(s - 12).wait_recv()
                aload_f(s - 12).start()

            @awhen(s - 10, mid)
            def _():
                n = s - 10
                aload_z(n).wait()
                AT[n % 4] = AS[n % 8] + AZ[n % 2]
                az2_copy(n).start()

            @awhen(s - 10, end)
            def _():
                az1_copy(s - 10).wait_send()

            @awhen(s - 9, mid)
            def _():
                az1_copy(s - 9).wait_recv()
                aload_z(s - 9).start()

            @awhen(s - 7)
            def _():
                n = s - 7
                aload_x(n).wait()
                ax_copy(n).wait_send()
                mine = pl.ds(pl.multiple_of(x * QUARTER, 16), QUARTER)
                AS[n % 8] = QQ[n % 4, mine, :] + VX[n % 2]

            @awhen(s - 7, end)
            def _():
                az1_copy(s - 7).start()

            @awhen(s - 6)
            def _():
                ax_copy(s - 6).wait_recv()
                aload_x(s - 6).start()

            @awhen(s - 4)
            def _():
                n = s - 4
                aload_y(n).wait()
                ay_copy(n).wait_send()
                QQ[n % 4] = PP[n % 4, y] + VY[n % 2]
                ax_copy(n).start()

            @awhen(s - 3)
            def _():
                ay_copy(s - 3).wait_recv()
                aload_y(s - 3).start()

            @awhen(s - 1)
            def _():
                n = s - 1
                aload_a(n).wait()
                aload_b(n).wait()
                PP[n % 4] = AA[n % 2] + AB[n % 2]
                ay_copy(n).start()

            @awhen(s)
            def _():
                ac_copy(s).wait_recv()
                aload_a(s).start()
                aload_b(s).start()

        def emit(b, left, right):
            copies = []
            for half in range(2):
                STG[half] = tn_dot(left[:, pl.ds(half * HALF, HALF)], right).astype(bf16)
                copies.append(local_copy(STG.at[half], d.at[b, half], stg_sem.at[half]))
                copies[half].start()
            for copy in copies:
                copy.wait()
            ac_copy(2 * b).start()
            ac_copy(2 * b + 1).start()

        def returned(rows):
            begin = rows.start
            one = H[pl.ds(pl.multiple_of(begin + ROWS, 128), 128), :].astype(f32)
            two = H[pl.ds(pl.multiple_of(begin + 2 * ROWS, 128), 128), :].astype(f32)
            three = H[pl.ds(pl.multiple_of(begin + 3 * ROWS, 128), 128), :].astype(f32)
            return one + two + three

        middle_backward(
            returned, lambda rows: H[rows, :MODEL_WIDTH], RT, RO, Y1, GB, G2, DL, DY, DA, GS
        )
        for half in range(2):
            columns = pl.ds(half * HALF, HALF)
            SM[half, 9:10, :] = GS[:, columns].astype(bf16)
            router = tn_dot(DL[...], H[zeroth, columns])
            SM[half, 0:8, :] = router[0:8].astype(bf16)
            SM[half, 10:16, :] = jnp.zeros((6, HALF), bf16)

        def out_block(b, _):
            emit(b, OB, DA[:, pl.ds(pl.multiple_of(b * WIDTH, WIDTH), WIDTH)])
            slot(28 + b)
            return 0

        need(5, 6)
        lax.fori_loop(0, 3, out_block, 0)
        need(14, 18)

        def dob_tile(t, _):
            ns = pl.ds(pl.multiple_of(t * 512, 512), 512)
            tile = nt_dot(DA[:, :HALF], W[1, 0, ns, :]) + nt_dot(DA[:, HALF:], W[1, 1, ns, :])
            DOB[:, ns] = tile.astype(bf16)
            slot(31 + t)
            return 0

        lax.fori_loop(0, 3, dob_tile, 0)
        need(6, 12)
        state = [34, 0]

        def run(slots_now, parts_now):
            first_slot, first_part = state

            def slot_step(n, _):
                slot(first_slot + n)
                return 0

            def part_step(n, _):
                aslot(first_part + n)
                return 0

            lax.fori_loop(0, slots_now, slot_step, 0)
            lax.fori_loop(0, parts_now, part_step, 0)
            state[0] += slots_now
            state[1] += parts_now

        def emit_query(b):
            emit(3 + b, H1, DQKV[:, pl.ds(b * WIDTH, WIDTH)])

        def tick(heads):
            if heads == 6:
                need(12, 13)
                emit_query(0)
            if heads == 9:
                emit_query(1)
            run(2, 2)

        heads_backward(QB, KB, VV, DOB, BIAS, LSE, COS, SIN, DQKV, DK, DV, tick)
        for b in (2, 3):
            emit_query(b)
            run(2, 2)
        need(13, 14)
        need(18, 26)
        done, parts_done = state

        def dh1_tile(t, _):
            ns = pl.ds(pl.multiple_of(t * 512, 512), 512)
            tile = nt_dot(DQKV[:, :HALF], W[0, 0, ns, :])
            tile = tile + nt_dot(DQKV[:, HALF:MODEL_WIDTH], W[0, 1, ns, :])
            Y1[:, ns] = tile + nt_dot(DQKV[:, MODEL_WIDTH:], W[0, 2, ns, :512])
            slot(done + t)
            aslot(parts_done + t)
            return 0

        lax.fori_loop(0, 3, dh1_tile, 0)
        done, parts_done = done + 3, parts_done + 3
        first_backward(Y1, XB, DY, G1, GB, GS)
        for half in range(2):
            SM[half, 8:9, :] = GS[:, pl.ds(half * HALF, HALF)].astype(bf16)
        result = local_copy(GB, hgrad, att.at[len(pairs) + 1])
        result.start()

        for i, device in enumerate((cdev, xdev, ydev, zdev, mdev)):
            hop = remote(SM, sa.at[i], s_s.at[i], s_r.at[i], device)
            hop.start()
            slot(done)
            aslot(parts_done)
            done, parts_done = done + 1, parts_done + 1
            hop.wait()
            load = local_copy(sa.at[i], SB, sl.at[0])
            load.start()
            load.wait()
            SM[...] = (SM[...].astype(f32) + SB[...].astype(f32)).astype(bf16)
        small = local_copy(SM, smo, sl.at[1])
        small.start()

        sums = [
            local_copy(p[0], p[1], att.at[n])
            for n, p in enumerate(((y1, Y1), (o_own, OB), (o_core, QB), (o_x, H1)))
        ]
        for copy in sums[:3]:
            copy.start()

        def first_drain(n, _):
            slot(done + n)
            aslot(parts_done + n)
            return 0

        lax.fori_loop(0, 8, first_drain, 0)
        done_now, parts_now = done + 8, parts_done + 8
        ox.wait()
        sums[3].start()
        for copy in sums:
            copy.wait()

        def sum_step(b, _):
            rows = pl.ds(pl.multiple_of(b * 128, 128), 128)
            total = OB[rows, :].astype(f32) + QB[rows, :].astype(f32) + H1[rows, :].astype(f32)
            DOB[rows, :] = (Y1[rows, :] + total).astype(bf16)
            return 0

        lax.fori_loop(0, ROWS // 128, sum_step, 0)
        forward_out = local_copy(DOB, hout, att.at[4])
        forward_out.start()
        last_slot = max(EXPERT_SLOTS - done_now, PART_SLOTS - parts_now)

        def drain(n, _):
            slot(done_now + n)
            aslot(parts_now + n)
            return 0

        lax.fori_loop(0, last_slot, drain, 0)
        small.wait()
        result.wait()
        forward_out.wait()

        def finish_part(n, _):
            ac_copy(n).wait_send()
            axg_copy(n).wait_send()
            ac1_copy(n).wait()
            ac2_copy(n).wait()
            return 0

        lax.fori_loop(0, PARTS, finish_part, 0)

    pl.run_scoped(
        attention,
        vm((ROWS, MODEL_WIDTH), f32), vm((ROWS, MODEL_WIDTH), f32),
        part(ROWS, MODEL_WIDTH), part(ROWS, MODEL_WIDTH), part(ROWS, MODEL_WIDTH),
        part(ROWS, MODEL_WIDTH), part(ROWS, MODEL_WIDTH), part(ROWS, 256), part(ROWS, 256),
        part(ROWS, MODEL_WIDTH), part(ROWS, MODEL_WIDTH), part(ROWS, 2048),
        vm((ROWS, ROWS), f32), vm((ROWS, PAD), f32), vm((ROWS, PAD), f32), vm((ROWS, PAD), f32),
        vm((ROWS, TOPK), jnp.int32), vm((1, ROWS), jnp.int32),
        part(ROWS, PAD), vm((1, MODEL_WIDTH), f32), vm((2, ROWS, PAD), f32),
        vm((2, ROWS, PAD), f32), part(2, HALF, WIDTH),
        part(2, 2, 192, WIDTH), part(2, 2, 192, WIDTH), part(4, 2, 192, WIDTH),
        part(2, 192, WIDTH), part(4, 192, WIDTH), part(2, QUARTER, WIDTH), part(8, QUARTER, WIDTH),
        part(2, QUARTER, WIDTH), part(4, QUARTER, WIDTH), part(2, QUARTER, WIDTH),
        part(4, QUARTER, WIDTH),
    )

    def finish(n, _):
        @pl.when(crosses(n))
        def _():
            x_copy(n).wait_send()

        @pl.when(crosses(n) & handed(n))
        def _():
            z4_copy(n).wait_send()

        c1_copy(n).wait()
        c2_copy(n).wait()
        y_copy(n).wait_send()
        return 0

    lax.fori_loop(0, CHUNKS, finish, 0)


def layer_call(*arrays):
    anyspace = pl.BlockSpec(memory_space=pl.ANY)
    dma = pltpu.SemaphoreType.DMA
    vmem = lambda *s: pltpu.VMEM(s, bf16)
    n = PARTS
    wide, narrow = (ROWS, MODEL_WIDTH), (ROWS, 256)
    shapes = [wide, (3, 8, HALF, FF), (HALF, BLOCKS * WIDTH), (2, 16, HALF), wide]
    shapes += [wide] * 3 + [(*wide, f32), wide, wide, narrow, narrow, wide, (ROWS, PAD, f32)]
    shapes += [(HALF, MODEL_WIDTH), (HALF, 256), (HALF, 256), (HALF, MODEL_WIDTH), (16, HALF)]
    shapes += [(3, ROWS, MODEL_WIDTH)]
    shapes += [(ROWS, WIDE)] * 2 + [(2, 3, MODEL_WIDTH, FF)] + [(CHUNKS, CHUNK, FF)] * 3
    shapes += [(BLOCKS, 2, HALF, WIDTH), (n, 2, 192, WIDTH), (n, 192, WIDTH)]
    shapes += [(n, QUARTER, WIDTH)] * 3 + [(5, 2, 16, HALF)]
    outputs = [
        jax.ShapeDtypeStruct(s[:-1], f32) if s[-1] is f32 else jax.ShapeDtypeStruct(s, bf16)
        for s in shapes
    ]
    many, few = dma((CHUNKS,)), dma((n,))
    scratch = [
        vmem(4 * ROWS, WIDE), vmem(2, 3, MODEL_WIDTH, FF), vmem(4 * ROWS, PAD), vmem(ROWS, WIDE),
        vmem(ROWS, MODEL_WIDTH), vmem(2, CHUNK, FF), vmem(2, CHUNK, FF), vmem(4, CHUNK, FF),
        vmem(2, CHUNK, FF), vmem(4, CHUNK, FF), vmem(2, CHUNK, FF), vmem(4, CHUNK, FF),
        vmem(2, 16, HALF), vmem(2, 16, HALF), vmem(PAD, MODEL_WIDTH),
        pltpu.VMEM((1, MODEL_WIDTH), f32), pltpu.VMEM((1, MODEL_WIDTH), f32),
        dma((16,)), dma((15,)), dma((15,)), dma((9,)), dma((9,)), dma((9,)), dma((9,)), dma((9,)),
        dma((9,)), dma((6,)), dma((6,)), dma((2,)), dma((2,)), dma((2,)), dma((2,)), dma((2,)),
        dma((2,)), dma((6,)), dma((7,)),
        dma((4,)), dma((2,)), many, many, dma((2,)), dma((2,)),
        many, many, dma((2,)), many, many, dma((2,)),
        many, many, dma((4,)), many, many, many, many, many, many, many, many,
        dma((2, 3)), dma((2, 3)), dma((2,)), dma((2,)), dma((8,)), dma((8,)), dma((3,)),
        few, few, dma((2, 2)), few, few, dma((2,)), few, few, dma((2,)), few, few, dma((2,)),
        few, few, dma((2,)), few, few, dma((4,)), few, few, few, few, few, few,
        dma((5,)), dma((5,)), dma((2,)), dma((32,)),
    ]
    return pl.pallas_call(
        layer_kernel,
        out_shape=outputs,
        in_specs=[anyspace] * len(arrays),
        out_specs=[anyspace] * len(shapes),
        scratch_shapes=scratch,
        compiler_params=pltpu.CompilerParams(
            collective_id=2, has_side_effects=True, vmem_limit_bytes=67 * 1000 * 1000
        ),
        name="layer",
    )(*arrays)[:5]


def attention_forward(hidden, segments, gain_one, w_q, w_k, w_v, w_o, gain_two):
    sequence_length = hidden.shape[0]
    group = QUERY_HEADS // KEY_VALUE_HEADS
    head_scale = HEAD_SIZE ** (-0.5)
    cosine, sine = tables(sequence_length, HEAD_SIZE)
    normed_f, scale_one = normalize(hidden, gain_one)
    h1 = normed_f.astype(bf16)
    qr = jnp.dot(h1, w_q, preferred_element_type=f32)
    kr = jnp.dot(h1, w_k, preferred_element_type=f32)
    values = jnp.dot(h1, w_v, preferred_element_type=f32).astype(bf16)
    values = values.reshape(sequence_length, KEY_VALUE_HEADS, HEAD_SIZE)
    qr = qr.reshape(sequence_length, QUERY_HEADS, HEAD_SIZE)
    kr = kr.reshape(sequence_length, KEY_VALUE_HEADS, HEAD_SIZE)
    queries = apply_rotary(qr, cosine, sine).astype(bf16)
    queries = queries.reshape(sequence_length, KEY_VALUE_HEADS, group, HEAD_SIZE)
    keys = apply_rotary(kr, cosine, sine).astype(bf16)
    position = jnp.arange(sequence_length)
    allowed = (position[None, :] <= position[:, None]) & (segments[:, None] == segments[None, :])
    scores = jnp.einsum("qkgd,skd->kgqs", queries, keys, preferred_element_type=f32) * head_scale
    scores = jnp.where(allowed, scores, -1e30)
    top_score = jnp.max(scores, axis=-1, keepdims=True)
    exp_scores = jnp.exp(scores - top_score)
    sum_exp = jnp.sum(exp_scores, axis=-1, keepdims=True)
    log_total = top_score + jnp.log(sum_exp)
    probs = (exp_scores / sum_exp).astype(bf16)
    mixed = jnp.einsum("kgqs,skd->qkgd", probs, values, preferred_element_type=f32)
    mixed = mixed.reshape(sequence_length, QUERY_HEADS * HEAD_SIZE).astype(bf16)
    middle = hidden + jnp.dot(mixed, w_o, preferred_element_type=f32)
    normed_two_f, scale_two = normalize(middle, gain_two)
    h2 = normed_two_f.astype(bf16)
    kept = (scale_one, h1, queries, keys, values, allowed, log_total, mixed, middle, scale_two)
    return h2, kept


def router_forward(h2, w_router, routes):
    logits = jnp.dot(h2, w_router, preferred_element_type=f32)
    probs = softmax_rows(logits)
    experts = w_router.shape[1]
    chosen = jnp.any(
        routes[:, :, None] == jnp.arange(experts, dtype=jnp.int32)[None, None, :], axis=1
    )
    picked = jnp.where(chosen, probs, 0.0)
    total = jnp.sum(picked, axis=-1, keepdims=True)
    return probs, chosen, total, picked / total


def router_backward(h2, w_router, probs, chosen, total, gates, gate_grads):
    gate_grads = jnp.where(chosen, gate_grads, 0.0)
    weighted = jnp.sum(gate_grads * gates, axis=-1, keepdims=True)
    prob_grad = jnp.where(chosen, (gate_grads - weighted) / total, 0.0)
    logit_grad = probs * (prob_grad - jnp.sum(prob_grad * probs, axis=-1, keepdims=True))
    logit_grad = logit_grad.astype(bf16)
    return contract(h2, logit_grad, 0, 0), contract(logit_grad, w_router, 1, 1)


def attention_backward(hidden, kept, gain_one, w_q, w_k, w_v, w_o, gain_two, upstream, dh2):
    scale_one, h1, queries, keys, values, allowed, log_total, mixed, middle, scale_two = kept
    sequence_length = hidden.shape[0]
    group = QUERY_HEADS // KEY_VALUE_HEADS
    head_scale = HEAD_SIZE ** (-0.5)
    cosine, sine = tables(sequence_length, HEAD_SIZE)
    middle_norm_grad, gain_two_grad = norm_back(middle, scale_two, gain_two, dh2)
    middle_grad = upstream + middle_norm_grad
    branch_grad = middle_grad.astype(bf16)
    out_proj_sum = contract(mixed, branch_grad, 0, 0)
    mixed_grad = contract(branch_grad, w_o, 1, 1).astype(bf16)
    mixed_grad = mixed_grad.reshape(sequence_length, KEY_VALUE_HEADS, group, HEAD_SIZE)
    probs = jnp.exp(
        jnp.einsum("qkgd,skd->kgqs", queries, keys, preferred_element_type=f32) * head_scale
        - log_total
    )
    probs = jnp.where(allowed, probs, 0.0)
    prob_back = jnp.einsum("qkgd,skd->kgqs", mixed_grad, values, preferred_element_type=f32)
    score_grad = probs * (prob_back - jnp.sum(prob_back * probs, axis=-1, keepdims=True))
    score_grad = score_grad.astype(bf16)
    dq = jnp.einsum("kgqs,skd->qkgd", score_grad, keys, preferred_element_type=f32) * head_scale
    dq = dq.reshape(sequence_length, QUERY_HEADS, HEAD_SIZE)
    dq = apply_rotary(dq, cosine, -sine).astype(bf16)
    dq = dq.reshape(sequence_length, QUERY_HEADS * HEAD_SIZE)
    dk = jnp.einsum("kgqs,qkgd->skd", score_grad, queries, preferred_element_type=f32) * head_scale
    dk = apply_rotary(dk, cosine, -sine).astype(bf16)
    dk = dk.reshape(sequence_length, KEY_VALUE_HEADS * HEAD_SIZE)
    dv = jnp.einsum("kgqs,qkgd->skd", probs.astype(bf16), mixed_grad, preferred_element_type=f32)
    dv = dv.astype(bf16).reshape(sequence_length, KEY_VALUE_HEADS * HEAD_SIZE)
    query_sum = contract(h1, dq, 0, 0)
    key_sum = contract(h1, dk, 0, 0)
    value_sum = contract(h1, dv, 0, 0)
    dh1 = contract(dq, w_q, 1, 1) + contract(dk, w_k, 1, 1) + contract(dv, w_v, 1, 1)
    hidden_norm_grad, gain_one_grad = norm_back(hidden, scale_one, gain_one, dh1)
    hidden_grad = (middle_grad + hidden_norm_grad).astype(bf16)
    return hidden_grad, (
        gain_one_grad,
        query_sum,
        key_sum,
        value_sum,
        out_proj_sum,
        gain_two_grad,
    )


def reduce_over_all(value, dimension):
    value = lax.psum_scatter(
        value.astype(bf16), "shard", scatter_dimension=dimension, tiled=True
    ).astype(f32)
    return lax.psum(value.astype(bf16), "rep").astype(f32)


def local(
    hidden_in,
    segment_ids,
    routes,
    out_grad,
    norm1_gain,
    w_query,
    key_weight,
    value_weight,
    w_out,
    norm2_gain,
    w_router,
    w_gate,
    w_up,
    w_down,
):
    small = jnp.concatenate(
        [w_router.T, norm1_gain[None], norm2_gain[None], jnp.zeros((6, HALF), bf16)], axis=0
    )
    cosine, sine = turn_tables(ROWS)
    hidden_out, grads, d, sm, hidden_grad = layer_call(
        hidden_in,
        out_grad,
        w_query,
        key_weight,
        value_weight,
        w_out,
        small,
        w_gate,
        w_up,
        w_down,
        cosine,
        sine,
        routes,
        segment_ids,
    )
    sm = lax.dynamic_index_in_dim(sm, lax.axis_index("shard"), 0, keepdims=False).astype(f32)
    d = d.astype(f32)
    attn = (sm[8], d[:, 1536:3072], d[:, 3072:3328], d[:, 3328:], d[:, :1536], sm[9], sm[:8].T)
    grads = [grads[m].astype(f32) for m in range(3)]
    return (hidden_out, hidden_grad, *attn, *grads)


def local_any(
    hidden_in,
    segment_ids,
    routes,
    out_grad,
    norm1_gain,
    w_query,
    key_weight,
    value_weight,
    w_out,
    norm2_gain,
    w_router,
    w_gate,
    w_up,
    w_down,
):
    wide = lambda w, axis: lax.all_gather(w, "shard", axis=axis, tiled=True)
    gain_one, gain_two = wide(norm1_gain, 0).astype(f32), wide(norm2_gain, 0).astype(f32)
    w_q, w_k, w_v, w_o = (wide(w, 0) for w in (w_query, key_weight, value_weight, w_out))
    router = wide(w_router, 0)
    hidden = hidden_in.astype(f32)
    h2, kept = attention_forward(
        hidden, segment_ids[0], gain_one, w_q, w_k, w_v, w_o, gain_two
    )
    probs, chosen, total, gates = router_forward(h2, router, routes)
    full = [wide(w, 1) for w in (w_gate, w_up, w_down)]

    def expert(carry, inputs):
        mixed, dh2 = carry
        gate_weight, up_weight, down_weight, gate = inputs
        gate = gate[:, None]
        ug = jnp.dot(h2, gate_weight, preferred_element_type=f32)
        uu = jnp.dot(h2, up_weight, preferred_element_type=f32)
        dh = jnp.dot(out_grad, down_weight, preferred_element_type=f32)
        sigma = jax.nn.sigmoid(ug)
        silu = ug * sigma
        hid = silu * uu
        gate_grad = jnp.sum(hid * dh, axis=1)
        hidden_rows = (hid * gate).astype(bf16)
        dug = (dh * gate * uu * sigma * (1.0 + ug * (1.0 - sigma))).astype(bf16)
        duu = (dh * gate * silu).astype(bf16)
        mixed = mixed + contract(hidden_rows, down_weight, 1, 1)
        dh2 = dh2 + contract(dug, gate_weight, 1, 1) + contract(duu, up_weight, 1, 1)
        sums = (contract(h2, dug, 0, 0), contract(h2, duu, 0, 0))
        sums = sums + (contract(out_grad, hidden_rows, 0, 0),)
        return (mixed, dh2), (gate_grad, *(s.astype(bf16) for s in sums))

    zeros = jnp.zeros(hidden.shape, f32)
    (mixed, dh2), (gate_grads, *sums) = lax.scan(expert, (zeros, zeros), (*full, gates.T))
    hidden_out = (kept[8] + mixed).astype(bf16)
    router_sum, routed = router_backward(h2, router, probs, chosen, total, gates, gate_grads.T)
    hidden_grad, attn = attention_backward(
        hidden, kept, gain_one, w_q, w_k, w_v, w_o, gain_two, out_grad.astype(f32), routed + dh2
    )
    attn = [reduce_over_all(value, 0) for value in attn + (router_sum,)]
    grads = [reduce_over_all(value, 1) for value in sums]
    return (hidden_out, hidden_grad, *attn, *grads)


def solution(mesh):
    rows, vector, matrix = P(("rep", "shard"), None), P("shard"), P("shard", None)
    stack = P(None, "shard", None)
    in_specs = (
        rows, rows, rows, rows, vector, matrix, matrix, matrix, matrix, vector, matrix,
        stack, stack, stack,
    )
    out_specs = (
        rows, rows, vector, matrix, matrix, matrix, matrix, vector, matrix, stack, stack, stack,
    )
    fits = dict(mesh.shape) == {"rep": 16, "shard": 2}
    body = local if fits else local_any
    return jax.shard_map(body, mesh=mesh, in_specs=in_specs, out_specs=out_specs, check_vma=False)
```

```python
import functools

import jax
import jax.numpy as jnp
import numpy as np
from jax import lax
from jax.experimental import pallas as pl
from jax.experimental.pallas import tpu as pltpu
from jax.sharding import PartitionSpec as P

MODEL_WIDTH = 1536
QUERY_HEADS = 12
KEY_VALUE_HEADS = 2
HEAD_SIZE = 128
TOPK = 4
FF = 768
HALF = 768
ROWS = 512
PAD = 128
WIDE = MODEL_WIDTH + PAD
CHUNK = 96
PER = HALF // CHUNK
CHUNKS = 6 * PER

epsilon = 1e-06
rope_base = 1000000.0
MESH = pl.DeviceIdType.MESH
bf16 = jnp.bfloat16
f32 = jnp.float32


def tables(sequence_length, row_width):
    frequency = rope_base ** (-2.0 * jnp.arange(row_width // 2, dtype=jnp.float32) / row_width)
    angles = jnp.arange(sequence_length, dtype=jnp.float32)[:, None] * frequency[None, :]
    angles = jnp.concatenate([angles, angles], axis=-1)
    return (jnp.cos(angles)[:, None, :], jnp.sin(angles)[:, None, :])


def apply_rotary(values, rotary_cosine, rotary_sine):
    half_width = values.shape[-1] // 2
    turned = jnp.concatenate([-values[..., half_width:], values[..., :half_width]], axis=-1)
    return values * rotary_cosine + turned * rotary_sine


def contract(left_side, right_side, left_dim, right_dim):
    return lax.dot_general(
        left_side,
        right_side,
        (((left_dim,), (right_dim,)), ((), ())),
        preferred_element_type=jnp.float32,
    )


def normalize(values, gain_vector):
    scale_rows = lax.rsqrt(jnp.mean(values * values, axis=-1, keepdims=True) + epsilon)
    return (values * scale_rows * gain_vector, scale_rows)


def norm_back(values, scale_rows, gain_vector, upstream):
    scaled = upstream * gain_vector
    gain_grad = jnp.sum(upstream * values * scale_rows, axis=0)
    inner_sum = jnp.sum(scaled * values, axis=-1, keepdims=True)
    return (scaled * scale_rows - values * scale_rows**3 * inner_sum / values.shape[-1], gain_grad)


def softmax_rows(values):
    top_value = jnp.max(values, axis=-1, keepdims=True)
    exp_values = jnp.exp(values - top_value)
    return exp_values / jnp.sum(exp_values, axis=-1, keepdims=True)


def place():
    rep = lax.axis_index("rep")
    y = lax.axis_index("shard")
    return rep // 4, (rep // 2) % 2, rep % 2, y


def at(z, x, c, y):
    return ((z * 2 + x) * 2 + c, y)


def remote(src, dst, send, recv, device):
    return pltpu.make_async_remote_copy(
        src_ref=src,
        dst_ref=dst,
        send_sem=send,
        recv_sem=recv,
        device_id=device,
        device_id_type=MESH,
    )


def greet(partners):
    barrier = pltpu.get_barrier_semaphore()
    for device in partners:
        pl.semaphore_signal(barrier, inc=1, device_id=device, device_id_type=MESH)
    pl.semaphore_wait(barrier, len(partners))


def nt_dot(a, b):
    return lax.dot_general(a, b, (((1,), (1,)), ((), ())), preferred_element_type=f32)


def tn_dot(a, b):
    return lax.dot_general(a, b, (((0,), (0,)), ((), ())), preferred_element_type=f32)


def turn_tables(length):
    half = HEAD_SIZE // 2
    exponent = np.float32(-2.0) * np.arange(half, dtype=np.float32) / np.float32(HEAD_SIZE)
    frequency = np.float32(rope_base) ** exponent
    angles = np.arange(length, dtype=np.float32)[:, None] * frequency[None, :]
    cosine, sine = np.cos(angles), np.sin(angles)
    cosine = np.concatenate([cosine, cosine], axis=1)
    sine = np.concatenate([-sine, sine], axis=1)
    return jnp.asarray(cosine, f32), jnp.asarray(sine, f32)


def router_rows(h2, router_rows_t, routes):
    logits = nt_dot(h2, router_rows_t)
    lane = lax.broadcasted_iota(jnp.int32, logits.shape, 1)
    real = lane < 8
    logits = jnp.where(real, logits, -1e30)
    top = jnp.max(logits, axis=1, keepdims=True)
    exp_values = jnp.where(real, jnp.exp(logits - top), 0.0)
    probs = exp_values / jnp.sum(exp_values, axis=1, keepdims=True)
    chosen = lane == routes[:, 0:1]
    for k in range(1, 4):
        chosen = chosen | (lane == routes[:, k : k + 1])
    picked = jnp.where(chosen, probs, 0.0)
    total = jnp.sum(picked, axis=1, keepdims=True)
    return probs, chosen, total, picked / total


def middle_backward(returned, h2, rt, routes, y1, g, gain_two, DL, DY, DA, GS):
    GS[...] = jnp.zeros_like(GS)

    def step(b, _):
        rows = pl.ds(pl.multiple_of(b * 128, 128), 128)
        probs, chosen, total, gates = router_rows(h2(rows), rt[...], routes[rows, :])
        back = returned(rows)
        packed = back[:, MODEL_WIDTH:]
        gate_grads = jnp.where(chosen, packed + pltpu.roll(packed, PAD - 8, 1), 0.0)
        weighted = jnp.sum(gate_grads * gates, axis=1, keepdims=True)
        prob_grad = jnp.where(chosen, (gate_grads - weighted) / total, 0.0)
        inner = jnp.sum(prob_grad * probs, axis=1, keepdims=True)
        logit_grad = (probs * (prob_grad - inner)).astype(bf16)
        DL[rows, :] = logit_grad
        dh2 = back[:, :MODEL_WIDTH] + jnp.dot(logit_grad, rt[...], preferred_element_type=f32)
        v = y1[rows, :]
        r = lax.rsqrt(jnp.mean(v * v, axis=1, keepdims=True) + epsilon)
        GS[...] = GS[...] + jnp.sum(dh2 * v * r, axis=0, keepdims=True)
        scaled = dh2 * gain_two[...]
        along = jnp.sum(scaled * v, axis=1, keepdims=True)
        dy = g[rows, :].astype(f32) + (scaled * r - v * (r * r * r * along / MODEL_WIDTH))
        DY[rows, :] = dy
        DA[rows, :] = dy.astype(bf16)
        return 0

    lax.fori_loop(0, ROWS // 128, step, 0)


def heads_backward(Q, K, V, DOB, BIAS, LSE, COS, SIN, DQKV, DK, DV, tick):
    scale = HEAD_SIZE ** (-0.5)
    DK[...] = jnp.zeros_like(DK)
    DV[...] = jnp.zeros_like(DV)
    for group in range(2):
        shared = pl.ds(group * HEAD_SIZE, HEAD_SIZE)

        def head(n, _, group=group, shared=shared):
            columns = pl.ds(pl.multiple_of((group * 6 + n) * HEAD_SIZE, HEAD_SIZE), HEAD_SIZE)
            lane = lax.broadcasted_iota(jnp.int32, (ROWS, PAD), 1)
            lse = jnp.sum(
                jnp.where(lane == group * 6 + n, LSE[...], 0.0), axis=1, keepdims=True
            )
            for block in range(2):
                rows, keys = pl.ds(block * 256, 256), pl.ds(0, 256 * (block + 1))
                q, dob = Q[rows, columns], DOB[rows, columns]
                k, v = K[keys, shared], V[keys, shared]
                logits = nt_dot(q, k) * scale + BIAS[rows, keys]
                p = jnp.exp(logits - lse[block * 256 : block * 256 + 256])
                dp = nt_dot(dob, v)
                inner = jnp.sum(dp * p, axis=1, keepdims=True)
                ds = (p * (dp - inner)).astype(bf16)
                dq = jnp.dot(ds, k, preferred_element_type=f32) * scale
                dq = dq * COS[rows, :] - pltpu.roll(dq, 64, 1) * SIN[rows, :]
                DQKV[rows, columns] = dq.astype(bf16)
                DK[group, keys, :] = DK[group, keys, :] + tn_dot(ds, q)
                DV[group, keys, :] = DV[group, keys, :] + tn_dot(p.astype(bf16), dob)
            return 0

        for n in range(0, 6, 3):
            lax.fori_loop(n, n + 3, head, 0)
            tick(group * 6 + n + 3)
        dk = DK[group] * scale
        dk = dk * COS[...] - pltpu.roll(dk, 64, 1) * SIN[...]
        DQKV[:, pl.ds(1536 + group * HEAD_SIZE, HEAD_SIZE)] = dk.astype(bf16)
        DQKV[:, pl.ds(1792 + group * HEAD_SIZE, HEAD_SIZE)] = DV[group].astype(bf16)


def first_backward(DH1, X, DY, gain_one, HG, GS):
    GS[...] = jnp.zeros_like(GS)

    def step(b, _):
        rows = pl.ds(pl.multiple_of(b * 128, 128), 128)
        v, up = X[rows, :].astype(f32), DH1[rows, :]
        r = lax.rsqrt(jnp.mean(v * v, axis=1, keepdims=True) + epsilon)
        GS[...] = GS[...] + jnp.sum(up * v * r, axis=0, keepdims=True)
        scaled = up * gain_one[...]
        along = jnp.sum(scaled * v, axis=1, keepdims=True)
        back = scaled * r - v * (r * r * r * along / MODEL_WIDTH)
        HG[rows, :] = (DY[rows, :] + back).astype(bf16)
        return 0

    lax.fori_loop(0, ROWS // 128, step, 0)


def mask_bias(seg_row, BIAS):
    row = lax.broadcasted_iota(jnp.int32, (ROWS, ROWS), 0)
    column = lax.broadcasted_iota(jnp.int32, (ROWS, ROWS), 1)
    ids = seg_row[0:1, :].astype(f32)
    same = jnp.transpose(jnp.broadcast_to(ids, (PAD, ROWS)))[:, 0:1] == ids
    BIAS[...] = jnp.where((column <= row) & same, 0.0, -1e30)


BLOCKS = 7
PARTS = 2 * BLOCKS
WIDTH = 512
QUARTER = 96
SLACK = 2
AT_ZL, AT_FL, AT_X = 1 + SLACK, 2 + 2 * SLACK, 3 + 3 * SLACK
AT_CX, AT_CZ = AT_X + 8, AT_X + 12
EXPERT_SLOTS = CHUNKS + AT_CZ + 1
PART_SLOTS = PARTS + 18


def layer_kernel(
    xin, g, wq, wk, wv, wo, sm, wg, wu, wd, cos, sin, routes, segr,
    hout, out, aout, smo, hgrad,
    o_own, o_core, o_x, y1, h1, q, k, v, ob, lse, wqo, wko, wvo, woo, smf, gl,
    r_core, r_x, gr, ya, za, zb, d, ca, yb, xb, zc, zd, sa,
    H, W, DG, CR, CO, VA, VB, VS, VZ, VT, VF, FN, SM, SB, RT, G1, G2,
    fl_s, wa_s, wa_r, wx_s, wx_r, wc_s, wc_r, wd_s, wd_r, wz_s, wz_r, hx_s, hx_r, hc_s, hc_r,
    hd_s, hd_r, own_s, st_s,
    loc, stg_sem, y_s, y_r, ld_a, ld_b,
    z1_s, z1_r, ld_z, z2_s, z2_r, ld_f, z3_s, z3_r, fo, x_s, x_r, c1_s, c1_r, c2_s, c2_r,
    z4_s, z4_r, rc_s, rc_r, rx_s, rx_r, rd_s, rd_r, ro,
    ac_s, ac_r, ald, ay_s, ay_r, aldy, ax_s, ax_r, aldx, az1_s, az1_r, aldz, az2_s, az2_r, aldf,
    az3_s, az3_r, afo, axg_s, axg_r, ac1_s, ac1_r, ac2_s, ac2_r, s_s, s_r, sl, att,
):
    z, x, c, y = place()
    mid = (z == 1) | (z == 2)
    end = jnp.logical_not(mid)
    ydev, xdev, cdev = at(z, x, c, 1 - y), at(z, 1 - x, c, y), at(z, x, 1 - c, y)
    zdev = at(z + 1 - 2 * (z % 2), x, c, y)
    mdev = at(3 - z, x, c, y)
    greet((ydev, xdev, cdev, zdev, mdev))
    shards = (wg, wu, wd)
    e0 = 2 * (2 * x + c)
    other = 2 * (2 * (1 - x) + c)
    h = z % 2
    local_copy = pltpu.make_async_copy
    vm = pltpu.VMEM
    part = lambda *shape: vm(shape, bf16)

    piece = HALF // 4
    own_piece, x_piece = (2 * x + c) * piece, (2 * (1 - x) + c) * piece
    kinds = [(wk, wko, 0, piece), (wv, wvo, 0, piece)]
    kinds += [(wq, wqo, n * 64, 64) for n in range(3)] + [(wo, woo, n * 64, 64) for n in range(3)]

    def copies(from_input, begin, send, receive, device):
        made = []
        for n, (whole, landed, shift, count) in enumerate(kinds):
            rows = pl.ds(pl.multiple_of(begin + shift, 64), count)
            src = whole if from_input else landed
            made.append(remote(src.at[rows], landed.at[rows], send.at[n], receive.at[n], device))
        return made

    wa = copies(True, own_piece, wa_s, wa_r, ydev)
    wa.append(remote(sm, smf, wa_s.at[8], wa_r.at[8], ydev))
    wx = copies(False, own_piece, wx_s, wx_r, xdev)
    wc = copies(False, own_piece, wc_s, wc_r, cdev)
    wt = copies(False, x_piece, wd_s, wd_r, cdev)
    gx = remote(g, gl.at[1], wx_s.at[8], wx_r.at[8], xdev)
    gc = remote(g, gl.at[0], wc_s.at[8], wc_r.at[8], cdev)
    gt = remote(gl.at[1], gl.at[2], wd_s.at[8], wd_r.at[8], cdev)

    def wy(n):
        j, m = n // 3, n % 3
        return remote(
            shards[m].at[e0 + j, pl.ds(h * 384, 384)],
            W.at[j, m, pl.ds(y * HALF + h * 384, 384)],
            wa_s.at[9 + n],
            wa_r.at[9 + n],
            ydev,
        )

    def wz(n):
        rows = pl.ds((1 - y) * HALF + h * 384, 384)
        ref = W.at[n // 3, n % 3, rows]
        return remote(ref, ref, wz_s.at[n], wz_r.at[n], zdev)

    def own_half(n):
        j, m = n // 3, n % 3
        return local_copy(shards[m].at[e0 + j], W.at[j, m, pl.ds(y * HALF, HALF)], own_s.at[n])

    def pass_on(n):
        wy(n).wait_recv()
        wz(n).start()

    def hx(b):
        src = H.at[pl.ds(b * 256, 256)]
        return remote(src, H.at[pl.ds(2 * ROWS + b * 256, 256)], hx_s.at[b], hx_r.at[b], xdev)

    def hc(b):
        src = H.at[pl.ds(b * 256, 256)]
        return remote(src, H.at[pl.ds(ROWS + b * 256, 256)], hc_s.at[b], hc_r.at[b], cdev)

    def hd(b):
        src = H.at[pl.ds(2 * ROWS + b * 256, 256)]
        return remote(src, H.at[pl.ds(3 * ROWS + b * 256, 256)], hd_s.at[b], hd_r.at[b], cdev)

    wa[8].start()
    for n in range(8):
        wa[n].start()
    gc.start()
    for n in range(6):
        wy(n).start()

    def front(X, H1, WQ, WKV, WO, Q, K, V, OB, BIAS, LSE, COS, SIN, RO, SR, SF, Y1):
        there = pl.ds(y * HALF, HALF)
        away = pl.ds((1 - y) * HALF, HALF)
        left, right = pl.ds(0, 256), pl.ds(256, 256)
        pairs = [
            (xin, X), (sm, SF.at[y]), (wk, WKV.at[there, left]), (wv, WKV.at[there, right]),
            (wq, WQ.at[there]), (wo, WO.at[there]), (cos, COS), (sin, SIN), (routes, RO),
            (segr, SR),
        ]
        loads = [local_copy(p[0], p[1], fl_s.at[n]) for n, p in enumerate(pairs)]
        for copy in loads:
            copy.start()
        for n in range(6):
            own_half(n).start()
        late = [
            local_copy(wko, WKV.at[away, left], fl_s.at[11]),
            local_copy(wvo, WKV.at[away, right], fl_s.at[12]),
            local_copy(wqo, WQ.at[away], fl_s.at[13]),
            local_copy(woo, WO.at[away], fl_s.at[14]),
            local_copy(smf, SF.at[1 - y], fl_s.at[15]),
        ]
        wa[8].wait_recv()
        late[4].start()
        for n in (0, 1):
            loads[n].wait()
        late[4].wait()
        row = lax.broadcasted_iota(jnp.int32, (16, HALF), 0)
        RT[...] = jnp.zeros_like(RT)
        for half in range(2):
            columns = pl.ds(half * HALF, HALF)
            small = SF[half].astype(f32)
            RT[0:16, columns] = jnp.where(row < 8, small, 0.0).astype(bf16)
            G1[:, columns] = jnp.sum(jnp.where(row == 8, small, 0.0), axis=0, keepdims=True)
            G2[:, columns] = jnp.sum(jnp.where(row == 9, small, 0.0), axis=0, keepdims=True)

        def norm_step(b, _):
            rows = pl.ds(pl.multiple_of(b * 128, 128), 128)
            value = X[rows, :].astype(f32)
            r = lax.rsqrt(jnp.mean(value * value, axis=1, keepdims=True) + epsilon)
            H1[rows, :] = (value * r * G1[...]).astype(bf16)
            return 0

        lax.fori_loop(0, ROWS // 128, norm_step, 0)
        for n in range(2, 10):
            loads[n].wait()
        mask_bias(SR, BIAS)
        def onward(n):
            wa[n].wait_recv()
            wx[n].start()
            wc[n].start()

        def across(n):
            wx[n].wait_recv()
            wt[n].start()

        for n in range(3):
            onward(n)
        for n in range(3):
            across(n)
            onward(n + 3)
        for n in (3, 4):
            across(n)
            onward(n + 3)
        gx.start()
        for n in range(5):
            wc[n].wait_recv()
            wt[n].wait_recv()
        for n in range(3):
            late[n].start()
        for n in range(3):
            late[n].wait()

        def rotate(u):
            return u * COS[...] + pltpu.roll(u, 64, 1) * SIN[...]

        def query_step(t, _):
            begin = pl.multiple_of(t * 512, 512)
            tile = jnp.dot(H1[...], WQ[:, pl.ds(begin, 512)], preferred_element_type=f32)
            for n in range(4):
                u = tile[:, n * HEAD_SIZE : (n + 1) * HEAD_SIZE]
                Q[:, pl.ds(begin + n * HEAD_SIZE, HEAD_SIZE)] = rotate(u).astype(bf16)
            return 0

        tile = jnp.dot(H1[...], WKV[...], preferred_element_type=f32)
        for n in range(2):
            columns = pl.ds(n * HEAD_SIZE, HEAD_SIZE)
            u = tile[:, n * HEAD_SIZE : (n + 1) * HEAD_SIZE]
            K[:, columns] = rotate(u).astype(bf16)
        V[...] = tile[:, 256:].astype(bf16)
        lax.fori_loop(0, 3, query_step, 0)
        for n in (5, 6, 7):
            across(n)
        pass_on(0)
        LSE[...] = jnp.zeros_like(LSE)
        scale = HEAD_SIZE ** (-0.5)
        for b in range(2):
            rows, keys = pl.ds(b * 256, 256), pl.ds(0, 256 * (b + 1))

            def head(n, _, rows=rows, keys=keys):
                columns = pl.ds(pl.multiple_of(n * HEAD_SIZE, HEAD_SIZE), HEAD_SIZE)
                shared = pl.ds(pl.multiple_of(n // 6 * HEAD_SIZE, HEAD_SIZE), HEAD_SIZE)
                logits = nt_dot(Q[rows, columns], K[keys, shared]) * scale + BIAS[rows, keys]
                top = jnp.max(logits, axis=1, keepdims=True)
                p = jnp.exp(logits - top)
                total = jnp.sum(p, axis=1, keepdims=True)
                lane = lax.broadcasted_iota(jnp.int32, (256, PAD), 1)
                LSE[rows, :] = jnp.where(lane == n, top + jnp.log(total), LSE[rows, :])
                p = (p * (1.0 / total)).astype(bf16)
                mixed = jnp.dot(p, V[keys, shared], preferred_element_type=f32)
                OB[rows, columns] = mixed.astype(bf16)
                return 0

            lax.fori_loop(0, QUERY_HEADS, head, 0)
            if b == 0:
                for n in (5, 6, 7):
                    wc[n].wait_recv()
                    wt[n].wait_recv()
                late[3].start()
                pass_on(1)
                late[3].wait()
            for t in range(3):
                ns = pl.ds(t * 512, 512)
                Y1[rows, ns] = X[rows, ns].astype(f32) + jnp.dot(
                    OB[rows, :], WO[:, ns], preferred_element_type=f32
                )
            for n in range(2):
                block = pl.ds(b * 256 + n * 128, 128)
                value = Y1[block, :]
                r = lax.rsqrt(jnp.mean(value * value, axis=1, keepdims=True) + epsilon)
                h2 = (value * r * G2[...]).astype(bf16)
                H[block, :MODEL_WIDTH] = h2
                gates = router_rows(h2, RT[...], RO[block, :])[3]
                high = gates.astype(bf16).astype(f32)
                H[block, MODEL_WIDTH:] = (high + pltpu.roll(gates - high, 8, 1)).astype(bf16)
            hx(b).start()
            hc(b).start()
        stores = [
            local_copy(p[0], p[1], st_s.at[n])
            for n, p in enumerate(
                ((Y1, y1), (H1, h1), (Q, q), (K, k), (V, v), (OB, ob), (LSE, lse))
            )
        ]
        for copy in stores:
            copy.start()
        pass_on(2)
        for copy in stores:
            copy.wait()

    pl.run_scoped(
        front,
        part(ROWS, MODEL_WIDTH), part(ROWS, MODEL_WIDTH), part(MODEL_WIDTH, MODEL_WIDTH),
        part(MODEL_WIDTH, 512), part(MODEL_WIDTH, MODEL_WIDTH), part(ROWS, MODEL_WIDTH),
        part(ROWS, 256), part(ROWS, 256), part(ROWS, MODEL_WIDTH), vm((ROWS, ROWS), f32),
        vm((ROWS, PAD), f32), vm((ROWS, PAD), f32), vm((ROWS, PAD), f32),
        vm((ROWS, TOPK), jnp.int32), vm((1, ROWS), jnp.int32),
        part(2, 16, HALF), vm((ROWS, MODEL_WIDTH), f32),
    )

    def parts_of(n):
        return n // (3 * PER), (n // PER) % 3, n % PER

    def y_copy(n):
        j, m, i = parts_of(n)
        src = gr.at[j, m, pl.ds((1 - y) * HALF + i * CHUNK, CHUNK)]
        return remote(src, ya.at[n], y_s.at[n], y_r.at[n], ydev)

    def spot(n, expert):
        j, m, i = parts_of(n)
        return out.at[m, expert + j, pl.ds(i * CHUNK, CHUNK)]

    def load_a(n):
        j, m, i = parts_of(n)
        src = gr.at[j, m, pl.ds(y * HALF + i * CHUNK, CHUNK)]
        return local_copy(src, VA.at[n % 2], ld_a.at[n % 2])

    def load_b(n):
        return local_copy(ya.at[n], VB.at[n % 2], ld_b.at[n % 2])

    def load_z(n):
        return local_copy(za.at[n], VZ.at[n % 2], ld_z.at[n % 2])

    def load_f(n):
        return local_copy(zb.at[n], VF.at[n % 2], ld_f.at[n % 2])

    def z1_copy(n):
        return remote(VS.at[n % 4], za.at[n], z1_s.at[n], z1_r.at[n], zdev)

    def z2_copy(n):
        return remote(VT.at[n % 4], zb.at[n], z2_s.at[n], z2_r.at[n], mdev)

    def z3_copy(n):
        return remote(FN.at[n % 4], spot(n, e0), z3_s.at[n], z3_r.at[n], zdev)

    def z4_copy(n):
        return remote(spot(n, other), spot(n, other), z4_s.at[n], z4_r.at[n], zdev)

    def store_f(n):
        return local_copy(FN.at[n % 4], spot(n, e0), fo.at[n % 4])

    def x_copy(n):
        return remote(spot(n, e0), spot(n, e0), x_s.at[n], x_r.at[n], xdev)

    def c1_copy(n):
        return remote(spot(n, e0), spot(n, e0), c1_s.at[n], c1_r.at[n], cdev)

    def c2_copy(n):
        return remote(spot(n, other), spot(n, other), c2_s.at[n], c2_r.at[n], cdev)

    def handed(n):
        return n % 2 == 1

    def crosses(n):
        return (n % 2 == 0) | ((n % 4 == 1) & mid) | ((n % 4 == 3) & end)

    def when(n, cond=None):
        ok = (n >= 0) & (n < CHUNKS)
        return pl.when(ok if cond is None else ok & cond)

    def slot(s):
        n = s - AT_CZ

        @when(n, jnp.logical_not(crosses(n + 4 * CHUNKS)))
        def _(n=n):
            z4_copy(n).wait_recv()
            c2_copy(n).start()

        n = s - AT_CX
        crossed = crosses(n + 4 * CHUNKS)

        @when(n, crossed)
        def _(n=n):
            x_copy(n).wait_recv()
            c2_copy(n).start()

        @when(n, crossed & handed(n + 4 * CHUNKS))
        def _(n=n):
            z4_copy(n).start()

        n = s - AT_X

        @when(n, mid)
        def _(n=n):
            store_f(n).wait()
            z3_copy(n).wait_send()

        @when(n, end)
        def _(n=n):
            z3_copy(n).wait_recv()

        @when(n, crosses(n + 4 * CHUNKS))
        def _(n=n):
            x_copy(n).start()

        @when(n)
        def _(n=n):
            c1_copy(n).start()

        n = s - AT_FL - 1

        @when(n, mid)
        def _(n=n):
            load_f(n).wait()
            z2_copy(n).wait_send()
            FN[n % 4] = VT[n % 4] + VF[n % 2]
            z3_copy(n).start()
            store_f(n).start()

        n = s - AT_FL

        @when(n, mid)
        def _(n=n):
            z2_copy(n).wait_recv()
            load_f(n).start()

        n = s - AT_ZL - 1

        @when(n, mid)
        def _(n=n):
            load_z(n).wait()
            VT[n % 4] = VS[n % 4] + VZ[n % 2]
            z2_copy(n).start()

        n = s - AT_ZL

        @when(n, mid)
        def _(n=n):
            z1_copy(n).wait_recv()
            load_z(n).start()

        n = s - 5

        @when(n, end)
        def _(n=n):
            z1_copy(n).wait_send()

        n = s - 1

        @when(n)
        def _(n=n):
            load_a(n).wait()
            load_b(n).wait()
            VS[n % 4] = VA[n % 2] + VB[n % 2]

        @when(n, end)
        def _(n=n):
            z1_copy(n).start()

        @when(s)
        def _():
            y_copy(s).wait_recv()
            load_a(s).start()
            load_b(s).start()

    def slots(first, last):
        def step(s, _):
            slot(s)
            return 0

        lax.fori_loop(first, last, step, 0)

    third, second = pl.ds(3 * ROWS, ROWS), pl.ds(2 * ROWS, ROWS)
    first, zeroth = pl.ds(ROWS, ROWS), pl.ds(0, ROWS)

    def experts(G, ACT, STG, RS, OS):
        gain_rows = [
            local_copy(src, G.at[pl.ds(n * ROWS, ROWS)], loc.at[n])
            for n, src in enumerate((g, gl.at[0], gl.at[1], gl.at[2]))
        ]
        gain_rows[0].start()
        gc.wait_recv()
        gain_rows[1].start()

        def gate_of(j, rows):
            lane = lax.broadcasted_iota(jnp.int32, (2 * ROWS, PAD), 1)
            packed = H[rows, MODEL_WIDTH:].astype(f32)
            picked = (lane == e0 + j) | (lane == e0 + j + 8)
            return jnp.sum(jnp.where(picked, packed, 0.0), axis=1, keepdims=True), lane

        def forward(j, begin, base=None):
            rows = pl.ds(begin, 2 * ROWS)
            gate, lane = gate_of(j, rows)

            def step(t, total):
                columns = pl.ds(pl.multiple_of(t * 256, 256), 256)
                ug = jnp.dot(
                    H[rows, :MODEL_WIDTH], W[j, 0, :, columns], preferred_element_type=f32
                )
                uu = jnp.dot(
                    H[rows, :MODEL_WIDTH], W[j, 1, :, columns], preferred_element_type=f32
                )
                dh = jnp.dot(G[rows, :], W[j, 2, :, columns], preferred_element_type=f32)
                sigma = jax.nn.sigmoid(ug)
                silu = ug * sigma
                hid = silu * uu
                ACT[j, 0, rows, columns] = (hid * gate).astype(bf16)
                dhg = dh * gate
                ACT[j, 1, rows, columns] = (
                    dhg * uu * sigma * (1.0 + ug * (1.0 - sigma))
                ).astype(bf16)
                ACT[j, 2, rows, columns] = (dhg * silu).astype(bf16)
                if base is not None:
                    slot(base + t)
                return total + jnp.sum(hid * dh, axis=1, keepdims=True)

            total = lax.fori_loop(0, FF // 256, step, jnp.zeros((2 * ROWS, 1), f32))
            high = total.astype(bf16).astype(f32)
            low = total - high
            here = jnp.where(lane == e0 + j, high, jnp.where(lane == e0 + j + 8, low, 0.0))
            if j == 0:
                DG[rows, :] = here.astype(bf16)
            else:
                DG[rows, :] = (DG[rows, :].astype(f32) + here).astype(bf16)

        def back_rows(rows, ns):
            o = nt_dot(ACT[0, 0, rows, :], W[0, 2, ns, :])
            o = o + nt_dot(ACT[1, 0, rows, :], W[1, 2, ns, :])
            e = nt_dot(ACT[0, 1, rows, :], W[0, 0, ns, :])
            e = e + nt_dot(ACT[0, 2, rows, :], W[0, 1, ns, :])
            e = e + nt_dot(ACT[1, 1, rows, :], W[1, 0, ns, :])
            e = e + nt_dot(ACT[1, 2, rows, :], W[1, 1, ns, :])
            return o, e

        def store_tile(j, m, half, i, place_in):
            rows = pl.ds(half * HALF + i * 384, 384)
            return local_copy(STG.at[place_in], gr.at[j, m, rows], stg_sem.at[place_in])

        def weight_tile(j, m, left, half, i, place_in):
            begin = half * HALF + i * 384
            lhs = left[:, pl.ds(pl.multiple_of(begin, 128), 384)]
            STG[place_in] = tn_dot(lhs, ACT[j, (m + 1) % 3]).astype(bf16)
            copy = store_tile(j, m, half, i, place_in)
            copy.start()
            return copy

        def weight_grads(j, base=None):
            done = 0
            for left, m0, steps in ((H, 0, 4), (G, 2, 2)):

                def step(n, _, left=left, m0=m0, done=done):
                    m, i = m0 + n // 2, n % 2
                    away = weight_tile(j, m, left, 1 - y, i, 0)

                    @pl.when(n + done > 0)
                    def _():
                        store_tile(j, m, y, i, 1).wait()

                    weight_tile(j, m, left, y, i, 1)
                    away.wait()
                    begin = (j * 3 + m) * PER + i * (384 // CHUNK)
                    for p in range(384 // CHUNK):
                        y_copy(begin + p).start()
                    if base is not None:
                        slot(base + done + n)
                    return 0

                lax.fori_loop(0, steps, step, 0)
                done += steps
            store_tile(j, 2, y, 1, 1).wait()

        def rc_copy(t, which):
            ns = pl.ds(pl.multiple_of(t * 512, 512), 512)
            src, dst = ((RS, CR), (OS, CO))[which]
            return remote(
                src.at[t % 2], dst.at[:, ns], rc_s.at[which, t], rc_r.at[which, t], cdev
            )

        def rb_copy(t, which):
            ns = pl.ds(pl.multiple_of(t * 512, 512), 512)
            src, dst = ((RS, r_core), (OS, o_core))[which]
            return remote(
                src.at[t % 2], dst.at[:, ns], rd_s.at[1 + which * 3 + t],
                rd_r.at[1 + which * 3 + t], cdev,
            )

        def ro_copy(t):
            ns = pl.ds(pl.multiple_of(t * 512, 512), 512)
            return local_copy(OS.at[t % 2], o_own.at[:, ns], ro.at[t])

        for n in range(3):
            wz(n).wait_recv()
            own_half(n).wait()
        gain_rows[0].wait()
        gain_rows[1].wait()
        for b in range(2):
            hc(b).wait_recv()
        pass_on(3)
        forward(0, 0)
        gx.wait_recv()
        gt.start()
        gain_rows[2].start()
        pass_on(4)
        for b in range(2):
            hx(b).wait_recv()
            hd(b).start()
        gt.wait_recv()
        gain_rows[3].start()
        for b in range(2):
            hd(b).wait_recv()
        gain_rows[2].wait()
        gain_rows[3].wait()
        forward(0, 2 * ROWS)
        pass_on(5)
        weight_grads(0)
        for n in range(3, 6):
            wz(n).wait_recv()
            own_half(n).wait()
        forward(1, 2 * ROWS, 0)

        def third_step(t, _):
            ns = pl.ds(pl.multiple_of(t * 512, 512), 512)

            @pl.when(t == 2)
            def _():
                rc_copy(0, 0).wait_send()
                rc_copy(0, 1).wait_send()

            o, e = back_rows(third, ns)
            RS[t % 2] = e.astype(bf16)
            OS[t % 2] = o.astype(bf16)
            rc_copy(t, 0).start()
            rc_copy(t, 1).start()
            slot(3 + t)
            return 0

        lax.fori_loop(0, 3, third_step, 0)
        dg_copy = remote(
            DG.at[third], CR.at[:, pl.ds(MODEL_WIDTH, PAD)], rd_s.at[0], rd_r.at[0], cdev
        )
        dg_copy.start()

        def second_step(t, _):
            ns = pl.ds(pl.multiple_of(t * 512, 512), 512)
            o, e = back_rows(second, ns)
            rc_copy(t, 0).wait_recv()
            rc_copy(t, 1).wait_recv()
            CR[:, ns] = (CR[:, ns].astype(f32) + e).astype(bf16)
            CO[:, ns] = (CO[:, ns].astype(f32) + o).astype(bf16)
            slot(6 + t)
            return 0

        lax.fori_loop(0, 3, second_step, 0)
        dg_copy.wait_recv()
        CR[:, MODEL_WIDTH:] = CR[:, MODEL_WIDTH:] + DG[second, :]
        rx.start()
        forward(1, 0, 9)
        weight_grads(1, 12)
        for which in range(2):
            for t in (1, 2):
                rc_copy(t, which).wait_send()
        dg_copy.wait_send()
        tail_b.start()

        def first_step(t, _):
            ns = pl.ds(pl.multiple_of(t * 512, 512), 512)

            @pl.when(t == 2)
            def _():
                rb_copy(0, 0).wait_send()
                rb_copy(0, 1).wait_send()

            o, e = back_rows(first, ns)
            RS[t % 2] = e.astype(bf16)
            OS[t % 2] = o.astype(bf16)
            rb_copy(t, 0).start()
            rb_copy(t, 1).start()
            slot(18 + t)
            return 0

        lax.fori_loop(0, 3, first_step, 0)
        for t in (1, 2):
            rb_copy(t, 0).wait_send()
            rb_copy(t, 1).wait_send()

        def zeroth_step(t, _):
            ns = pl.ds(pl.multiple_of(t * 512, 512), 512)
            o, e = back_rows(zeroth, ns)

            @pl.when(t == 2)
            def _():
                ro_copy(0).wait()

            H[first, ns] = e.astype(bf16)
            OS[t % 2] = o.astype(bf16)
            ro_copy(t).start()
            slot(21 + t)
            return 0

        lax.fori_loop(0, 3, zeroth_step, 0)
        H[first, MODEL_WIDTH:] = DG[zeroth, :]
        for t in range(3):
            rb_copy(t, 0).wait_recv()
            rb_copy(t, 1).wait_recv()
        for t in (1, 2):
            ro_copy(t).wait()
        for n in range(6):
            wy(n).wait_send()
            wz(n).wait_send()
        for n in range(8):
            wa[n].wait_send()
            wx[n].wait_send()
            wc[n].wait_send()
            wt[n].wait_send()
        wa[8].wait_send()
        for copy in (gx, gc, gt):
            copy.wait_send()
        for b in range(2):
            hx(b).wait_send()
            hc(b).wait_send()
            hd(b).wait_send()
        rx.wait_send()

    rx = remote(CR, r_x, rx_s.at[0], rx_r.at[0], xdev)
    ox = remote(CO, o_x, rx_s.at[1], rx_r.at[1], xdev)
    tail_b = remote(
        DG.at[first], r_core.at[:, pl.ds(MODEL_WIDTH, PAD)], rd_s.at[7], rd_r.at[7], cdev
    )
    pl.run_scoped(
        experts,
        vm((4 * ROWS, MODEL_WIDTH), bf16),
        vm((2, 3, 4 * ROWS, FF), bf16),
        vm((2, 384, FF), bf16),
        vm((2, ROWS, 512), bf16),
        vm((2, ROWS, 512), bf16),
    )
    ox.start()
    tail_b.wait()

    def attention(
        Y1, DY, GB, XB, H1, OB, QB, KB, VV, DA, DOB, DQKV, BIAS, LSE, COS, SIN, RO,
        SR, DL, GS, DK, DV, STG,
        AA, AB, PP, VY, QQ, VX, AS, AZ, AT, AF, AN,
    ):
        pairs = [
            (segr, SR), (y1, Y1), (g, GB), (routes, RO), (r_core, H.at[second]),
            (ob, OB), (q, QB), (k, KB), (v, VV), (lse, LSE), (cos, COS), (sin, SIN), (h1, H1),
            (xin, XB),
        ]
        for n, ws in ((1, (wo, woo)), (0, (wq, wqo))):
            for w, rows in zip(ws, (pl.ds(y * HALF, HALF), pl.ds((1 - y) * HALF, HALF))):
                for side in range(2):
                    pairs.append((w.at[:, pl.ds(side * HALF, HALF)], W.at[n, side, rows]))
        for ws, columns in (((wk, wko), pl.ds(0, 256)), ((wv, wvo), pl.ds(256, 256))):
            for w, rows in zip(ws, (pl.ds(y * HALF, HALF), pl.ds((1 - y) * HALF, HALF))):
                pairs.append((w, W.at[0, 2, rows, columns]))
        loads = [local_copy(p[0], p[1], att.at[n]) for n, p in enumerate(pairs)]
        for copy in loads:
            copy.start()

        def need(first, last):
            for copy in loads[first:last]:
                copy.wait()

        slots(24, 26)
        need(0, 1)
        mask_bias(SR, BIAS)
        slots(26, 28)
        need(1, 5)
        rx.wait_recv()
        last = local_copy(r_x, H.at[third], att.at[len(pairs)])
        last.start()
        last.wait()

        def rows_of(n):
            q_, i = n // 2, n % 2
            return q_, i * 384

        def ac_copy(n):
            b, begin = rows_of(n)
            src = d.at[b, :, pl.ds(begin + (1 - c) * 192, 192)]
            return remote(src, ca.at[n], ac_s.at[n], ac_r.at[n], cdev)

        def aload_a(n):
            b, begin = rows_of(n)
            return local_copy(d.at[b, :, pl.ds(begin + c * 192, 192)], AA.at[n % 2], ald.at[0, n % 2])

        def aload_b(n):
            return local_copy(ca.at[n], AB.at[n % 2], ald.at[1, n % 2])

        def ay_copy(n):
            return remote(PP.at[n % 4, 1 - y], yb.at[n], ay_s.at[n], ay_r.at[n], ydev)

        def aload_y(n):
            return local_copy(yb.at[n], VY.at[n % 2], aldy.at[n % 2])

        def ax_copy(n):
            src = QQ.at[n % 4, pl.ds((1 - x) * QUARTER, QUARTER)]
            return remote(src, xb.at[n], ax_s.at[n], ax_r.at[n], xdev)

        def aload_x(n):
            return local_copy(xb.at[n], VX.at[n % 2], aldx.at[n % 2])

        def az1_copy(n):
            return remote(AS.at[n % 8], zc.at[n], az1_s.at[n], az1_r.at[n], zdev)

        def aload_z(n):
            return local_copy(zc.at[n], AZ.at[n % 2], aldz.at[n % 2])

        def az2_copy(n):
            return remote(AT.at[n % 4], zd.at[n], az2_s.at[n], az2_r.at[n], mdev)

        def aload_f(n):
            return local_copy(zd.at[n], AF.at[n % 2], aldf.at[n % 2])

        def aspot(n, xx, cc):
            b, begin = rows_of(n)
            columns = pl.ds(pl.multiple_of(b * WIDTH, WIDTH), WIDTH)
            return aout.at[pl.ds(begin + cc * 192 + xx * QUARTER, QUARTER), columns]

        def az3_copy(n):
            return remote(AN.at[n % 4], aspot(n, x, c), az3_s.at[n], az3_r.at[n], zdev)

        def astore(n):
            return local_copy(AN.at[n % 4], aspot(n, x, c), afo.at[n % 4])

        def axg_copy(n):
            return remote(aspot(n, x, c), aspot(n, x, c), axg_s.at[n], axg_r.at[n], xdev)

        def ac1_copy(n):
            return remote(aspot(n, x, c), aspot(n, x, c), ac1_s.at[n], ac1_r.at[n], cdev)

        def ac2_copy(n):
            return remote(aspot(n, 1 - x, c), aspot(n, 1 - x, c), ac2_s.at[n], ac2_r.at[n], cdev)

        def awhen(n, cond=None):
            ok = (n >= 0) & (n < PARTS)
            return pl.when(ok if cond is None else ok & cond)

        def aslot(s):
            @awhen(s - 17)
            def _():
                axg_copy(s - 17).wait_recv()
                ac2_copy(s - 17).start()

            @awhen(s - 15, mid)
            def _():
                astore(s - 15).wait()
                az3_copy(s - 15).wait_send()

            @awhen(s - 15, end)
            def _():
                az3_copy(s - 15).wait_recv()

            @awhen(s - 15)
            def _():
                axg_copy(s - 15).start()
                ac1_copy(s - 15).start()

            @awhen(s - 13, mid)
            def _():
                n = s - 13
                aload_f(n).wait()
                az2_copy(n).wait_send()
                AN[n % 4] = AT[n % 4] + AF[n % 2]
                az3_copy(n).start()
                astore(n).start()

            @awhen(s - 12, mid)
            def _():
                az2_copy(s - 12).wait_recv()
                aload_f(s - 12).start()

            @awhen(s - 10, mid)
            def _():
                n = s - 10
                aload_z(n).wait()
                AT[n % 4] = AS[n % 8] + AZ[n % 2]
                az2_copy(n).start()

            @awhen(s - 10, end)
            def _():
                az1_copy(s - 10).wait_send()

            @awhen(s - 9, mid)
            def _():
                az1_copy(s - 9).wait_recv()
                aload_z(s - 9).start()

            @awhen(s - 7)
            def _():
                n = s - 7
                aload_x(n).wait()
                ax_copy(n).wait_send()
                mine = pl.ds(pl.multiple_of(x * QUARTER, 16), QUARTER)
                AS[n % 8] = QQ[n % 4, mine, :] + VX[n % 2]

            @awhen(s - 7, end)
            def _():
                az1_copy(s - 7).start()

            @awhen(s - 6)
            def _():
                ax_copy(s - 6).wait_recv()
                aload_x(s - 6).start()

            @awhen(s - 4)
            def _():
                n = s - 4
                aload_y(n).wait()
                ay_copy(n).wait_send()
                QQ[n % 4] = PP[n % 4, y] + VY[n % 2]
                ax_copy(n).start()

            @awhen(s - 3)
            def _():
                ay_copy(s - 3).wait_recv()
                aload_y(s - 3).start()

            @awhen(s - 1)
            def _():
                n = s - 1
                aload_a(n).wait()
                aload_b(n).wait()
                PP[n % 4] = AA[n % 2] + AB[n % 2]
                ay_copy(n).start()

            @awhen(s)
            def _():
                ac_copy(s).wait_recv()
                aload_a(s).start()
                aload_b(s).start()

        def emit(b, left, right):
            copies = []
            for half in range(2):
                STG[half] = tn_dot(left[:, pl.ds(half * HALF, HALF)], right).astype(bf16)
                copies.append(local_copy(STG.at[half], d.at[b, half], stg_sem.at[half]))
                copies[half].start()
            for copy in copies:
                copy.wait()
            ac_copy(2 * b).start()
            ac_copy(2 * b + 1).start()

        def returned(rows):
            begin = rows.start
            one = H[pl.ds(pl.multiple_of(begin + ROWS, 128), 128), :].astype(f32)
            two = H[pl.ds(pl.multiple_of(begin + 2 * ROWS, 128), 128), :].astype(f32)
            three = H[pl.ds(pl.multiple_of(begin + 3 * ROWS, 128), 128), :].astype(f32)
            return one + two + three

        middle_backward(
            returned, lambda rows: H[rows, :MODEL_WIDTH], RT, RO, Y1, GB, G2, DL, DY, DA, GS
        )
        for half in range(2):
            columns = pl.ds(half * HALF, HALF)
            SM[half, 9:10, :] = GS[:, columns].astype(bf16)
            router = tn_dot(DL[...], H[zeroth, columns])
            SM[half, 0:8, :] = router[0:8].astype(bf16)
            SM[half, 10:16, :] = jnp.zeros((6, HALF), bf16)

        def out_block(b, _):
            emit(b, OB, DA[:, pl.ds(pl.multiple_of(b * WIDTH, WIDTH), WIDTH)])
            slot(28 + b)
            return 0

        need(5, 6)
        lax.fori_loop(0, 3, out_block, 0)
        need(14, 18)

        def dob_tile(t, _):
            ns = pl.ds(pl.multiple_of(t * 512, 512), 512)
            tile = nt_dot(DA[:, :HALF], W[1, 0, ns, :]) + nt_dot(DA[:, HALF:], W[1, 1, ns, :])
            DOB[:, ns] = tile.astype(bf16)
            slot(31 + t)
            return 0

        lax.fori_loop(0, 3, dob_tile, 0)
        need(6, 12)
        state = [34, 0]

        def run(slots_now, parts_now):
            first_slot, first_part = state

            def slot_step(n, _):
                slot(first_slot + n)
                return 0

            def part_step(n, _):
                aslot(first_part + n)
                return 0

            lax.fori_loop(0, slots_now, slot_step, 0)
            lax.fori_loop(0, parts_now, part_step, 0)
            state[0] += slots_now
            state[1] += parts_now

        def emit_query(b):
            emit(3 + b, H1, DQKV[:, pl.ds(b * WIDTH, WIDTH)])

        def tick(heads):
            if heads == 6:
                need(12, 13)
                emit_query(0)
            if heads == 9:
                emit_query(1)
            run(2, 2)

        heads_backward(QB, KB, VV, DOB, BIAS, LSE, COS, SIN, DQKV, DK, DV, tick)
        for b in (2, 3):
            emit_query(b)
            run(2, 2)
        need(13, 14)
        need(18, 26)
        done, parts_done = state

        def dh1_tile(t, _):
            ns = pl.ds(pl.multiple_of(t * 512, 512), 512)
            tile = nt_dot(DQKV[:, :HALF], W[0, 0, ns, :])
            tile = tile + nt_dot(DQKV[:, HALF:MODEL_WIDTH], W[0, 1, ns, :])
            Y1[:, ns] = tile + nt_dot(DQKV[:, MODEL_WIDTH:], W[0, 2, ns, :512])
            slot(done + t)
            aslot(parts_done + t)
            return 0

        lax.fori_loop(0, 3, dh1_tile, 0)
        done, parts_done = done + 3, parts_done + 3
        first_backward(Y1, XB, DY, G1, GB, GS)
        for half in range(2):
            SM[half, 8:9, :] = GS[:, pl.ds(half * HALF, HALF)].astype(bf16)
        result = local_copy(GB, hgrad, att.at[len(pairs) + 1])
        result.start()

        for i, device in enumerate((cdev, xdev, ydev, zdev, mdev)):
            hop = remote(SM, sa.at[i], s_s.at[i], s_r.at[i], device)
            hop.start()
            slot(done)
            aslot(parts_done)
            done, parts_done = done + 1, parts_done + 1
            hop.wait()
            load = local_copy(sa.at[i], SB, sl.at[0])
            load.start()
            load.wait()
            SM[...] = (SM[...].astype(f32) + SB[...].astype(f32)).astype(bf16)
        small = local_copy(SM, smo, sl.at[1])
        small.start()

        sums = [
            local_copy(p[0], p[1], att.at[n])
            for n, p in enumerate(((y1, Y1), (o_own, OB), (o_core, QB), (o_x, H1)))
        ]
        for copy in sums[:3]:
            copy.start()

        def first_drain(n, _):
            slot(done + n)
            aslot(parts_done + n)
            return 0

        lax.fori_loop(0, 8, first_drain, 0)
        done_now, parts_now = done + 8, parts_done + 8
        ox.wait()
        sums[3].start()
        for copy in sums:
            copy.wait()

        def sum_step(b, _):
            rows = pl.ds(pl.multiple_of(b * 128, 128), 128)
            total = OB[rows, :].astype(f32) + QB[rows, :].astype(f32) + H1[rows, :].astype(f32)
            DOB[rows, :] = (Y1[rows, :] + total).astype(bf16)
            return 0

        lax.fori_loop(0, ROWS // 128, sum_step, 0)
        forward_out = local_copy(DOB, hout, att.at[4])
        forward_out.start()
        last_slot = max(EXPERT_SLOTS - done_now, PART_SLOTS - parts_now)

        def drain(n, _):
            slot(done_now + n)
            aslot(parts_now + n)
            return 0

        lax.fori_loop(0, last_slot, drain, 0)
        small.wait()
        result.wait()
        forward_out.wait()

        def finish_part(n, _):
            ac_copy(n).wait_send()
            axg_copy(n).wait_send()
            ac1_copy(n).wait()
            ac2_copy(n).wait()
            return 0

        lax.fori_loop(0, PARTS, finish_part, 0)

    pl.run_scoped(
        attention,
        vm((ROWS, MODEL_WIDTH), f32), vm((ROWS, MODEL_WIDTH), f32),
        part(ROWS, MODEL_WIDTH), part(ROWS, MODEL_WIDTH), part(ROWS, MODEL_WIDTH),
        part(ROWS, MODEL_WIDTH), part(ROWS, MODEL_WIDTH), part(ROWS, 256), part(ROWS, 256),
        part(ROWS, MODEL_WIDTH), part(ROWS, MODEL_WIDTH), part(ROWS, 2048),
        vm((ROWS, ROWS), f32), vm((ROWS, PAD), f32), vm((ROWS, PAD), f32), vm((ROWS, PAD), f32),
        vm((ROWS, TOPK), jnp.int32), vm((1, ROWS), jnp.int32),
        part(ROWS, PAD), vm((1, MODEL_WIDTH), f32), vm((2, ROWS, PAD), f32),
        vm((2, ROWS, PAD), f32), part(2, HALF, WIDTH),
        part(2, 2, 192, WIDTH), part(2, 2, 192, WIDTH), part(4, 2, 192, WIDTH),
        part(2, 192, WIDTH), part(4, 192, WIDTH), part(2, QUARTER, WIDTH), part(8, QUARTER, WIDTH),
        part(2, QUARTER, WIDTH), part(4, QUARTER, WIDTH), part(2, QUARTER, WIDTH),
        part(4, QUARTER, WIDTH),
    )

    def finish(n, _):
        @pl.when(crosses(n))
        def _():
            x_copy(n).wait_send()

        @pl.when(crosses(n) & handed(n))
        def _():
            z4_copy(n).wait_send()

        c1_copy(n).wait()
        c2_copy(n).wait()
        y_copy(n).wait_send()
        return 0

    lax.fori_loop(0, CHUNKS, finish, 0)


def layer_call(*arrays):
    anyspace = pl.BlockSpec(memory_space=pl.ANY)
    dma = pltpu.SemaphoreType.DMA
    vmem = lambda *s: pltpu.VMEM(s, bf16)
    n = PARTS
    wide, narrow = (ROWS, MODEL_WIDTH), (ROWS, 256)
    shapes = [wide, (3, 8, HALF, FF), (HALF, BLOCKS * WIDTH), (2, 16, HALF), wide]
    shapes += [wide] * 3 + [(*wide, f32), wide, wide, narrow, narrow, wide, (ROWS, PAD, f32)]
    shapes += [(HALF, MODEL_WIDTH), (HALF, 256), (HALF, 256), (HALF, MODEL_WIDTH), (16, HALF)]
    shapes += [(3, ROWS, MODEL_WIDTH)]
    shapes += [(ROWS, WIDE)] * 2 + [(2, 3, MODEL_WIDTH, FF)] + [(CHUNKS, CHUNK, FF)] * 3
    shapes += [(BLOCKS, 2, HALF, WIDTH), (n, 2, 192, WIDTH), (n, 192, WIDTH)]
    shapes += [(n, QUARTER, WIDTH)] * 3 + [(5, 2, 16, HALF)]
    outputs = [
        jax.ShapeDtypeStruct(s[:-1], f32) if s[-1] is f32 else jax.ShapeDtypeStruct(s, bf16)
        for s in shapes
    ]
    many, few = dma((CHUNKS,)), dma((n,))
    scratch = [
        vmem(4 * ROWS, WIDE), vmem(2, 3, MODEL_WIDTH, FF), vmem(4 * ROWS, PAD), vmem(ROWS, WIDE),
        vmem(ROWS, MODEL_WIDTH), vmem(2, CHUNK, FF), vmem(2, CHUNK, FF), vmem(4, CHUNK, FF),
        vmem(2, CHUNK, FF), vmem(4, CHUNK, FF), vmem(2, CHUNK, FF), vmem(4, CHUNK, FF),
        vmem(2, 16, HALF), vmem(2, 16, HALF), vmem(PAD, MODEL_WIDTH),
        pltpu.VMEM((1, MODEL_WIDTH), f32), pltpu.VMEM((1, MODEL_WIDTH), f32),
        dma((16,)), dma((15,)), dma((15,)), dma((9,)), dma((9,)), dma((9,)), dma((9,)), dma((9,)),
        dma((9,)), dma((6,)), dma((6,)), dma((2,)), dma((2,)), dma((2,)), dma((2,)), dma((2,)),
        dma((2,)), dma((6,)), dma((7,)),
        dma((4,)), dma((2,)), many, many, dma((2,)), dma((2,)),
        many, many, dma((2,)), many, many, dma((2,)),
        many, many, dma((4,)), many, many, many, many, many, many, many, many,
        dma((2, 3)), dma((2, 3)), dma((2,)), dma((2,)), dma((8,)), dma((8,)), dma((3,)),
        few, few, dma((2, 2)), few, few, dma((2,)), few, few, dma((2,)), few, few, dma((2,)),
        few, few, dma((2,)), few, few, dma((4,)), few, few, few, few, few, few,
        dma((5,)), dma((5,)), dma((2,)), dma((32,)),
    ]
    return pl.pallas_call(
        layer_kernel,
        out_shape=outputs,
        in_specs=[anyspace] * len(arrays),
        out_specs=[anyspace] * len(shapes),
        scratch_shapes=scratch,
        compiler_params=pltpu.CompilerParams(
            collective_id=2, has_side_effects=True, vmem_limit_bytes=67 * 1000 * 1000
        ),
        name="layer",
    )(*arrays)[:5]


def attention_forward(hidden, segments, gain_one, w_q, w_k, w_v, w_o, gain_two):
    sequence_length = hidden.shape[0]
    group = QUERY_HEADS // KEY_VALUE_HEADS
    head_scale = HEAD_SIZE ** (-0.5)
    cosine, sine = tables(sequence_length, HEAD_SIZE)
    normed_f, scale_one = normalize(hidden, gain_one)
    h1 = normed_f.astype(bf16)
    qr = jnp.dot(h1, w_q, preferred_element_type=f32)
    kr = jnp.dot(h1, w_k, preferred_element_type=f32)
    values = jnp.dot(h1, w_v, preferred_element_type=f32).astype(bf16)
    values = values.reshape(sequence_length, KEY_VALUE_HEADS, HEAD_SIZE)
    qr = qr.reshape(sequence_length, QUERY_HEADS, HEAD_SIZE)
    kr = kr.reshape(sequence_length, KEY_VALUE_HEADS, HEAD_SIZE)
    queries = apply_rotary(qr, cosine, sine).astype(bf16)
    queries = queries.reshape(sequence_length, KEY_VALUE_HEADS, group, HEAD_SIZE)
    keys = apply_rotary(kr, cosine, sine).astype(bf16)
    position = jnp.arange(sequence_length)
    allowed = (position[None, :] <= position[:, None]) & (segments[:, None] == segments[None, :])
    scores = jnp.einsum("qkgd,skd->kgqs", queries, keys, preferred_element_type=f32) * head_scale
    scores = jnp.where(allowed, scores, -1e30)
    top_score = jnp.max(scores, axis=-1, keepdims=True)
    exp_scores = jnp.exp(scores - top_score)
    sum_exp = jnp.sum(exp_scores, axis=-1, keepdims=True)
    log_total = top_score + jnp.log(sum_exp)
    probs = (exp_scores / sum_exp).astype(bf16)
    mixed = jnp.einsum("kgqs,skd->qkgd", probs, values, preferred_element_type=f32)
    mixed = mixed.reshape(sequence_length, QUERY_HEADS * HEAD_SIZE).astype(bf16)
    middle = hidden + jnp.dot(mixed, w_o, preferred_element_type=f32)
    normed_two_f, scale_two = normalize(middle, gain_two)
    h2 = normed_two_f.astype(bf16)
    kept = (scale_one, h1, queries, keys, values, allowed, log_total, mixed, middle, scale_two)
    return h2, kept


def router_forward(h2, w_router, routes):
    logits = jnp.dot(h2, w_router, preferred_element_type=f32)
    probs = softmax_rows(logits)
    experts = w_router.shape[1]
    chosen = jnp.any(
        routes[:, :, None] == jnp.arange(experts, dtype=jnp.int32)[None, None, :], axis=1
    )
    picked = jnp.where(chosen, probs, 0.0)
    total = jnp.sum(picked, axis=-1, keepdims=True)
    return probs, chosen, total, picked / total


def router_backward(h2, w_router, probs, chosen, total, gates, gate_grads):
    gate_grads = jnp.where(chosen, gate_grads, 0.0)
    weighted = jnp.sum(gate_grads * gates, axis=-1, keepdims=True)
    prob_grad = jnp.where(chosen, (gate_grads - weighted) / total, 0.0)
    logit_grad = probs * (prob_grad - jnp.sum(prob_grad * probs, axis=-1, keepdims=True))
    logit_grad = logit_grad.astype(bf16)
    return contract(h2, logit_grad, 0, 0), contract(logit_grad, w_router, 1, 1)


def attention_backward(hidden, kept, gain_one, w_q, w_k, w_v, w_o, gain_two, upstream, dh2):
    scale_one, h1, queries, keys, values, allowed, log_total, mixed, middle, scale_two = kept
    sequence_length = hidden.shape[0]
    group = QUERY_HEADS // KEY_VALUE_HEADS
    head_scale = HEAD_SIZE ** (-0.5)
    cosine, sine = tables(sequence_length, HEAD_SIZE)
    middle_norm_grad, gain_two_grad = norm_back(middle, scale_two, gain_two, dh2)
    middle_grad = upstream + middle_norm_grad
    branch_grad = middle_grad.astype(bf16)
    out_proj_sum = contract(mixed, branch_grad, 0, 0)
    mixed_grad = contract(branch_grad, w_o, 1, 1).astype(bf16)
    mixed_grad = mixed_grad.reshape(sequence_length, KEY_VALUE_HEADS, group, HEAD_SIZE)
    probs = jnp.exp(
        jnp.einsum("qkgd,skd->kgqs", queries, keys, preferred_element_type=f32) * head_scale
        - log_total
    )
    probs = jnp.where(allowed, probs, 0.0)
    prob_back = jnp.einsum("qkgd,skd->kgqs", mixed_grad, values, preferred_element_type=f32)
    score_grad = probs * (prob_back - jnp.sum(prob_back * probs, axis=-1, keepdims=True))
    score_grad = score_grad.astype(bf16)
    dq = jnp.einsum("kgqs,skd->qkgd", score_grad, keys, preferred_element_type=f32) * head_scale
    dq = dq.reshape(sequence_length, QUERY_HEADS, HEAD_SIZE)
    dq = apply_rotary(dq, cosine, -sine).astype(bf16)
    dq = dq.reshape(sequence_length, QUERY_HEADS * HEAD_SIZE)
    dk = jnp.einsum("kgqs,qkgd->skd", score_grad, queries, preferred_element_type=f32) * head_scale
    dk = apply_rotary(dk, cosine, -sine).astype(bf16)
    dk = dk.reshape(sequence_length, KEY_VALUE_HEADS * HEAD_SIZE)
    dv = jnp.einsum("kgqs,qkgd->skd", probs.astype(bf16), mixed_grad, preferred_element_type=f32)
    dv = dv.astype(bf16).reshape(sequence_length, KEY_VALUE_HEADS * HEAD_SIZE)
    query_sum = contract(h1, dq, 0, 0)
    key_sum = contract(h1, dk, 0, 0)
    value_sum = contract(h1, dv, 0, 0)
    dh1 = contract(dq, w_q, 1, 1) + contract(dk, w_k, 1, 1) + contract(dv, w_v, 1, 1)
    hidden_norm_grad, gain_one_grad = norm_back(hidden, scale_one, gain_one, dh1)
    hidden_grad = (middle_grad + hidden_norm_grad).astype(bf16)
    return hidden_grad, (
        gain_one_grad,
        query_sum,
        key_sum,
        value_sum,
        out_proj_sum,
        gain_two_grad,
    )


def reduce_over_all(value, dimension):
    value = lax.psum_scatter(
        value.astype(bf16), "shard", scatter_dimension=dimension, tiled=True
    ).astype(f32)
    return lax.psum(value.astype(bf16), "rep").astype(f32)


def local(
    hidden_in,
    segment_ids,
    routes,
    out_grad,
    norm1_gain,
    w_query,
    key_weight,
    value_weight,
    w_out,
    norm2_gain,
    w_router,
    w_gate,
    w_up,
    w_down,
):
    small = jnp.concatenate(
        [w_router.T, norm1_gain[None], norm2_gain[None], jnp.zeros((6, HALF), bf16)], axis=0
    )
    cosine, sine = turn_tables(ROWS)
    hidden_out, grads, d, sm, hidden_grad = layer_call(
        hidden_in,
        out_grad,
        w_query,
        key_weight,
        value_weight,
        w_out,
        small,
        w_gate,
        w_up,
        w_down,
        cosine,
        sine,
        routes,
        segment_ids,
    )
    sm = lax.dynamic_index_in_dim(sm, lax.axis_index("shard"), 0, keepdims=False).astype(f32)
    d = d.astype(f32)
    attn = (sm[8], d[:, 1536:3072], d[:, 3072:3328], d[:, 3328:], d[:, :1536], sm[9], sm[:8].T)
    grads = [grads[m].astype(f32) for m in range(3)]
    return (hidden_out, hidden_grad, *attn, *grads)


def local_any(
    hidden_in,
    segment_ids,
    routes,
    out_grad,
    norm1_gain,
    w_query,
    key_weight,
    value_weight,
    w_out,
    norm2_gain,
    w_router,
    w_gate,
    w_up,
    w_down,
):
    wide = lambda w, axis: lax.all_gather(w, "shard", axis=axis, tiled=True)
    gain_one, gain_two = wide(norm1_gain, 0).astype(f32), wide(norm2_gain, 0).astype(f32)
    w_q, w_k, w_v, w_o = (wide(w, 0) for w in (w_query, key_weight, value_weight, w_out))
    router = wide(w_router, 0)
    hidden = hidden_in.astype(f32)
    h2, kept = attention_forward(
        hidden, segment_ids[0], gain_one, w_q, w_k, w_v, w_o, gain_two
    )
    probs, chosen, total, gates = router_forward(h2, router, routes)
    full = [wide(w, 1) for w in (w_gate, w_up, w_down)]

    def expert(carry, inputs):
        mixed, dh2 = carry
        gate_weight, up_weight, down_weight, gate = inputs
        gate = gate[:, None]
        ug = jnp.dot(h2, gate_weight, preferred_element_type=f32)
        uu = jnp.dot(h2, up_weight, preferred_element_type=f32)
        dh = jnp.dot(out_grad, down_weight, preferred_element_type=f32)
        sigma = jax.nn.sigmoid(ug)
        silu = ug * sigma
        hid = silu * uu
        gate_grad = jnp.sum(hid * dh, axis=1)
        hidden_rows = (hid * gate).astype(bf16)
        dug = (dh * gate * uu * sigma * (1.0 + ug * (1.0 - sigma))).astype(bf16)
        duu = (dh * gate * silu).astype(bf16)
        mixed = mixed + contract(hidden_rows, down_weight, 1, 1)
        dh2 = dh2 + contract(dug, gate_weight, 1, 1) + contract(duu, up_weight, 1, 1)
        sums = (contract(h2, dug, 0, 0), contract(h2, duu, 0, 0))
        sums = sums + (contract(out_grad, hidden_rows, 0, 0),)
        return (mixed, dh2), (gate_grad, *(s.astype(bf16) for s in sums))

    zeros = jnp.zeros(hidden.shape, f32)
    (mixed, dh2), (gate_grads, *sums) = lax.scan(expert, (zeros, zeros), (*full, gates.T))
    hidden_out = (kept[8] + mixed).astype(bf16)
    router_sum, routed = router_backward(h2, router, probs, chosen, total, gates, gate_grads.T)
    hidden_grad, attn = attention_backward(
        hidden, kept, gain_one, w_q, w_k, w_v, w_o, gain_two, out_grad.astype(f32), routed + dh2
    )
    attn = [reduce_over_all(value, 0) for value in attn + (router_sum,)]
    grads = [reduce_over_all(value, 1) for value in sums]
    return (hidden_out, hidden_grad, *attn, *grads)


def solution(mesh):
    rows, vector, matrix = P(("rep", "shard"), None), P("shard"), P("shard", None)
    stack = P(None, "shard", None)
    in_specs = (
        rows, rows, rows, rows, vector, matrix, matrix, matrix, matrix, vector, matrix,
        stack, stack, stack,
    )
    out_specs = (
        rows, rows, vector, matrix, matrix, matrix, matrix, vector, matrix, stack, stack, stack,
    )
    fits = dict(mesh.shape) == {"rep": 16, "shard": 2}
    body = local if fits else local_any
    return jax.shard_map(body, mesh=mesh, in_specs=in_specs, out_specs=out_specs, check_vma=False)
```
